128 devices in a mesh: grp: 16 (over y, x), seq: 8 (over z, core).
Axes of the slice: x: 4, y: 4, z: 4, core: 2. Of those that a mesh axis runs over, the one named last changes fastest.
Arguments:
- tokens: bfloat16 [16384, 768], P(('grp', 'seq')), may hold values from -24 to 24
- segments: int32 [16, 1024], P('grp', 'seq'), may hold values from 0 to 3, never falling along the last dimension, each value on 1 to 512 neighbouring positions
- rel_bucket: int32 [1024], replicated, may hold values from 0 to 31
- routes: int32 [16384, 2], P(('grp', 'seq')), may hold values from 0 to 15, all different within a row; in each aligned block of 128 rows (0 to 127, 128 to 255, ...) at most 24 rows name the same one
- gain_attn: bfloat16 [2, 768], replicated, may hold values from 0.5 to 1.5
- wqkv: bfloat16 [2, 768, 2304], P(None, ('grp', 'seq')), may hold values from -0.21875 to 0.21875
- wout: bfloat16 [2, 768, 768], P(None, ('grp', 'seq')), may hold values from -0.875 to 0.875
- bucket_bias_table: bfloat16 [2, 32, 12], replicated, may hold values from -3 to 3
- gain_ffn: bfloat16 [2, 768], replicated, may hold values from 0.5 to 1.5
- router: bfloat16 [2, 768, 16], replicated, may hold values from -0.21875 to 0.21875
- w_in: bfloat16 [2, 16, 768, 3072], P(None, 'grp', 'seq'), may hold values from -0.21875 to 0.21875
- w_out: bfloat16 [2, 16, 3072, 768], P(None, 'grp', 'seq'), may hold values from -0.875 to 0.875
- cotangent: float32 [16384, 768], P(('grp', 'seq')), may hold values from -6 to 6
Outputs:
- out_tokens: bfloat16 [16384, 768], P(('grp', 'seq'))
- grad_tokens: float32 [16384, 768], P(('grp', 'seq'))
- grad_gain_attn: float32 [2, 768], replicated
- grad_wqkv: float32 [2, 768, 2304], P(None, ('grp', 'seq'))
- grad_wout: float32 [2, 768, 768], P(None, ('grp', 'seq'))
- grad_table: float32 [2, 32, 12], replicated
- grad_gain_ffn: float32 [2, 768], replicated
- grad_router: float32 [2, 768, 16], replicated
- grad_w_in: float32 [2, 16, 768, 3072], P(None, 'grp', 'seq')
- grad_w_out: float32 [2, 16, 3072, 768], P(None, 'grp', 'seq')
The draws below stay inside these ranges and needn't reach their ends.
Inputs may be any that keep to these rules, and one draw needn't show every extreme that they name: `segments`: along a sequence the document numbers never fall; each document spans at most half of 1024 positions, and one spans exactly that many. `routes`: each row names 2 different experts. Within the 128 rows of one device no expert is named more than 24 times, and in every draw some expert is named exactly 24 times in some device's rows.
All inputs are finite; a program needn't handle non-finite values.
Results may differ from the reference program's by a relative error of at most 0.022.
Values may be sent and summed in bfloat16 or wider, within the bound.
A program may use at most 256 MiB of HBM per device.

```python
import math
import jax
import jax.numpy as jnp
import numpy as np
from jax import lax

D = 768
HEADS = 12
HEAD_DIM = 64
FF = 3072
TOP = 2
BUCKETS = 32
LAYERS = 2
DOCS = 4
SEQ_LEN = 1024
SEQS = 16
TOK_DEV = 128
TOKENS = 16384
EXPERTS = 16
CAP = 24


def place_ends(entries, key, smallest, high):
    extent = entries.shape
    index_at = [jax.random.randint(jax.random.fold_in(key, axis), (), 0, extent[axis]) for axis in range(len(extent))]
    entries = entries.at[tuple(index_at)].set(smallest)
    longest = extent.index(max(extent))
    index_at[longest] = (index_at[longest] + 1) % extent[longest]
    return entries.at[tuple(index_at)].set(high)


def with_spikes(values, stream_key, source, target, shards_of, factor):
    owner, partner = [(jnp.arange(values.shape[axis_at]) // (values.shape[axis_at] // shards_of)).reshape([-1 if axis == axis_at else 1 for axis in range(values.ndim)]) for axis_at in (source, target)]
    chosen = jax.random.permutation(stream_key, shards_of)[partner]
    strong = (owner == chosen) | (owner == (partner + shards_of // 2) % shards_of)
    return jnp.where(strong, factor * values, values)


def block_levels(stream_key, dims, cuts, least, top_value):
    gain = 1.0
    for position, parts in cuts:
        draws = jax.random.uniform(jax.random.fold_in(jax.random.fold_in(stream_key, 6), position), (parts,), jnp.float32, least / len(cuts), top_value / len(cuts))
        gain = gain * jnp.repeat(jnp.exp(draws), dims[position] // parts).reshape((-1,) + (1,) * (len(dims) - 1 - position))
    return gain


def split_up(amount, total, limit, lean):
    weights = [(1 << 20) // math.isqrt(grade ** lean) + 1 for grade in range(2, amount + 1)]
    rest, counts = total - limit - (amount - 1), [1] * (amount - 1)
    while rest > 0:
        free = [i for i in range(amount - 1) if counts[i] < limit]
        pool, left = sum([weights[i] for i in free]), rest
        for i in free:
            extra = min(limit - counts[i], max(1, left * weights[i] // pool), rest)
            counts[i] = counts[i] + extra
            rest = rest - extra
    return np.array([limit] + counts)


def uneven(rng, count, total, reach, slope):
    if count == 2:
        one = jax.random.randint(rng, (), max(1, total - reach), min(reach, total - 1) + 1)
        return jnp.stack([one, total - one])
    sizes = jnp.asarray(split_up(count, total, reach, slope), jnp.int32)
    couples = (count - 1) // 2
    donor, taker = sizes[1:1 + 2 * couples:2], sizes[2:2 + 2 * couples:2]
    margin = jnp.minimum(donor - 1, reach - taker)
    shifted = jax.random.randint(jax.random.fold_in(rng, 1), (couples,), 0, 1 << 20) % (margin + 1)
    sizes = sizes.at[1:1 + 2 * couples:2].set(donor - shifted).at[2:2 + 2 * couples:2].set(taker + shifted)
    return sizes[jax.random.permutation(jax.random.fold_in(rng, 2), count)]


def deal_out(own_key, own, number, rows, number_of, top, limit, lean):
    ranking = jax.random.permutation(own_key, number_of)
    crowded, usual = load_shares(number_of, rows * top, limit, lean, True), load_shares(number_of, rows * top, limit, lean, False)
    places = jnp.arange(number_of)

    def named(tallies, rotation):
        used = int((tallies > 0).sum())
        fixed = max(1, used // 4)
        moved = fixed + (places - fixed + rotation * (used - fixed)) % max(1, number_of - fixed)
        return jnp.zeros((number_of,), jnp.int32).at[ranking[jnp.where(places < fixed, places, moved)]].set(jnp.asarray(tallies, jnp.int32))

    tallies = jnp.where(number % 4 == 0, named(crowded, number // 4), named(usual, number - number // 4 - 1))
    mixed = jax.random.permutation(jax.random.fold_in(own, 3), number_of)
    donor, sink = mixed[0:number_of // 2 * 2:2], mixed[1:number_of // 2 * 2:2]
    margin = jnp.minimum(tallies[donor] - 1, limit - tallies[sink]) // 2
    margin = jnp.where((donor == ranking[0]) | (sink == ranking[0]) | (tallies[sink] == 0), 0, jnp.maximum(margin, 0))
    moved = jax.random.randint(jax.random.fold_in(own, 4), (number_of // 2,), 0, 1 << 20) % (margin + 1)
    tallies = tallies.at[donor].add(-moved).at[sink].add(moved)
    labels = jnp.searchsorted(jnp.cumsum(tallies), jnp.arange(rows * top), side="right").astype(jnp.int32)
    grid = labels.reshape(top, rows).T
    grid = grid[jax.random.permutation(jax.random.fold_in(own, 1), rows)]
    rotation = jax.random.randint(jax.random.fold_in(own, 2), (rows, 1), 0, top)
    return jnp.take_along_axis(grid, (jnp.arange(top)[None, :] + rotation) % top, axis=1)


def load_shares(amount, total, reach, lean, full):
    portions = [(1 << 20) // math.isqrt(rank ** lean) + 1 for rank in range(1, amount + 1)]
    largest = reach if full else min(reach, max(-(-total // amount), total * portions[0] // sum(portions)))
    least = 1 if total - largest >= amount - 1 else 0
    given, surplus = [largest] + [least] * (amount - 1), total - largest - least * (amount - 1)
    while surplus > 0:
        free = [i for i in range(1, amount) if given[i] < largest] or [i for i in range(1, amount) if given[i] < reach]
        mass, remaining = sum([portions[i] for i in free]), surplus
        for i in free:
            extra = min(reach - given[i], max(1, remaining * portions[i] // mass), surplus)
            given[i] = given[i] + extra
            surplus = surplus - extra
    return np.array(given)


def bell_draw(own_key, shape, width, limit, cuts=(), held_as=jnp.bfloat16):
    level = block_levels(own_key, shape, cuts, -0.22, 0.18) if cuts else 1.0
    values = jax.random.normal(own_key, shape, jnp.float32) * width * level
    return jnp.minimum(jnp.maximum(values, -limit), limit).astype(held_as)


def gaussian_with(key, extent, spread, bound, cuts, heavy, kind=jnp.bfloat16):
    values = spread * jax.random.normal(key, extent, jnp.float32)
    if cuts:
        values = values * block_levels(key, extent, cuts, -0.22, 0.18)
    return jnp.clip(with_spikes(values, jax.random.fold_in(key, 3), *heavy), -bound, bound).astype(kind)


def setup_inputs(seed: int = 0) -> dict:
    seeds = jax.random.split(jax.random.key(seed), 14)
    tokens = gaussian_with(seeds[0], (TOKENS, D), 1.0, 24.0, ((0, 128),), (0, 1, 128, 5.5))
    segments = jax.vmap(lambda own: jnp.searchsorted(jnp.cumsum(uneven(own, DOCS, SEQ_LEN, SEQ_LEN // 2, 1)), jnp.arange(SEQ_LEN), side="right"))(jax.random.split(seeds[1], SEQS)).reshape((SEQS, SEQ_LEN)).astype(jnp.int32)
    rel_bucket = place_ends(jax.random.randint(seeds[2], (SEQ_LEN,), 0, BUCKETS), jax.random.fold_in(seeds[2], 1), 0, BUCKETS - 1).astype(jnp.int32)
    routes_keys = jax.random.split(jax.random.fold_in(seeds[3], 1), TOKENS // TOK_DEV)
    routes_turns = jax.random.permutation(jax.random.fold_in(seeds[3], 3), TOKENS // TOK_DEV)
    routes = jax.vmap(lambda own, number: deal_out(jax.random.fold_in(seeds[3], 2), own, number, TOK_DEV, EXPERTS, TOP, CAP, 2))(routes_keys, routes_turns).reshape((TOKENS, TOP))
    gain_attn = jnp.clip(1.0 + 0.1 * jax.random.normal(seeds[4], (LAYERS, D), jnp.float32), 0.5, 1.5).astype(jnp.bfloat16)
    wqkv = bell_draw(seeds[5], (LAYERS, D, 3 * D), D ** -0.5, 0.21875, ((1, 128),))
    wout = bell_draw(seeds[6], (LAYERS, D, D), (D // 16) ** -0.5, 0.875, ((1, 128),))
    bucket_bias_table = bell_draw(seeds[7], (LAYERS, BUCKETS, HEADS), 0.5, 3.0)
    gain_ffn = jnp.clip(1.0 + 0.1 * jax.random.normal(seeds[8], (LAYERS, D), jnp.float32), 0.5, 1.5).astype(jnp.bfloat16)
    router = bell_draw(seeds[9], (LAYERS, D, EXPERTS), D ** -0.5, 0.21875)
    w_in = bell_draw(seeds[10], (LAYERS, EXPERTS, D, FF), D ** -0.5, 0.21875, ((1, 16), (2, 8)))
    w_out = bell_draw(seeds[11], (LAYERS, EXPERTS, FF, D), (FF // 64) ** -0.5, 0.875, ((1, 16), (2, 8)))
    cotangent = bell_draw(seeds[12], (TOKENS, D), 1.0, 6.0, ((0, 128),), jnp.float32)
    return {"tokens": tokens, "segments": segments, "rel_bucket": rel_bucket, "routes": routes, "gain_attn": gain_attn, "wqkv": wqkv, "wout": wout, "bucket_bias_table": bucket_bias_table, "gain_ffn": gain_ffn, "router": router, "w_in": w_in, "w_out": w_out, "cotangent": cotangent}


EPS = 1e-06
MASKED = -1e+30
highest = lax.Precision.HIGHEST

@jax.custom_vjp
def low(v):
    return lax.optimization_barrier(v.astype(jnp.bfloat16)).astype(jnp.float32)

@jax.custom_vjp
def low_back(v):
    return v

def low_keep(v):
    return (low(v), None)

def low_pass(kept, grad):
    return (grad,)

def back_keep(v):
    return (v, None)

def back_low(kept, grad):
    return (low(grad),)
low.defvjp(low_keep, low_pass)
low_back.defvjp(back_keep, back_low)

def rms_norm(values, gain_row):
    return values * lax.rsqrt(lax.optimization_barrier(jnp.mean(values * values, axis=-1, keepdims=True)) + EPS) * gain_row

def expert_block(inputs):
    row_block, weight_in, weight_out = inputs
    pre_act = low_back(jnp.dot(row_block, weight_in, precision=highest))
    activated = low(jax.nn.gelu(pre_act))
    return low_back(low(jnp.dot(activated, weight_out, precision=highest)))

def reference(tokens, segments, rel_bucket, routes, gain_attn, wqkv, wout, bucket_bias_table, gain_ffn, router, w_in, w_out, cotangent):
    blocks = TOKENS // TOK_DEV
    positions = jnp.arange(SEQ_LEN, dtype=jnp.int32)
    distance = positions[:, None] - positions[None, :]
    causal = distance >= 0
    bucket_ids = jnp.take(rel_bucket, jnp.maximum(distance, 0).astype(jnp.int32))
    flat_routes = routes.reshape(blocks, TOK_DEV * TOP)
    expert_ids = jnp.arange(EXPERTS, dtype=jnp.int32)
    expert_hot = (flat_routes[:, :, None] == expert_ids[None, None, :]).astype(jnp.int32)
    rank_counts = jnp.cumsum(expert_hot, axis=1) - expert_hot
    slot_rank = lax.optimization_barrier(jnp.sum(rank_counts * expert_hot, axis=2))
    block_index_list = jnp.arange(blocks, dtype=jnp.int32)[:, None]
    slot_index = ((flat_routes * blocks + block_index_list) * CAP + slot_rank).reshape(-1).astype(jnp.int32)
    route_hot = (routes[:, :, None] == expert_ids[None, None, :]).astype(jnp.float32)
    scale = HEAD_DIM ** (-0.5)

    def attention(projected, table_rows):
        per_seq = projected.reshape(SEQS, SEQ_LEN, 3 * D)

        def attend_over_sequence(pair_item):
            seq_block, seg_row = pair_item
            query_heads = seq_block[:, :D].reshape(SEQ_LEN, HEADS, HEAD_DIM)
            key_heads = seq_block[:, D:2 * D].reshape(SEQ_LEN, HEADS, HEAD_DIM)
            value_heads = seq_block[:, 2 * D:].reshape(SEQ_LEN, HEADS, HEAD_DIM)
            scores = jnp.einsum('qhd,khd->hqk', query_heads, key_heads, precision=highest) * scale
            scores = low_back(scores + jnp.take(table_rows.T, bucket_ids, axis=1))
            allowed = causal & (seg_row[:, None] == seg_row[None, :])
            scores = jnp.where(allowed[None], scores, MASKED)
            weights_low = low(jax.nn.softmax(scores, axis=-1))
            combined = jnp.einsum('hqk,khd->qhd', weights_low, value_heads, precision=highest)
            return combined.reshape(SEQ_LEN, D)
        gathered = lax.map(jax.checkpoint(attend_over_sequence), (per_seq, segments))
        return low_back(low(gathered.reshape(TOKENS, D)))

    def forward(hidden, gains_a, proj_in, proj_out, tables, gains_f, routers, experts_in, experts_out):
        for layer_index in range(LAYERS):
            normed = low(rms_norm(hidden, gains_a[layer_index]))
            projected = low_back(low(jnp.dot(normed, proj_in[layer_index], precision=highest)))
            attended = attention(projected, tables[layer_index])
            middle = hidden + low_back(jnp.dot(attended, proj_out[layer_index], precision=highest))
            mixed_in = low(rms_norm(middle, gains_f[layer_index]))
            router_probs = jax.nn.softmax(jnp.dot(mixed_in, routers[layer_index], precision=highest), axis=-1)
            gate_values = lax.optimization_barrier(jnp.sum(router_probs[:, None, :] * route_hot, axis=2))
            pair_rows = jnp.repeat(mixed_in, TOP, axis=0)
            buffer = jnp.zeros((EXPERTS * blocks * CAP, D), dtype=mixed_in.dtype).at[slot_index].add(pair_rows)
            produced = lax.map(jax.checkpoint(expert_block), (buffer.reshape(EXPERTS, blocks * CAP, D), experts_in[layer_index], experts_out[layer_index]))
            returned = jnp.take(produced.reshape(-1, D), slot_index, axis=0).reshape(TOKENS, TOP, D)
            hidden = middle + lax.optimization_barrier(jnp.sum(gate_values[:, :, None] * returned, axis=1))
        return hidden
    floats = tuple((array.astype(jnp.float32) for array in (tokens, gain_attn, wqkv, wout, bucket_bias_table, gain_ffn, router, w_in, w_out)))
    result, pullback = jax.vjp(forward, *floats)
    gradients = pullback(cotangent.astype(jnp.float32))
    return (result.astype(jnp.bfloat16), gradients[0], gradients[1], gradients[2], gradients[3], gradients[4], gradients[5], gradients[6], gradients[7], gradients[8])
```

```python
import jax
import jax.numpy as jnp
from jax import lax
from jax.experimental import pallas as pl
from jax.experimental.pallas import tpu as pltpu
from jax.sharding import PartitionSpec as P

D = 768
HEADS = 12
HEAD_DIM = 64
PAIRS = HEADS // 2
TOP = 2
BUCKETS = 32
LAYERS = 2
BACK = 4
EPS = 1e-06
MASKED = -1e30
SCALE = HEAD_DIM**-0.5
BF = jnp.bfloat16
F32 = jnp.float32
highest = lax.Precision.HIGHEST
VMEM = pltpu.VMEM


def dot(a, b, contract=((1,), (0,))):
    return lax.dot_general(a, b, (contract, ((), ())), preferred_element_type=F32)


def inv_root(values):
    return lax.rsqrt(jnp.mean(values * values, axis=-1, keepdims=True) + EPS)


def norm_backward(values, scale_rows, gain_row, grad_out):
    scaled = grad_out * gain_row
    grad_gain = jnp.sum(grad_out * values * scale_rows, axis=0)
    cubed = scale_rows * scale_rows * scale_rows
    input_gradient = scale_rows * scaled - values * cubed * jnp.mean(
        values * scaled, axis=-1, keepdims=True
    )
    return (input_gradient, grad_gain)


def head_scores(q2, k2, low_lanes, head, allowed, bias_ref, width, span):
    mine = low_lanes if head % 2 == 0 else jnp.logical_not(low_lanes)
    q_head = jnp.where(mine, q2, jnp.zeros_like(q2))
    scores = dot(q_head, k2, ((1,), (1,))) * SCALE
    row = jnp.broadcast_to(bias_ref[head : head + 1, :], (q2.shape[0], span))
    bias = pltpu.roll(row, 0, 1, stride=1, stride_axis=0)[:, :width]
    return q_head, mine, jnp.where(allowed, scores + bias, MASKED)


def allowed_pairs(off_ref, segq_ref, segk_ref, rows, width):
    i = lax.broadcasted_iota(jnp.int32, (rows, width), 0)
    j = lax.broadcasted_iota(jnp.int32, (rows, width), 1)
    return (off_ref[0] + i - j >= 0) & (segq_ref[...] == segk_ref[...])


def attention_kernel(off_ref, q_ref, kv_ref, segq_ref, segk_ref, bias_ref, out_ref, lse_ref):
    rows, width, span = q_ref.shape[0], kv_ref.shape[0], bias_ref.shape[1]
    allowed = allowed_pairs(off_ref, segq_ref, segk_ref, rows, width)
    low_lanes = lax.broadcasted_iota(jnp.int32, (rows, 128), 1) < HEAD_DIM
    lane = lax.broadcasted_iota(jnp.int32, (rows, 128), 1)
    totals = jnp.zeros((rows, 128), F32)
    for pair in range(PAIRS):
        at = slice(pair * 128, pair * 128 + 128)
        q2, k2 = q_ref[:, at], kv_ref[:, at]
        v2 = kv_ref[:, D + pair * 128 : D + pair * 128 + 128]
        both = []
        for head in (2 * pair, 2 * pair + 1):
            _, _, scores = head_scores(q2, k2, low_lanes, head, allowed, bias_ref, width, span)
            row_max = jnp.max(scores, axis=1, keepdims=True)
            exponent = jnp.exp(scores - row_max)
            row_total = jnp.sum(exponent, axis=1, keepdims=True)
            weights = (exponent / row_total).astype(BF)
            both.append(dot(weights, v2))
            totals = jnp.where(lane == head, row_max + jnp.log(row_total), totals)
        out_ref[:, at] = jnp.where(low_lanes, both[0], both[1]).astype(BF)
    lse_ref[...] = totals


def attention_back_kernel(
    off_ref, q_ref, kv_ref, segq_ref, segk_ref, bias_ref, lse_ref, grad_ref, dq_ref, dkv_ref, diag_ref
):
    rows, width, span = q_ref.shape[0], kv_ref.shape[0], bias_ref.shape[1]
    allowed = allowed_pairs(off_ref, segq_ref, segk_ref, rows, width)
    low_lanes = lax.broadcasted_iota(jnp.int32, (rows, 128), 1) < HEAD_DIM
    lane = lax.broadcasted_iota(jnp.int32, (rows, 128), 1)
    i = lax.broadcasted_iota(jnp.int32, (rows, rows), 0)
    j = lax.broadcasted_iota(jnp.int32, (rows, rows), 1)
    flip = (i + j == rows - 1).astype(BF)
    for pair in range(PAIRS):
        at = slice(pair * 128, pair * 128 + 128)
        at_v = slice(D + pair * 128, D + pair * 128 + 128)
        q2, k2, v2, g2 = q_ref[:, at], kv_ref[:, at], kv_ref[:, at_v], grad_ref[:, at]
        dq, dk, dv = [], None, None
        for head in (2 * pair, 2 * pair + 1):
            q_head, mine, scores = head_scores(q2, k2, low_lanes, head, allowed, bias_ref, width, span)
            log_total = jnp.sum(jnp.where(lane == head, lse_ref[...], 0.0), axis=1, keepdims=True)
            probs = jnp.exp(scores - log_total)
            g_head = jnp.where(mine, g2, jnp.zeros_like(g2))
            grad_probs = dot(g_head, v2, ((1,), (1,)))
            inner = jnp.sum(probs * grad_probs, axis=1, keepdims=True)
            grad_scores = (probs * (grad_probs - inner)).astype(BF)
            dq.append(dot(grad_scores, k2))
            dk_head = dot(grad_scores, q_head, ((0,), (0,)))
            dv_head = dot(probs.astype(BF), g_head, ((0,), (0,)))
            dk = dk_head if dk is None else dk + dk_head
            dv = dv_head if dv is None else dv + dv_head
            turned = jnp.concatenate(
                [dot(flip, grad_scores), jnp.zeros((rows, span - width), F32)], axis=1
            )
            turned = pltpu.roll(turned, span - (rows - 1), 1, stride=1, stride_axis=0)
            diag_ref[head : head + 1, :] = jnp.sum(turned, axis=0, keepdims=True)
        dq_ref[:, at] = (jnp.where(low_lanes, dq[0], dq[1]) * SCALE).astype(BF)
        dkv_ref[:, at] = (dk * SCALE).astype(BF)
        dkv_ref[:, at_v] = dv.astype(BF)


def vmem_specs(n):
    return [pl.BlockSpec(memory_space=VMEM) for _ in range(n)]


def attention(off, queries, kv, segq, segk, bias):
    return pl.pallas_call(
        attention_kernel,
        out_shape=(
            jax.ShapeDtypeStruct(queries.shape, BF),
            jax.ShapeDtypeStruct((queries.shape[0], 128), F32),
        ),
        in_specs=[pl.BlockSpec(memory_space=pltpu.SMEM)] + vmem_specs(5),
        out_specs=tuple(vmem_specs(2)),
        compiler_params=pltpu.CompilerParams(vmem_limit_bytes=32 * 2**20),
    )(off, queries, kv, segq, segk, bias)


def attention_back(off, queries, kv, segq, segk, bias, lse, grad):
    return pl.pallas_call(
        attention_back_kernel,
        out_shape=(
            jax.ShapeDtypeStruct(queries.shape, BF),
            jax.ShapeDtypeStruct(kv.shape, BF),
            jax.ShapeDtypeStruct(bias.shape, F32),
        ),
        in_specs=[pl.BlockSpec(memory_space=pltpu.SMEM)] + vmem_specs(7),
        out_specs=tuple(vmem_specs(3)),
        compiler_params=pltpu.CompilerParams(vmem_limit_bytes=32 * 2**20),
    )(off, queries, kv, segq, segk, bias, lse, grad)


def to_peers(rows):
    return lax.all_to_all(rows, "grp", split_axis=0, concat_axis=0, tiled=True)


def gather_attn(wqkv, wout, layer_index):
    own = jnp.concatenate([wqkv[layer_index], wout[layer_index]], axis=1)
    own = own.reshape(-1, 128)
    full = lax.all_gather(lax.all_gather(own, "seq", axis=0, tiled=True), "grp", axis=0, tiled=True)
    return full.reshape(D, -1)


def gather_experts(w_in, w_out, layer_index):
    first = lax.all_gather(w_in[layer_index, 0], "seq", axis=0, tiled=True)
    second = lax.all_gather(w_out[layer_index, 0], "seq", axis=0, tiled=True)
    return first, second


def on_device(
    tokens,
    segments,
    rel_bucket,
    routes,
    gain_attn,
    wqkv,
    wout,
    bucket_bias_table,
    gain_ffn,
    router,
    w_in,
    w_out,
    cotangent,
):
    count_q = tokens.shape[0]
    experts = lax.axis_size("grp")
    blocks = lax.axis_size("seq")
    capacity = max(2, 3 * count_q * TOP // (2 * experts))
    window = (BACK + 1) * count_q
    span = window + count_q
    me = lax.axis_index("seq")
    first_block = jnp.clip(me - BACK, 0, blocks - BACK - 1)
    start = first_block * count_q
    off = (me * count_q - start).astype(jnp.int32)

    place = jnp.arange(span, dtype=jnp.int32)
    distance = off - jnp.where(place < window, place, place - span)
    pick = (distance[:, None] == jnp.arange(rel_bucket.shape[0], dtype=jnp.int32)[None, :]).astype(BF)
    bucket_at = dot(pick, rel_bucket.astype(BF)[:, None])[:, 0].astype(jnp.int32)
    in_range = (distance >= 0) & (distance < rel_bucket.shape[0])
    bucket_hot = (
        (bucket_at[None, :] == jnp.arange(BUCKETS, dtype=jnp.int32)[:, None]) & in_range[None, :]
    ).astype(BF)
    bias_rows = [dot(bucket_bias_table[l], bucket_hot, ((0,), (0,))) for l in range(LAYERS)]

    expert_ids = jnp.arange(experts, dtype=jnp.int32)
    flat_routes = jnp.concatenate([routes[:, 0], routes[:, 1]])
    hot = (flat_routes[:, None] == expert_ids[None, :]).astype(BF)
    number = jnp.arange(TOP * count_q, dtype=jnp.int32)
    ranks = dot((number[:, None] > number[None, :]).astype(BF), hot)
    rank = jnp.sum(ranks * hot.astype(F32), axis=1).astype(jnp.int32)
    target = flat_routes * capacity + rank
    slots = jnp.arange(experts * capacity, dtype=jnp.int32)
    dispatch = (slots[:, None] == target[None, :]).astype(BF)
    dispatch_tokens = dispatch[:, :count_q] + dispatch[:, count_q:]
    route_hot = hot.astype(F32).reshape(TOP, count_q, experts)

    seg_own = segments[0].astype(F32)
    seg_col = seg_own[:, None]
    hidden_state = tokens.astype(F32)
    gains_a, gains_f = gain_attn.astype(F32), gain_ffn.astype(F32)
    stored = []
    seg_keys = None
    attn_full = [gather_attn(wqkv, wout, l) for l in range(LAYERS)]
    expert_full = [gather_experts(w_in, w_out, l) for l in range(LAYERS)]
    for l in range(LAYERS):
        qkv_mat, out_mat = attn_full[l][:, : 3 * D], attn_full[l][:, 3 * D :]
        first_mat, second_mat = expert_full[l]
        scale_one = inv_root(hidden_state)
        normed = (hidden_state * scale_one * gains_a[l]).astype(BF)
        projected = dot(normed, qkv_mat).astype(BF)
        queries = projected[:, :D]
        kv_own = projected[:, D:]
        if l == 0:
            tail = jnp.broadcast_to(seg_col, (count_q, 128)).astype(BF)
            kv_own = jnp.concatenate([kv_own, tail], axis=1)
        kv = lax.all_gather(kv_own, "seq", axis=0, tiled=True)
        kv = lax.dynamic_slice_in_dim(kv, start, window, axis=0)
        if l == 0:
            seg_keys = kv[:, 2 * D].astype(F32)[None, :]
            kv = kv[:, : 2 * D]
        off_arr = off.reshape(1)
        attended, lse = attention(off_arr, queries, kv, seg_col, seg_keys, bias_rows[l])
        middle = hidden_state + dot(attended, out_mat)
        scale_two = inv_root(middle)
        mixed_in = (middle * scale_two * gains_f[l]).astype(BF)
        router_probs = jax.nn.softmax(dot(mixed_in, router[l]), axis=-1)
        gate_values = jnp.sum(router_probs[None] * route_hot, axis=2)
        send_rows = dot(dispatch_tokens, mixed_in).astype(BF)
        expert_rows = to_peers(send_rows.reshape(experts, capacity, D)).reshape(-1, D)
        pre_act = dot(expert_rows, first_mat)
        activated = jax.nn.gelu(pre_act).astype(BF)
        expert_out = dot(activated, second_mat).astype(BF)
        returned = to_peers(expert_out.reshape(experts, capacity, D)).reshape(-1, D)
        pair_out = dot(dispatch, returned, ((0,), (0,))).reshape(TOP, count_q, D)
        new_state = middle + jnp.sum(gate_values[:, :, None] * pair_out, axis=0)
        stored.append(
            (hidden_state, scale_one, normed, queries, kv, lse, attended, middle, scale_two,
             mixed_in, router_probs, gate_values, pair_out, expert_rows, pre_act, activated)
        )
        hidden_state = new_state
    out_tokens = hidden_state.astype(BF)

    grad_state = cotangent
    small = [None] * LAYERS
    attn_grads = [None] * LAYERS
    first_grads = [None] * LAYERS
    second_grads = [None] * LAYERS
    for l in reversed(range(LAYERS)):
        (state_in, scale_one, normed, queries, kv, lse, attended, middle, scale_two,
         mixed_in, router_probs, gate_values, pair_out, expert_rows, pre_act, activated) = stored[l]
        qkv_mat, out_mat = attn_full[l][:, : 3 * D], attn_full[l][:, 3 * D :]
        first_mat, second_mat = expert_full[l]
        grad_gates = jnp.sum(grad_state[None] * pair_out, axis=2)
        grad_pairs = (gate_values[:, :, None] * grad_state[None]).astype(BF).reshape(-1, D)
        send_grads = dot(dispatch, grad_pairs).astype(BF)
        grad_rows = to_peers(send_grads.reshape(experts, capacity, D)).reshape(-1, D)
        grad_act = dot(grad_rows, second_mat, ((1,), (1,)))
        _, gelu_pull = jax.vjp(jax.nn.gelu, pre_act)
        grad_pre = gelu_pull(grad_act)[0].astype(BF)
        grad_inputs = dot(grad_pre, first_mat, ((1,), (1,))).astype(BF)
        grad_back = to_peers(grad_inputs.reshape(experts, capacity, D)).reshape(-1, D)
        grad_second = dot(activated, grad_rows, ((0,), (0,))).astype(BF)
        grad_first = dot(expert_rows, grad_pre, ((0,), (0,))).astype(BF)
        first_grads[l] = lax.psum_scatter(grad_first, "seq", scatter_dimension=0, tiled=True).astype(F32)
        second_grads[l] = lax.psum_scatter(grad_second, "seq", scatter_dimension=0, tiled=True).astype(F32)
        grad_mixed = dot(dispatch_tokens, grad_back, ((0,), (0,)))
        grad_probs = jnp.sum(grad_gates[:, :, None] * route_hot, axis=0)
        grad_logits = router_probs * (
            grad_probs - jnp.sum(router_probs * grad_probs, axis=-1, keepdims=True)
        )
        router_grad = jnp.dot(mixed_in.astype(F32).T, grad_logits, precision=highest)
        grad_mixed = grad_mixed + jnp.dot(grad_logits, router[l].astype(F32).T, precision=highest)
        grad_mid, gain_f_grad = norm_backward(middle, scale_two, gains_f[l], grad_mixed)
        grad_mid = grad_mid + grad_state
        branch_grad = grad_mid.astype(BF)
        grad_out_proj = dot(attended, branch_grad, ((0,), (0,))).astype(BF)
        grad_attended = dot(branch_grad, out_mat, ((1,), (1,))).astype(BF)
        dq, dkv, diag = attention_back(
            off_arr, queries, kv, seg_col, seg_keys, bias_rows[l], lse, grad_attended
        )
        table_grad = lax.dot_general(
            bucket_hot.astype(F32), diag, (((1,), (1,)), ((), ())), precision=highest
        )
        dkv_all = lax.dynamic_update_slice_in_dim(
            jnp.zeros((blocks * count_q, 2 * D), BF), dkv, start, axis=0
        )
        dkv_own = lax.psum_scatter(dkv_all, "seq", scatter_dimension=0, tiled=True)
        grad_proj = jnp.concatenate([dq, dkv_own], axis=1)
        grad_in_proj = dot(normed, grad_proj, ((0,), (0,))).astype(BF)
        grad_normed = dot(grad_proj, qkv_mat, ((1,), (1,)))
        grad_prev, gain_a_grad = norm_backward(state_in, scale_one, gains_a[l], grad_normed)
        grad_state = grad_mid + grad_prev
        both = jnp.concatenate([grad_in_proj, grad_out_proj], axis=1).reshape(-1, 128)
        both = lax.psum_scatter(both, "grp", scatter_dimension=0, tiled=True)
        both = lax.psum_scatter(both, "seq", scatter_dimension=0, tiled=True)
        attn_grads[l] = both.reshape(-1, 4 * D).astype(F32)
        small[l] = (gain_a_grad, gain_f_grad, router_grad, table_grad)
    sizes = [D, D, D * experts, BUCKETS * HEADS]
    flat = jnp.concatenate([part.reshape(-1) for l in range(LAYERS) for part in small[l]])
    flat = lax.psum(flat.reshape(-1, 128), ("grp", "seq")).reshape(LAYERS, -1)
    sums, at = [], 0
    for size in sizes:
        sums.append(flat[:, at : at + size])
        at += size
    attn = jnp.stack(attn_grads)
    return (
        out_tokens,
        grad_state,
        sums[0],
        attn[:, :, : 3 * D],
        attn[:, :, 3 * D :],
        sums[3].reshape(LAYERS, BUCKETS, HEADS),
        sums[1],
        sums[2].reshape(LAYERS, D, experts),
        jnp.stack(first_grads)[:, None],
        jnp.stack(second_grads)[:, None],
    )


def solution(mesh):
    rows = P(("grp", "seq"), None)
    slab = P(None, ("grp", "seq"), None)
    expert = P(None, "grp", "seq", None)
    return jax.shard_map(
        on_device,
        mesh=mesh,
        in_specs=(
            rows, P("grp", "seq"), P(), rows, P(), slab, slab, P(), P(), P(), expert, expert, rows,
        ),
        out_specs=(rows, rows, P(), slab, slab, P(), P(), P(), expert, expert),
        check_vma=False,
    )
```

```python
import jax
import jax.numpy as jnp
from jax import lax
from jax.experimental import pallas as pl
from jax.experimental.pallas import tpu as pltpu
from jax.sharding import PartitionSpec as P

D = 768
HEADS = 12
HEAD_DIM = 64
PAIRS = HEADS // 2
TOP = 2
BUCKETS = 32
LAYERS = 2
BACK = 4
EPS = 1e-06
MASKED = -1e30
SCALE = HEAD_DIM**-0.5
BF = jnp.bfloat16
F32 = jnp.float32
highest = lax.Precision.HIGHEST
VMEM = pltpu.VMEM


def dot(a, b, contract=((1,), (0,))):
    return lax.dot_general(a, b, (contract, ((), ())), preferred_element_type=F32)


def inv_root(values):
    return lax.rsqrt(jnp.mean(values * values, axis=-1, keepdims=True) + EPS)


def norm_backward(values, scale_rows, gain_row, grad_out):
    scaled = grad_out * gain_row
    grad_gain = jnp.sum(grad_out * values * scale_rows, axis=0)
    cubed = scale_rows * scale_rows * scale_rows
    input_gradient = scale_rows * scaled - values * cubed * jnp.mean(
        values * scaled, axis=-1, keepdims=True
    )
    return (input_gradient, grad_gain)


def head_scores(q2, k2, low_lanes, head, allowed, bias_ref, width, span):
    mine = low_lanes if head % 2 == 0 else jnp.logical_not(low_lanes)
    q_head = jnp.where(mine, q2, jnp.zeros_like(q2))
    scores = dot(q_head, k2, ((1,), (1,))) * SCALE
    row = jnp.broadcast_to(bias_ref[head : head + 1, :], (q2.shape[0], span))
    bias = pltpu.roll(row, 0, 1, stride=1, stride_axis=0)[:, :width]
    return q_head, mine, jnp.where(allowed, scores + bias, MASKED)


def first_key_block():
    me = lax.axis_index("seq")
    return me // BACK * (me % BACK)


def allowed_pairs(off_ref, segq_ref, segk_ref, rows, width):
    i = lax.broadcasted_iota(jnp.int32, (rows, width), 0)
    j = lax.broadcasted_iota(jnp.int32, (rows, width), 1)
    return (off_ref[0] + i - j >= 0) & (segq_ref[...] == segk_ref[...])


def attention_kernel(off_ref, q_ref, kv_ref, segq_ref, segk_ref, bias_ref, out_ref, lse_ref):
    rows, width, span = q_ref.shape[0], segk_ref.shape[1], bias_ref.shape[1]
    first = first_key_block()
    window = pl.ds(pl.multiple_of(first * rows, rows), width)
    allowed = allowed_pairs(off_ref, segq_ref, segk_ref, rows, width)
    low_lanes = lax.broadcasted_iota(jnp.int32, (rows, 128), 1) < HEAD_DIM
    lane = lax.broadcasted_iota(jnp.int32, (rows, 128), 1)
    totals = jnp.zeros((rows, 128), F32)
    for pair in range(PAIRS):
        at = slice(pair * 128, pair * 128 + 128)
        q2, k2 = q_ref[:, at], kv_ref[window, at]
        v2 = kv_ref[window, D + pair * 128 : D + pair * 128 + 128]
        both = []
        for head in (2 * pair, 2 * pair + 1):
            _, _, scores = head_scores(q2, k2, low_lanes, head, allowed, bias_ref, width, span)
            row_max = jnp.max(scores, axis=1, keepdims=True)
            exponent = jnp.exp(scores - row_max)
            row_total = jnp.sum(exponent, axis=1, keepdims=True)
            weights = (exponent / row_total).astype(BF)
            both.append(dot(weights, v2))
            totals = jnp.where(lane == head, row_max + jnp.log(row_total), totals)
        out_ref[:, at] = jnp.where(low_lanes, both[0], both[1]).astype(BF)
    lse_ref[...] = totals


def attention_back_kernel(
    off_ref, q_ref, kv_ref, segq_ref, segk_ref, bias_ref, lse_ref, grad_ref, dq_ref, dkv_ref, diag_ref
):
    rows, width, span = q_ref.shape[0], segk_ref.shape[1], bias_ref.shape[1]
    first = first_key_block()
    window = pl.ds(pl.multiple_of(first * rows, rows), width)
    allowed = allowed_pairs(off_ref, segq_ref, segk_ref, rows, width)
    low_lanes = lax.broadcasted_iota(jnp.int32, (rows, 128), 1) < HEAD_DIM
    lane = lax.broadcasted_iota(jnp.int32, (rows, 128), 1)
    i = lax.broadcasted_iota(jnp.int32, (rows, rows), 0)
    j = lax.broadcasted_iota(jnp.int32, (rows, rows), 1)
    flip = (i + j == rows - 1).astype(BF)
    dkv_ref[...] = jnp.zeros_like(dkv_ref)
    for pair in range(PAIRS):
        at = slice(pair * 128, pair * 128 + 128)
        at_v = slice(D + pair * 128, D + pair * 128 + 128)
        q2, k2, v2, g2 = q_ref[:, at], kv_ref[window, at], kv_ref[window, at_v], grad_ref[:, at]
        dq, dk, dv = [], None, None
        for head in (2 * pair, 2 * pair + 1):
            q_head, mine, scores = head_scores(q2, k2, low_lanes, head, allowed, bias_ref, width, span)
            log_total = jnp.sum(jnp.where(lane == head, lse_ref[...], 0.0), axis=1, keepdims=True)
            probs = jnp.exp(scores - log_total)
            g_head = jnp.where(mine, g2, jnp.zeros_like(g2))
            grad_probs = dot(g_head, v2, ((1,), (1,)))
            inner = jnp.sum(probs * grad_probs, axis=1, keepdims=True)
            grad_scores = (probs * (grad_probs - inner)).astype(BF)
            dq.append(dot(grad_scores, k2))
            dk_head = dot(grad_scores, q_head, ((0,), (0,)))
            dv_head = dot(probs.astype(BF), g_head, ((0,), (0,)))
            dk = dk_head if dk is None else dk + dk_head
            dv = dv_head if dv is None else dv + dv_head
            turned = jnp.concatenate(
                [dot(flip, grad_scores), jnp.zeros((rows, span - width), F32)], axis=1
            )
            turned = pltpu.roll(turned, span - (rows - 1), 1, stride=1, stride_axis=0)
            diag_ref[head : head + 1, :] = jnp.sum(turned, axis=0, keepdims=True)
        dq_ref[:, at] = (jnp.where(low_lanes, dq[0], dq[1]) * SCALE).astype(BF)
        blocks = pl.ds(first, width // rows)
        dkv_ref[blocks, :, at] = (dk * SCALE).astype(BF).reshape(-1, rows, 128)
        dkv_ref[blocks, :, at_v] = dv.astype(BF).reshape(-1, rows, 128)


def vmem_specs(n):
    return [pl.BlockSpec(memory_space=VMEM) for _ in range(n)]


def attention(off, queries, kv, segq, segk, bias):
    return pl.pallas_call(
        attention_kernel,
        out_shape=(
            jax.ShapeDtypeStruct(queries.shape, BF),
            jax.ShapeDtypeStruct((queries.shape[0], 128), F32),
        ),
        in_specs=[pl.BlockSpec(memory_space=pltpu.SMEM)] + vmem_specs(5),
        out_specs=tuple(vmem_specs(2)),
        compiler_params=pltpu.CompilerParams(vmem_limit_bytes=32 * 2**20),
    )(off, queries, kv, segq, segk, bias)


def attention_back(off, queries, kv, segq, segk, bias, lse, grad):
    return pl.pallas_call(
        attention_back_kernel,
        out_shape=(
            jax.ShapeDtypeStruct(queries.shape, BF),
            jax.ShapeDtypeStruct((kv.shape[0] // queries.shape[0], queries.shape[0], kv.shape[1]), BF),
            jax.ShapeDtypeStruct(bias.shape, F32),
        ),
        in_specs=[pl.BlockSpec(memory_space=pltpu.SMEM)] + vmem_specs(7),
        out_specs=tuple(vmem_specs(3)),
        compiler_params=pltpu.CompilerParams(vmem_limit_bytes=32 * 2**20),
    )(off, queries, kv, segq, segk, bias, lse, grad)


MESH_ID = pl.DeviceIdType.MESH
SIDE = 4


def place_of_device():
    grp, seq = lax.axis_index("grp"), lax.axis_index("seq")
    return [grp // SIDE, grp % SIDE, seq // 2], seq % 2


def device_at(coords, core):
    return (coords[0] * SIDE + coords[1], coords[2] * 2 + core)


def moved(coords, axis, delta):
    return [(c + delta) % SIDE if a == axis else c for a, c in enumerate(coords)]


def remote(src, dst, send_sem, recv_sem, device):
    return pltpu.make_async_remote_copy(
        src_ref=src, dst_ref=dst, send_sem=send_sem, recv_sem=recv_sem, device_id=device, device_id_type=MESH_ID
    )


def greet(devices):
    barrier = pltpu.get_barrier_semaphore()
    for device in devices:
        pl.semaphore_signal(barrier, inc=1, device_id=device, device_id_type=MESH_ID)
    pl.semaphore_wait(barrier, len(devices))


def all_partners(coords, core):
    partners = [device_at(moved(coords, a, d), core) for a in range(3) for d in range(1, SIDE)]
    return partners + [device_at(coords, 1 - core)]


def attn_gather_kernel(own_ref, seg_ref, full_ref, segs_ref, send_sem, recv_sem, core_send, core_recv, seg_send, seg_recv):
    coords, core = place_of_device()
    sibling = device_at(coords, 1 - core)
    y, x, z = coords
    for p in range(3):
        full_ref[p, y, x, z, core] = own_ref[p]
    segs_ref[z, core] = seg_ref[...]
    greet(all_partners(coords, core))

    def region(p, free, fixed=None):
        index = [slice(None) if a in free else coords[a] for a in range(3)]
        if fixed is not None:
            index[fixed[0]] = fixed[1]
        return full_ref.at[(p, *index, core)]

    seg_copies = []
    for d in range(1, SIDE):
        one = segs_ref.at[z, core]
        seg_copies.append(remote(one, one, seg_send.at[d - 1], seg_recv.at[d - 1], device_at(moved(coords, 2, d), core)))
        seg_copies[-1].start()
    copies = {}
    core_copies = []

    def to_sibling(part, number):
        core_copies.append(remote(part, part, core_send.at[number], core_recv.at[number], sibling))
        core_copies[-1].start()

    for k in range(3):
        for p in range(3):
            if k:
                for d in (1, 3, 2):
                    copies[k - 1, p, d].wait_recv()
            axis, free = (p + k) % 3, [(p + i) % 3 for i in range(k)]
            part = region(p, free)
            for d in (1, 3, 2):
                copies[k, p, d] = remote(
                    part, part, send_sem.at[k, p, d - 1], recv_sem.at[k, p, d - 1],
                    device_at(moved(coords, axis, d), core),
                )
                copies[k, p, d].start()
            if k == 2:
                to_sibling(part, 4 * p)
    for copy in seg_copies:
        copy.wait_recv()
    part = segs_ref.at[:, core]
    seg_last = remote(part, part, seg_send.at[3], seg_recv.at[3], sibling)
    seg_last.start()
    for d in (1, 3, 2):
        for p in range(3):
            axis = (p + 2) % 3
            copies[2, p, d].wait_recv()
            came = (coords[axis] + SIDE - d) % SIDE
            to_sibling(region(p, [a for a in range(3) if a != axis], (axis, came)), 4 * p + d)
    for copy in copies.values():
        copy.wait_send()
    for copy in seg_copies:
        copy.wait_send()
    seg_last.wait()
    for copy in core_copies:
        copy.wait()


def attn_gather(own, seg):
    sems = [pltpu.SemaphoreType.DMA((3, 3, 3))] * 2 + [pltpu.SemaphoreType.DMA((12,))] * 2
    sems += [pltpu.SemaphoreType.DMA((4,))] * 2
    return pl.pallas_call(
        attn_gather_kernel,
        out_shape=(
            jax.ShapeDtypeStruct((3, SIDE, SIDE, SIDE, 2) + own.shape[1:], BF),
            jax.ShapeDtypeStruct((SIDE, 2) + seg.shape, F32),
        ),
        in_specs=vmem_specs(2),
        out_specs=tuple(vmem_specs(2)),
        scratch_shapes=sems,
        compiler_params=pltpu.CompilerParams(
            collective_id=0, has_side_effects=True, vmem_limit_bytes=40 * 2**20
        ),
    )(own, seg)


def reduce_kernel(
    x_ref, small_ref, out_ref, small_out, got_core, y_ref, got_one, z_ref, got_two, w_ref, got_three,
    s_core, s_got, core_send, core_recv, send_sem, recv_sem, s_core_send, s_core_recv, s_send, s_recv,
):
    coords, core = place_of_device()
    sibling = device_at(coords, 1 - core)
    greet(all_partners(coords, core))
    first = []
    for p in range(3):
        copy = remote(
            x_ref.at[p, :, :, :, 1 - core], got_core.at[p], core_send.at[p], core_recv.at[p], sibling
        )
        copy.start()
        first.append(copy)
    s_first = remote(small_ref, s_core, s_core_send, s_core_recv, sibling)
    s_first.start()

    def spread(p, k, source, target):
        axis = (p + k) % 3
        left = [a for a in range(3) if a not in [(p + i) % 3 for i in range(k)]]
        out = []
        for d in (1, 3, 2):
            to = moved(coords, axis, d)
            index = tuple(to[axis] if a == axis else slice(None) for a in left)
            copy = remote(
                source.at[(p, *index)], target.at[p, d - 1], send_sem.at[k, p, d - 1], recv_sem.at[k, p, d - 1],
                device_at(to, core),
            )
            copy.start()
            out.append(copy)
        return out

    def spread_small(p, k):
        axis, out = (p + k) % 3, []
        for d in (1, 3, 2):
            copy = remote(
                s_got.at[k, p, 0], s_got.at[k, p, d], s_send.at[k, p, d - 1], s_recv.at[k, p, d - 1],
                device_at(moved(coords, axis, d), core),
            )
            copy.start()
            out.append(copy)
        return out

    def small_sum(p, k):
        axis = (p + k) % 3
        total = s_got[k, p, coords[axis]]
        for v in range(1, SIDE):
            total = total + s_got[k, p, (coords[axis] + SIDE - v) % SIDE]
        return total

    sent, s_sent = {}, {}
    s_first.wait()
    for p in range(3):
        s_got[0, p, 0] = small_ref[p] + s_core[p]
        s_sent[0, p] = spread_small(p, 0)
    for p in range(3):
        first[p].wait()

        def add_core(i, carry, p=p):
            a, b, c = i // (SIDE * SIDE), i // SIDE % SIDE, i % SIDE
            total = x_ref[p, a, b, c, core].astype(F32) + got_core[p, a, b, c].astype(F32)
            y_ref[p, a, b, c] = total.astype(BF)
            return carry

        lax.fori_loop(0, SIDE**3, add_core, 0)
        sent[0, p] = spread(p, 0, y_ref, got_one)
    for p in range(3):
        for copy in s_sent[0, p]:
            copy.wait()
        s_got[1, p, 0] = small_sum(p, 0)
        s_sent[1, p] = spread_small(p, 1)
    for p in range(3):
        for copy in sent[0, p]:
            copy.wait()
        axis = p

        def add_one(i, carry, p=p, axis=axis):
            a, b = i // SIDE, i % SIDE
            index = [a, b]
            index.insert(axis, coords[axis])
            total = y_ref[(p, *index)].astype(F32)
            for d in range(3):
                total = total + got_one[p, d, a, b].astype(F32)
            z_ref[p, a, b] = total.astype(BF)
            return carry

        lax.fori_loop(0, SIDE**2, add_one, 0)
        sent[1, p] = spread(p, 1, z_ref, got_two)
    for p in range(3):
        for copy in s_sent[1, p]:
            copy.wait()
        s_got[2, p, 0] = small_sum(p, 1)
        s_sent[2, p] = spread_small(p, 2)
    for p in range(3):
        for copy in sent[1, p]:
            copy.wait()
        axis = (p + 1) % 3
        left = [a for a in range(3) if a != p]

        def add_two(i, carry, p=p, axis=axis, left=left):
            index = tuple(coords[axis] if a == axis else i for a in left)
            total = z_ref[(p, *index)].astype(F32)
            for d in range(3):
                total = total + got_two[p, d, i].astype(F32)
            w_ref[p, i] = total.astype(BF)
            return carry

        lax.fori_loop(0, SIDE, add_two, 0)
        sent[2, p] = spread(p, 2, w_ref, got_three)
    for p in range(3):
        for copy in s_sent[2, p]:
            copy.wait()
        small_out[p] = small_sum(p, 2)
    for p in range(3):
        for copy in sent[2, p]:
            copy.wait()
        total = w_ref[p, coords[(p + 2) % 3]].astype(F32)
        for d in range(3):
            total = total + got_three[p, d].astype(F32)
        out_ref[p] = total


def reduce_all(x, small):
    block, part = x.shape[-2:], small.shape[1:]
    dma = pltpu.SemaphoreType.DMA
    return pl.pallas_call(
        reduce_kernel,
        out_shape=(jax.ShapeDtypeStruct((3,) + block, F32), jax.ShapeDtypeStruct(small.shape, F32)),
        in_specs=vmem_specs(2),
        out_specs=tuple(vmem_specs(2)),
        scratch_shapes=[
            VMEM((3, SIDE, SIDE, SIDE) + block, BF),
            VMEM((3, SIDE, SIDE, SIDE) + block, BF),
            VMEM((3, 3, SIDE, SIDE) + block, BF),
            VMEM((3, SIDE, SIDE) + block, BF),
            VMEM((3, 3, SIDE) + block, BF),
            VMEM((3, SIDE) + block, BF),
            VMEM((3, 3) + block, BF),
            VMEM(small.shape, F32),
            VMEM((3, 3, SIDE) + part, F32),
            dma((3,)), dma((3,)), dma((3, 3, 3)), dma((3, 3, 3)), dma(()), dma(()), dma((3, 3, 3)), dma((3, 3, 3)),
        ],
        compiler_params=pltpu.CompilerParams(
            collective_id=1, has_side_effects=True, vmem_limit_bytes=50 * 2**20
        ),
    )(x, small)


def kv_gather(own_ref, kv_ref, send_sem, recv_sem):
    coords, core = place_of_device()
    z, rows = coords[2], own_ref.shape[0]
    half = rows // 2
    up, down = moved(coords, 2, 1), moved(coords, 2, 3)
    up_z, down_z, far_z = (z + 1) % SIDE, (z + 3) % SIDE, (z + 2) % SIDE
    sibling = device_at(coords, 1 - core)

    def block(at, start=0, size=rows):
        return kv_ref.at[pl.ds(pl.multiple_of((at * 2 + core) * rows + start, half), size)]

    copies = []

    def send(part, number, device):
        copy = remote(part, part, send_sem.at[number], recv_sem.at[number], device)
        copy.start()
        copies.append(copy)
        return copy

    kv_ref[pl.ds(pl.multiple_of((z * 2 + core) * rows, rows), rows), :] = own_ref[...]
    greet([device_at(up, core), device_at(down, core), sibling])
    went_up = send(block(z), 0, device_at(up, core))
    went_down = send(block(z), 1, device_at(down, core))
    from_core = [send(block(z), 2, sibling)]
    went_up.wait_recv()
    far_up = send(block(down_z, 0, half), 3, device_at(up, core))
    from_core.append(send(block(down_z), 4, sibling))
    went_down.wait_recv()
    far_down = send(block(up_z, half, half), 5, device_at(down, core))
    from_core.append(send(block(up_z), 6, sibling))
    far_up.wait_recv()
    from_core.append(send(block(far_z, 0, half), 7, sibling))
    far_down.wait_recv()
    from_core.append(send(block(far_z, half, half), 8, sibling))
    for copy in from_core:
        copy.wait_recv()
    for copy in copies:
        copy.wait_send()


def kv_scatter(grads_ref, out_ref, got_core, sums, got_far, got_near, send_sem, recv_sem):
    coords, core = place_of_device()
    z, rows = coords[2], out_ref.shape[0]
    half = rows // 2
    up, down = device_at(moved(coords, 2, 1), core), device_at(moved(coords, 2, 3), core)
    up_z, down_z, far_z = (z + 1) % SIDE, (z + 3) % SIDE, (z + 2) % SIDE
    sibling = device_at(coords, 1 - core)
    greet([up, down, sibling])
    copies = []

    def send(src, dst, number, device):
        copy = remote(src, dst, send_sem.at[number], recv_sem.at[number], device)
        copy.start()
        copies.append(copy)
        return copy

    order = [far_z, up_z, down_z, z]
    cross = [send(grads_ref.at[at * 2 + 1 - core], got_core.at[n], n, sibling) for n, at in enumerate(order)]

    def total(n):
        cross[n].wait_recv()
        return grads_ref[order[n] * 2 + core].astype(F32) + got_core[n].astype(F32)

    sums[0] = total(0).astype(BF)
    far_up = send(sums.at[0, pl.ds(0, half)], got_far.at[0], 4, up)
    far_down = send(sums.at[0, pl.ds(half, half)], got_far.at[1], 5, down)
    up_sum, down_sum = total(1), total(2)
    sums[1, half:] = up_sum[half:].astype(BF)
    sums[2, :half] = down_sum[:half].astype(BF)
    far_up.wait_recv()
    sums[1, :half] = (up_sum[:half] + got_far[0].astype(F32)).astype(BF)
    near_up = send(sums.at[1], got_near.at[0], 6, up)
    far_down.wait_recv()
    sums[2, half:] = (down_sum[half:] + got_far[1].astype(F32)).astype(BF)
    near_down = send(sums.at[2], got_near.at[1], 7, down)
    own = total(3)
    near_up.wait_recv()
    near_down.wait_recv()
    out_ref[...] = (own + got_near[0].astype(F32) + got_near[1].astype(F32)).astype(BF)
    for copy in copies:
        copy.wait_send()

def gather_keys(own):
    return pl.pallas_call(
        kv_gather,
        out_shape=jax.ShapeDtypeStruct((2 * SIDE * own.shape[0], own.shape[1]), BF),
        in_specs=vmem_specs(1),
        out_specs=vmem_specs(1)[0],
        scratch_shapes=[pltpu.SemaphoreType.DMA((9,))] * 2,
        compiler_params=pltpu.CompilerParams(
            collective_id=2, has_side_effects=True, vmem_limit_bytes=20 * 2**20
        ),
    )(own)


def scatter_key_grads(grads):
    block = grads.shape[1:]
    return pl.pallas_call(
        kv_scatter,
        out_shape=jax.ShapeDtypeStruct(block, BF),
        in_specs=vmem_specs(1),
        out_specs=vmem_specs(1)[0],
        scratch_shapes=[
            VMEM((SIDE,) + block, BF),
            VMEM((3,) + block, BF),
            VMEM((2, block[0] // 2, block[1]), BF),
            VMEM((2,) + block, BF),
            pltpu.SemaphoreType.DMA((8,)),
            pltpu.SemaphoreType.DMA((8,)),
        ],
        compiler_params=pltpu.CompilerParams(
            collective_id=3, has_side_effects=True, vmem_limit_bytes=20 * 2**20
        ),
    )(grads)


def to_peers(rows):
    return lax.all_to_all(rows, "grp", split_axis=0, concat_axis=0, tiled=True)


def gather_attn(wqkv, wout, segments):
    layers, shard = wqkv.shape[0], wqkv.shape[1]
    own = jnp.concatenate([wqkv, wout], axis=2).reshape(3, -1, 128)
    seg = jnp.broadcast_to(segments.astype(F32), (8, segments.shape[1]))
    full, segs = attn_gather(own, seg)
    full = full.reshape(3, 2 * SIDE**3, -1, 128).transpose(1, 0, 2, 3)
    full = full.reshape(2 * SIDE**3, layers, shard, -1).transpose(1, 0, 2, 3)
    return full.reshape(layers, 2 * SIDE**3 * shard, -1), segs[:, :, 0].reshape(1, -1)


def gather_experts(w_in, w_out, layer_index):
    first = lax.all_gather(w_in[layer_index, 0], "seq", axis=0, tiled=True)
    second = lax.all_gather(w_out[layer_index, 0], "seq", axis=0, tiled=True)
    return first, second


def on_device(
    tokens,
    segments,
    rel_bucket,
    routes,
    gain_attn,
    wqkv,
    wout,
    bucket_bias_table,
    gain_ffn,
    router,
    w_in,
    w_out,
    cotangent,
):
    count_q = tokens.shape[0]
    experts = lax.axis_size("grp")
    capacity = max(2, 3 * count_q * TOP // (2 * experts))
    window = (BACK + 1) * count_q
    span = window + count_q
    me = lax.axis_index("seq")
    start = first_key_block() * count_q
    off = (me * count_q - start).astype(jnp.int32)

    place = jnp.arange(span, dtype=jnp.int32)
    distance = off - jnp.where(place < window, place, place - span)
    pick = (distance[:, None] == jnp.arange(rel_bucket.shape[0], dtype=jnp.int32)[None, :]).astype(BF)
    bucket_at = dot(pick, rel_bucket.astype(BF)[:, None])[:, 0].astype(jnp.int32)
    in_range = (distance >= 0) & (distance < rel_bucket.shape[0])
    bucket_hot = (
        (bucket_at[None, :] == jnp.arange(BUCKETS, dtype=jnp.int32)[:, None]) & in_range[None, :]
    ).astype(BF)
    bias_rows = [dot(bucket_bias_table[l], bucket_hot, ((0,), (0,))) for l in range(LAYERS)]

    expert_ids = jnp.arange(experts, dtype=jnp.int32)
    flat_routes = jnp.concatenate([routes[:, 0], routes[:, 1]])
    hot = (flat_routes[:, None] == expert_ids[None, :]).astype(BF)
    number = jnp.arange(TOP * count_q, dtype=jnp.int32)
    ranks = dot((number[:, None] > number[None, :]).astype(BF), hot)
    rank = jnp.sum(ranks * hot.astype(F32), axis=1).astype(jnp.int32)
    target = flat_routes * capacity + rank
    slots = jnp.arange(experts * capacity, dtype=jnp.int32)
    dispatch = (slots[:, None] == target[None, :]).astype(BF)
    dispatch_tokens = dispatch[:, :count_q] + dispatch[:, count_q:]
    route_hot = hot.astype(F32).reshape(TOP, count_q, experts)

    seg_own = segments[0].astype(F32)
    seg_col = seg_own[:, None]
    hidden_state = tokens.astype(F32)
    gains_a, gains_f = gain_attn.astype(F32), gain_ffn.astype(F32)
    stored = []
    attn_full, segs = gather_attn(wqkv, wout, segments)
    seg_keys = lax.dynamic_slice_in_dim(segs, start, window, axis=1)
    expert_full = [gather_experts(w_in, w_out, l) for l in range(LAYERS)]
    for l in range(LAYERS):
        qkv_mat, out_mat = attn_full[l][:, : 3 * D], attn_full[l][:, 3 * D :]
        first_mat, second_mat = expert_full[l]
        scale_one = inv_root(hidden_state)
        normed = (hidden_state * scale_one * gains_a[l]).astype(BF)
        projected = dot(normed, qkv_mat).astype(BF)
        queries = projected[:, :D]
        kv_own = projected[:, D:]
        kv = gather_keys(kv_own)
        off_arr = off.reshape(1)
        attended, lse = attention(off_arr, queries, kv, seg_col, seg_keys, bias_rows[l])
        middle = hidden_state + dot(attended, out_mat)
        scale_two = inv_root(middle)
        mixed_in = (middle * scale_two * gains_f[l]).astype(BF)
        router_probs = jax.nn.softmax(dot(mixed_in, router[l]), axis=-1)
        gate_values = jnp.sum(router_probs[None] * route_hot, axis=2)
        send_rows = dot(dispatch_tokens, mixed_in).astype(BF)
        expert_rows = to_peers(send_rows.reshape(experts, capacity, D)).reshape(-1, D)
        pre_act = dot(expert_rows, first_mat)
        activated = jax.nn.gelu(pre_act).astype(BF)
        expert_out = dot(activated, second_mat).astype(BF)
        returned = to_peers(expert_out.reshape(experts, capacity, D)).reshape(-1, D)
        pair_out = dot(dispatch, returned, ((0,), (0,))).reshape(TOP, count_q, D)
        new_state = middle + jnp.sum(gate_values[:, :, None] * pair_out, axis=0)
        stored.append(
            (hidden_state, scale_one, normed, queries, kv, lse, attended, middle, scale_two,
             mixed_in, router_probs, gate_values, pair_out, expert_rows, pre_act, activated)
        )
        hidden_state = new_state
    out_tokens = hidden_state.astype(BF)

    grad_state = cotangent
    small = [None] * LAYERS
    attn_grads = [None] * LAYERS
    first_grads = [None] * LAYERS
    second_grads = [None] * LAYERS
    for l in reversed(range(LAYERS)):
        (state_in, scale_one, normed, queries, kv, lse, attended, middle, scale_two,
         mixed_in, router_probs, gate_values, pair_out, expert_rows, pre_act, activated) = stored[l]
        qkv_mat, out_mat = attn_full[l][:, : 3 * D], attn_full[l][:, 3 * D :]
        first_mat, second_mat = expert_full[l]
        grad_gates = jnp.sum(grad_state[None] * pair_out, axis=2)
        grad_pairs = (gate_values[:, :, None] * grad_state[None]).astype(BF).reshape(-1, D)
        send_grads = dot(dispatch, grad_pairs).astype(BF)
        grad_rows = to_peers(send_grads.reshape(experts, capacity, D)).reshape(-1, D)
        grad_act = dot(grad_rows, second_mat, ((1,), (1,)))
        _, gelu_pull = jax.vjp(jax.nn.gelu, pre_act)
        grad_pre = gelu_pull(grad_act)[0].astype(BF)
        grad_inputs = dot(grad_pre, first_mat, ((1,), (1,))).astype(BF)
        grad_back = to_peers(grad_inputs.reshape(experts, capacity, D)).reshape(-1, D)
        grad_second = dot(activated, grad_rows, ((0,), (0,))).astype(BF)
        grad_first = dot(expert_rows, grad_pre, ((0,), (0,))).astype(BF)
        first_grads[l] = lax.psum_scatter(grad_first, "seq", scatter_dimension=0, tiled=True).astype(F32)
        second_grads[l] = lax.psum_scatter(grad_second, "seq", scatter_dimension=0, tiled=True).astype(F32)
        grad_mixed = dot(dispatch_tokens, grad_back, ((0,), (0,)))
        grad_probs = jnp.sum(grad_gates[:, :, None] * route_hot, axis=0)
        grad_logits = router_probs * (
            grad_probs - jnp.sum(router_probs * grad_probs, axis=-1, keepdims=True)
        )
        router_grad = jnp.dot(mixed_in.astype(F32).T, grad_logits, precision=highest)
        grad_mixed = grad_mixed + jnp.dot(grad_logits, router[l].astype(F32).T, precision=highest)
        grad_mid, gain_f_grad = norm_backward(middle, scale_two, gains_f[l], grad_mixed)
        grad_mid = grad_mid + grad_state
        branch_grad = grad_mid.astype(BF)
        grad_out_proj = dot(attended, branch_grad, ((0,), (0,))).astype(BF)
        grad_attended = dot(branch_grad, out_mat, ((1,), (1,))).astype(BF)
        dq, dkv, diag = attention_back(
            off_arr, queries, kv, seg_col, seg_keys, bias_rows[l], lse, grad_attended
        )
        table_grad = lax.dot_general(
            bucket_hot.astype(F32), diag, (((1,), (1,)), ((), ())), precision=highest
        )
        dkv_own = scatter_key_grads(dkv)
        grad_proj = jnp.concatenate([dq, dkv_own], axis=1)
        grad_in_proj = dot(normed, grad_proj, ((0,), (0,))).astype(BF)
        grad_normed = dot(grad_proj, qkv_mat, ((1,), (1,)))
        grad_prev, gain_a_grad = norm_backward(state_in, scale_one, gains_a[l], grad_normed)
        grad_state = grad_mid + grad_prev
        attn_grads[l] = jnp.concatenate([grad_in_proj, grad_out_proj], axis=1)
        small[l] = (gain_a_grad, gain_f_grad, router_grad, table_grad)
    sizes = [D, D, D * experts, BUCKETS * HEADS]
    flat = jnp.concatenate([part.reshape(-1) for l in range(LAYERS) for part in small[l]])
    used = flat.size
    padded = -(-used // (3 * 8 * 128)) * 3 * 8 * 128
    devices = 2 * SIDE**3
    whole = jnp.stack(attn_grads).reshape(LAYERS, devices, -1, 128).transpose(1, 0, 2, 3)
    whole = whole.reshape(devices, 3, -1, 128).transpose(1, 0, 2, 3)
    whole = whole.reshape(3, SIDE, SIDE, SIDE, 2, -1, 128)
    attn, flat = reduce_all(whole, jnp.pad(flat, (0, padded - used)).reshape(3, -1, 128))
    attn = attn.reshape(LAYERS, -1, 4 * D)
    flat = flat.reshape(-1)[:used].reshape(LAYERS, -1)
    sums, at = [], 0
    for size in sizes:
        sums.append(flat[:, at : at + size])
        at += size
    return (
        out_tokens,
        grad_state,
        sums[0],
        attn[:, :, : 3 * D],
        attn[:, :, 3 * D :],
        sums[3].reshape(LAYERS, BUCKETS, HEADS),
        sums[1],
        sums[2].reshape(LAYERS, D, experts),
        jnp.stack(first_grads)[:, None],
        jnp.stack(second_grads)[:, None],
    )


def solution(mesh):
    rows = P(("grp", "seq"), None)
    slab = P(None, ("grp", "seq"), None)
    expert = P(None, "grp", "seq", None)
    return jax.shard_map(
        on_device,
        mesh=mesh,
        in_specs=(
            rows, P("grp", "seq"), P(), rows, P(), slab, slab, P(), P(), P(), expert, expert, rows,
        ),
        out_specs=(rows, rows, P(), slab, slab, P(), P(), P(), expert, expert),
        check_vma=False,
    )
```

```python
import functools

import jax
import jax.numpy as jnp
from jax import lax
from jax.experimental import pallas as pl
from jax.experimental.pallas import tpu as pltpu
from jax.sharding import PartitionSpec as P

D = 768
HEADS = 12
HEAD_DIM = 64
PAIRS = HEADS // 2
TOP = 2
BUCKETS = 32
LAYERS = 2
BACK = 4
EPS = 1e-06
MASKED = -1e30
SCALE = HEAD_DIM**-0.5
BF = jnp.bfloat16
F32 = jnp.float32
highest = lax.Precision.HIGHEST
VMEM = pltpu.VMEM
LITTLE = pl.CostEstimate(flops=1024, bytes_accessed=1024, transcendentals=0)


def dot(a, b, contract=((1,), (0,))):
    return lax.dot_general(a, b, (contract, ((), ())), preferred_element_type=F32)


def inv_root(values):
    return lax.rsqrt(jnp.mean(values * values, axis=-1, keepdims=True) + EPS)


def norm_backward(values, scale_rows, gain_row, grad_out):
    scaled = grad_out * gain_row
    grad_gain = jnp.sum(grad_out * values * scale_rows, axis=0)
    cubed = scale_rows * scale_rows * scale_rows
    input_gradient = scale_rows * scaled - values * cubed * jnp.mean(
        values * scaled, axis=-1, keepdims=True
    )
    return (input_gradient, grad_gain)


def head_scores(q2, k2, low_lanes, head, allowed, bias_ref, width, span):
    mine = low_lanes if head % 2 == 0 else jnp.logical_not(low_lanes)
    q_head = jnp.where(mine, q2, jnp.zeros_like(q2))
    scores = dot(q_head, k2, ((1,), (1,))) * SCALE
    row = jnp.broadcast_to(bias_ref[head : head + 1, :], (q2.shape[0], span))
    bias = pltpu.roll(row, 0, 1, stride=1, stride_axis=0)[:, :width]
    return q_head, mine, jnp.where(allowed, scores + bias, MASKED)


def first_key_block():
    me = lax.axis_index("seq")
    return me // BACK * (me % BACK)


def allowed_pairs(off_ref, segq_ref, segk_ref, rows, width):
    i = lax.broadcasted_iota(jnp.int32, (rows, width), 0)
    j = lax.broadcasted_iota(jnp.int32, (rows, width), 1)
    return (off_ref[0] + i - j >= 0) & (segq_ref[...] == segk_ref[...])


def attention_kernel(off_ref, q_ref, kv_ref, segq_ref, segk_ref, bias_ref, out_ref, lse_ref):
    rows, width, span = q_ref.shape[0], segk_ref.shape[1], bias_ref.shape[1]
    first = first_key_block()
    window = pl.ds(pl.multiple_of(first * rows, rows), width)
    allowed = allowed_pairs(off_ref, segq_ref, segk_ref, rows, width)
    low_lanes = lax.broadcasted_iota(jnp.int32, (rows, 128), 1) < HEAD_DIM
    lane = lax.broadcasted_iota(jnp.int32, (rows, 128), 1)
    totals = jnp.zeros((rows, 128), F32)
    for pair in range(PAIRS):
        at = slice(pair * 128, pair * 128 + 128)
        q2, k2 = q_ref[:, at], kv_ref[window, at]
        v2 = kv_ref[window, D + pair * 128 : D + pair * 128 + 128]
        both = []
        for head in (2 * pair, 2 * pair + 1):
            _, _, scores = head_scores(q2, k2, low_lanes, head, allowed, bias_ref, width, span)
            row_max = jnp.max(scores, axis=1, keepdims=True)
            exponent = jnp.exp(scores - row_max)
            row_total = jnp.sum(exponent, axis=1, keepdims=True)
            weights = (exponent / row_total).astype(BF)
            both.append(dot(weights, v2))
            totals = jnp.where(lane == head, row_max + jnp.log(row_total), totals)
        out_ref[:, at] = jnp.where(low_lanes, both[0], both[1]).astype(BF)
    lse_ref[...] = totals


def attention_back_kernel(
    off_ref, q_ref, kv_ref, segq_ref, segk_ref, bias_ref, lse_ref, grad_ref, dq_ref, dkv_ref, diag_ref
):
    rows, width, span = q_ref.shape[0], segk_ref.shape[1], bias_ref.shape[1]
    first = first_key_block()
    window = pl.ds(pl.multiple_of(first * rows, rows), width)
    allowed = allowed_pairs(off_ref, segq_ref, segk_ref, rows, width)
    low_lanes = lax.broadcasted_iota(jnp.int32, (rows, 128), 1) < HEAD_DIM
    lane = lax.broadcasted_iota(jnp.int32, (rows, 128), 1)
    i = lax.broadcasted_iota(jnp.int32, (rows, rows), 0)
    j = lax.broadcasted_iota(jnp.int32, (rows, rows), 1)
    flip = (i + j == rows - 1).astype(BF)
    dkv_ref[...] = jnp.zeros_like(dkv_ref)
    for pair in range(PAIRS):
        at = slice(pair * 128, pair * 128 + 128)
        at_v = slice(D + pair * 128, D + pair * 128 + 128)
        q2, k2, v2, g2 = q_ref[:, at], kv_ref[window, at], kv_ref[window, at_v], grad_ref[:, at]
        dq, dk, dv = [], None, None
        for head in (2 * pair, 2 * pair + 1):
            q_head, mine, scores = head_scores(q2, k2, low_lanes, head, allowed, bias_ref, width, span)
            log_total = jnp.sum(jnp.where(lane == head, lse_ref[...], 0.0), axis=1, keepdims=True)
            probs = jnp.exp(scores - log_total)
            g_head = jnp.where(mine, g2, jnp.zeros_like(g2))
            grad_probs = dot(g_head, v2, ((1,), (1,)))
            inner = jnp.sum(probs * grad_probs, axis=1, keepdims=True)
            grad_scores = (probs * (grad_probs - inner)).astype(BF)
            dq.append(dot(grad_scores, k2))
            dk_head = dot(grad_scores, q_head, ((0,), (0,)))
            dv_head = dot(probs.astype(BF), g_head, ((0,), (0,)))
            dk = dk_head if dk is None else dk + dk_head
            dv = dv_head if dv is None else dv + dv_head
            turned = jnp.concatenate(
                [dot(flip, grad_scores), jnp.zeros((rows, span - width), F32)], axis=1
            )
            turned = pltpu.roll(turned, span - (rows - 1), 1, stride=1, stride_axis=0)
            diag_ref[head : head + 1, :] = jnp.sum(turned, axis=0, keepdims=True)
        dq_ref[:, at] = (jnp.where(low_lanes, dq[0], dq[1]) * SCALE).astype(BF)
        blocks = pl.ds(first, width // rows)
        dkv_ref[blocks, :, at] = (dk * SCALE).astype(BF).reshape(-1, rows, 128)
        dkv_ref[blocks, :, at_v] = dv.astype(BF).reshape(-1, rows, 128)


def vmem_specs(n):
    return [pl.BlockSpec(memory_space=VMEM) for _ in range(n)]


def attention(off, queries, kv, segq, segk, bias):
    return pl.pallas_call(
        attention_kernel,
        out_shape=(
            jax.ShapeDtypeStruct(queries.shape, BF),
            jax.ShapeDtypeStruct((queries.shape[0], 128), F32),
        ),
        in_specs=[pl.BlockSpec(memory_space=pltpu.SMEM)] + vmem_specs(5),
        out_specs=tuple(vmem_specs(2)),
        cost_estimate=LITTLE,
        compiler_params=pltpu.CompilerParams(vmem_limit_bytes=32 * 2**20),
    )(off, queries, kv, segq, segk, bias)


def attention_back(off, queries, kv, segq, segk, bias, lse, grad):
    return pl.pallas_call(
        attention_back_kernel,
        out_shape=(
            jax.ShapeDtypeStruct(queries.shape, BF),
            jax.ShapeDtypeStruct((kv.shape[0] // queries.shape[0], queries.shape[0], kv.shape[1]), BF),
            jax.ShapeDtypeStruct(bias.shape, F32),
        ),
        in_specs=[pl.BlockSpec(memory_space=pltpu.SMEM)] + vmem_specs(7),
        out_specs=tuple(vmem_specs(3)),
        cost_estimate=LITTLE,
        compiler_params=pltpu.CompilerParams(vmem_limit_bytes=32 * 2**20),
    )(off, queries, kv, segq, segk, bias, lse, grad)


MESH_ID = pl.DeviceIdType.MESH
QKV_BLOCKS = 6
SIDE = 4


def place_of_device():
    grp, seq = lax.axis_index("grp"), lax.axis_index("seq")
    return [grp // SIDE, grp % SIDE, seq // 2], seq % 2


def device_at(coords, core):
    return (coords[0] * SIDE + coords[1], coords[2] * 2 + core)


def moved(coords, axis, delta):
    return [(c + delta) % SIDE if a == axis else c for a, c in enumerate(coords)]


def remote(src, dst, send_sem, recv_sem, device):
    return pltpu.make_async_remote_copy(
        src_ref=src, dst_ref=dst, send_sem=send_sem, recv_sem=recv_sem, device_id=device, device_id_type=MESH_ID
    )


def greet(devices):
    barrier = pltpu.get_barrier_semaphore()
    for device in devices:
        pl.semaphore_signal(barrier, inc=1, device_id=device, device_id_type=MESH_ID)
    pl.semaphore_wait(barrier, len(devices))


def sequence_partners(coords, core):
    seq = coords[2] * 2 + core
    others = [(seq + d) % (2 * SIDE) for d in range(1, 2 * SIDE)]
    return [(coords[0] * SIDE + coords[1], s) for s in others], others


def all_partners(coords, core):
    partners = [device_at(moved(coords, a, d), core) for a in range(2) for d in range(1, SIDE)]
    return partners + sequence_partners(coords, core)[0]


def attn_gather_kernel(
    own_ref, seg_ref, pick_ref, full_ref, segs_ref, rows_ref,
    row_send, row_recv, send_sem, recv_sem, core_send, core_recv, seg_send, seg_recv,
):
    coords, core = place_of_device()
    sibling = device_at(coords, 1 - core)
    y, x, z = coords
    seq = z * 2 + core
    greet(all_partners(coords, core))
    rows_ref[seq] = own_ref[seq]
    segs_ref[z, core] = seg_ref[...]
    devices, numbers = sequence_partners(coords, core)
    row_copies = []
    for n, (device, s) in enumerate(zip(devices, numbers)):
        row_copies.append(remote(own_ref.at[s], rows_ref.at[seq], row_send.at[n], row_recv.at[n], device))
        row_copies[-1].start()
    seg_copies = []
    for d in range(1, SIDE):
        one = segs_ref.at[z, core]
        seg_copies.append(remote(one, one, seg_send.at[d - 1], seg_recv.at[d - 1], device_at(moved(coords, 2, d), core)))
        seg_copies[-1].start()
    for copy in row_copies:
        copy.wait()
    for l in range(LAYERS):
        flat = rows_ref[:, l].reshape(-1, own_ref.shape[-1])
        block = dot(pick_ref[...], flat).astype(BF)
        for p in range(3):
            full_ref[z, core, l, y, x, p] = block[16 * p : 16 * p + 16]

    def region(p, free, fixed=None):
        at = [slice(None) if a in free else coords[a] for a in range(3)]
        if fixed is not None:
            at[fixed[0]] = fixed[1]
        return full_ref.at[at[2], core, :, at[0], at[1], p]

    copies = {}
    core_copies = []

    def to_sibling(part, number):
        core_copies.append(remote(part, part, core_send.at[number], core_recv.at[number], sibling))
        core_copies[-1].start()

    for k in range(3):
        for p in range(3):
            if k:
                for d in (1, 3, 2):
                    copies[k - 1, p, d].wait_recv()
            axis, free = (p + k) % 3, [(p + i) % 3 for i in range(k)]
            part = region(p, free)
            for d in (1, 3, 2):
                copies[k, p, d] = remote(
                    part, part, send_sem.at[k, p, d - 1], recv_sem.at[k, p, d - 1],
                    device_at(moved(coords, axis, d), core),
                )
                copies[k, p, d].start()
            if k == 2:
                to_sibling(part, 4 * p)
    for copy in seg_copies:
        copy.wait_recv()
    part = segs_ref.at[:, core]
    seg_last = remote(part, part, seg_send.at[3], seg_recv.at[3], sibling)
    seg_last.start()
    for d in (1, 3, 2):
        for p in range(3):
            axis = (p + 2) % 3
            copies[2, p, d].wait_recv()
            came = (coords[axis] + SIDE - d) % SIDE
            to_sibling(region(p, [a for a in range(3) if a != axis], (axis, came)), 4 * p + d)
    for copy in copies.values():
        copy.wait_send()
    for copy in seg_copies:
        copy.wait_send()
    seg_last.wait()
    for copy in core_copies:
        copy.wait()


def attn_gather(own, seg, pick):
    dma = pltpu.SemaphoreType.DMA
    width = own.shape[-1]
    return pl.pallas_call(
        attn_gather_kernel,
        out_shape=(
            jax.ShapeDtypeStruct((SIDE, 2, LAYERS, SIDE, SIDE, 3, 16, width), BF),
            jax.ShapeDtypeStruct((SIDE, 2) + seg.shape, F32),
        ),
        in_specs=vmem_specs(3),
        out_specs=tuple(vmem_specs(2)),
        scratch_shapes=[VMEM(own.shape, BF), dma((7,)), dma((7,)), dma((3, 3, 3)), dma((3, 3, 3)),
                        dma((12,)), dma((12,)), dma((4,)), dma((4,))],
        cost_estimate=LITTLE,
        compiler_params=pltpu.CompilerParams(
            collective_id=0, has_side_effects=True, vmem_limit_bytes=40 * 2**20
        ),
    )(own, seg, pick)


def reduce_kernel(
    x0_ref, x1_ref, small_ref, pick_ref, out_ref, small_out, got_core, y_ref, got_one, z_ref, got_two, w_ref, got_three,
    rows_ref, s_core, s_got, core_send, core_recv, send_sem, recv_sem, s_core_send, s_core_recv, s_send, s_recv,
    row_send, row_recv,
):
    coords, core = place_of_device()
    sibling = device_at(coords, 1 - core)
    greet(all_partners(coords, core))
    x_refs = (x0_ref, x1_ref)
    order = (2, 0, 1)
    first = {}
    for p in range(3):
        for l in range(LAYERS):
            first[p, l] = remote(
                x_refs[l].at[:, 1 - core, :, :, p], got_core.at[p, l], core_send.at[p, l], core_recv.at[p, l], sibling
            )
            first[p, l].start()
    s_first = remote(small_ref, s_core, s_core_send, s_core_recv, sibling)
    s_first.start()

    def axes_left(p, k):
        gone = [(p + i) % 3 for i in range(k)]
        return [a for a in order if a not in gone]

    def spread(p, k, source, target):
        axis, out = (p + k) % 3, []
        for d in (1, 3, 2):
            to = moved(coords, axis, d)
            index = tuple(to[axis] if a == axis else slice(None) for a in axes_left(p, k))
            copy = remote(
                source.at[(p, *index)], target.at[p, d - 1], send_sem.at[k, p, d - 1], recv_sem.at[k, p, d - 1],
                device_at(to, core),
            )
            copy.start()
            out.append(copy)
        return out

    def spread_small(p, k):
        axis, out = (p + k) % 3, []
        for d in (1, 3, 2):
            copy = remote(
                s_got.at[k, p, 0], s_got.at[k, p, d], s_send.at[k, p, d - 1], s_recv.at[k, p, d - 1],
                device_at(moved(coords, axis, d), core),
            )
            copy.start()
            out.append(copy)
        return out

    def small_sum(p, k):
        axis = (p + k) % 3
        total = s_got[k, p, coords[axis]]
        for v in range(1, SIDE):
            total = total + s_got[k, p, (coords[axis] + SIDE - v) % SIDE]
        return total

    sent, s_sent = {}, {}
    s_first.wait()
    for p in range(3):
        s_got[0, p, 0] = small_ref[p] + s_core[p]
        s_sent[0, p] = spread_small(p, 0)
    for p in range(3):
        for l in range(LAYERS):
            first[p, l].wait()

        def add_core(i, carry, p=p):
            a, b, c = i // (SIDE * SIDE), i // SIDE % SIDE, i % SIDE
            for l in range(LAYERS):
                total = x_refs[l][a, core, b, c, p].astype(F32) + got_core[p, l, a, b, c].astype(F32)
                y_ref[p, a, b, c, l] = total.astype(BF)
            return carry

        lax.fori_loop(0, SIDE**3, add_core, 0)
        sent[0, p] = spread(p, 0, y_ref, got_one)
    for p in range(3):
        for copy in s_sent[0, p]:
            copy.wait()
        s_got[1, p, 0] = small_sum(p, 0)
        s_sent[1, p] = spread_small(p, 1)
    for p in range(3):
        for copy in sent[0, p]:
            copy.wait()
        at = order.index(p)

        def add_one(i, carry, p=p, at=at):
            a, b = i // SIDE, i % SIDE
            index = [a, b]
            index.insert(at, coords[p])
            total = y_ref[(p, *index)].astype(F32)
            for d in range(3):
                total = total + got_one[p, d, a, b].astype(F32)
            z_ref[p, a, b] = total.astype(BF)
            return carry

        lax.fori_loop(0, SIDE**2, add_one, 0)
        sent[1, p] = spread(p, 1, z_ref, got_two)
    for p in range(3):
        for copy in s_sent[1, p]:
            copy.wait()
        s_got[2, p, 0] = small_sum(p, 1)
        s_sent[2, p] = spread_small(p, 2)
    for p in range(3):
        for copy in sent[1, p]:
            copy.wait()
        axis = (p + 1) % 3

        def add_two(i, carry, p=p, axis=axis):
            index = tuple(coords[axis] if a == axis else i for a in axes_left(p, 1))
            total = z_ref[(p, *index)].astype(F32)
            for d in range(3):
                total = total + got_two[p, d, i].astype(F32)
            w_ref[p, i] = total.astype(BF)
            return carry

        lax.fori_loop(0, SIDE, add_two, 0)
        sent[2, p] = spread(p, 2, w_ref, got_three)
    for p in range(3):
        for copy in s_sent[2, p]:
            copy.wait()
        small_out[p] = small_sum(p, 2)
    blocks = []
    for p in range(3):
        for copy in sent[2, p]:
            copy.wait()
        total = w_ref[p, coords[(p + 2) % 3]].astype(F32)
        for d in range(3):
            total = total + got_three[p, d].astype(F32)
        blocks.append(total.astype(BF))
    for l in range(LAYERS):
        block = jnp.concatenate([part[l] for part in blocks], axis=0)
        spread_rows = dot(pick_ref[...], block, ((0,), (0,))).astype(BF)
        rows_ref[:, l] = spread_rows.reshape(2 * SIDE, 16, -1)
    seq = coords[2] * 2 + core
    out_ref[seq] = rows_ref[seq]
    devices, numbers = sequence_partners(coords, core)
    last = []
    for n, (device, s) in enumerate(zip(devices, numbers)):
        last.append(remote(rows_ref.at[s], out_ref.at[seq], row_send.at[n], row_recv.at[n], device))
        last[-1].start()
    for copy in last:
        copy.wait()


def reduce_all(x0, x1, small, pick):
    width, part = x0.shape[-1], small.shape[1:]
    block = (LAYERS, 16, width)
    rows = (2 * SIDE, LAYERS, 16, width)
    dma = pltpu.SemaphoreType.DMA
    return pl.pallas_call(
        reduce_kernel,
        out_shape=(jax.ShapeDtypeStruct(rows, BF), jax.ShapeDtypeStruct(small.shape, F32)),
        in_specs=vmem_specs(4),
        out_specs=tuple(vmem_specs(2)),
        scratch_shapes=[
            VMEM((3, LAYERS, SIDE, SIDE, SIDE, 16, width), BF),
            VMEM((3, SIDE, SIDE, SIDE) + block, BF),
            VMEM((3, 3, SIDE, SIDE) + block, BF),
            VMEM((3, SIDE, SIDE) + block, BF),
            VMEM((3, 3, SIDE) + block, BF),
            VMEM((3, SIDE) + block, BF),
            VMEM((3, 3) + block, BF),
            VMEM(rows, BF),
            VMEM(small.shape, F32),
            VMEM((3, 3, SIDE) + part, F32),
            dma((3, LAYERS)), dma((3, LAYERS)), dma((3, 3, 3)), dma((3, 3, 3)), dma(()), dma(()),
            dma((3, 3, 3)), dma((3, 3, 3)), dma((7,)), dma((7,)),
        ],
        cost_estimate=LITTLE,
        compiler_params=pltpu.CompilerParams(
            collective_id=1, has_side_effects=True, vmem_limit_bytes=50 * 2**20
        ),
    )(x0, x1, small, pick)


def project_kernel(x_ref, w_ref, out_ref):
    width = w_ref.shape[3]
    for s in range(w_ref.shape[0]):
        out_ref[:, s * width : (s + 1) * width] = dot(x_ref[...], w_ref[s, 0]).astype(out_ref.dtype)


def project(x, full, layer, first, count, dtype):
    depth, width = full.shape[2:]
    some = 3 if count % 3 == 0 else count
    return pl.pallas_call(
        project_kernel,
        grid=(count // some,),
        out_shape=jax.ShapeDtypeStruct((x.shape[0], count * width), dtype),
        in_specs=[
            pl.BlockSpec(x.shape, lambda s: (0, 0)),
            pl.BlockSpec((some, 1, depth, width), lambda s: (first // some + s, layer, 0, 0)),
        ],
        out_specs=pl.BlockSpec((x.shape[0], some * width), lambda s: (0, s)),
        cost_estimate=LITTLE,
        compiler_params=pltpu.CompilerParams(vmem_limit_bytes=56 * 2**20),
    )(x, full)


def project_back_kernel(x_ref, w_ref, out_ref):
    @pl.when(pl.program_id(0) == 0)
    def _():
        out_ref[...] = jnp.zeros_like(out_ref)

    width = w_ref.shape[3]
    for s in range(w_ref.shape[0]):
        out_ref[...] += dot(x_ref[:, s * width : (s + 1) * width], w_ref[s, 0], ((1,), (1,)))


def project_back(x, full, layer, first, count):
    depth, width = full.shape[2:]
    some = 3 if count % 3 == 0 else count
    return pl.pallas_call(
        project_back_kernel,
        grid=(count // some,),
        out_shape=jax.ShapeDtypeStruct((x.shape[0], depth), F32),
        in_specs=[
            pl.BlockSpec((x.shape[0], some * width), lambda s: (0, s)),
            pl.BlockSpec((some, 1, depth, width), lambda s: (first // some + s, layer, 0, 0)),
        ],
        out_specs=pl.BlockSpec((x.shape[0], depth), lambda s: (0, 0)),
        cost_estimate=LITTLE,
        compiler_params=pltpu.CompilerParams(vmem_limit_bytes=56 * 2**20),
    )(x, full)


def weight_grad_kernel(normed_ref, attended_ref, proj_ref, branch_ref, out_ref):
    step, width = pl.program_id(0), out_ref.shape[2]

    def fill(left, right):
        for s in range(out_ref.shape[0]):
            out_ref[s] = dot(left[...], right[:, s * width : (s + 1) * width], ((0,), (0,))).astype(BF)

    @pl.when(step < QKV_BLOCKS // 2)
    def _():
        fill(normed_ref, proj_ref)

    @pl.when(step >= QKV_BLOCKS // 2)
    def _():
        fill(attended_ref, branch_ref)


def weight_grads(normed, attended, grad_proj, branch_grad):
    rows, width = normed.shape[0], grad_proj.shape[1] // QKV_BLOCKS
    last = QKV_BLOCKS // 2 - 1
    return pl.pallas_call(
        weight_grad_kernel,
        grid=(SIDE,),
        out_shape=jax.ShapeDtypeStruct((2 * SIDE, D, width), BF),
        in_specs=[
            pl.BlockSpec((rows, D), lambda s: (0, 0)),
            pl.BlockSpec((rows, D), lambda s: (0, 0)),
            pl.BlockSpec((rows, 2 * width), lambda s: (0, jnp.minimum(s, last))),
            pl.BlockSpec((rows, 2 * width), lambda s: (0, 0)),
        ],
        out_specs=pl.BlockSpec((2, D, width), lambda s: (s, 0, 0)),
        cost_estimate=LITTLE,
        compiler_params=pltpu.CompilerParams(vmem_limit_bytes=56 * 2**20),
    )(normed, attended, grad_proj, branch_grad)


def kv_gather(own_ref, kv_ref, send_sem, recv_sem):
    coords, core = place_of_device()
    z, rows = coords[2], own_ref.shape[0]
    half = rows // 2
    up, down = moved(coords, 2, 1), moved(coords, 2, 3)
    up_z, down_z, far_z = (z + 1) % SIDE, (z + 3) % SIDE, (z + 2) % SIDE
    sibling = device_at(coords, 1 - core)

    def block(at, start=0, size=rows):
        return kv_ref.at[pl.ds(pl.multiple_of((at * 2 + core) * rows + start, half), size)]

    copies = []

    def send(part, number, device):
        copy = remote(part, part, send_sem.at[number], recv_sem.at[number], device)
        copy.start()
        copies.append(copy)
        return copy

    kv_ref[pl.ds(pl.multiple_of((z * 2 + core) * rows, rows), rows), :] = own_ref[...]
    greet([device_at(up, core), device_at(down, core), sibling])
    went_up = send(block(z), 0, device_at(up, core))
    went_down = send(block(z), 1, device_at(down, core))
    from_core = [send(block(z), 2, sibling)]
    went_up.wait_recv()
    far_up = send(block(down_z, 0, half), 3, device_at(up, core))
    from_core.append(send(block(down_z), 4, sibling))
    went_down.wait_recv()
    far_down = send(block(up_z, half, half), 5, device_at(down, core))
    from_core.append(send(block(up_z), 6, sibling))
    far_up.wait_recv()
    from_core.append(send(block(far_z, 0, half), 7, sibling))
    far_down.wait_recv()
    from_core.append(send(block(far_z, half, half), 8, sibling))
    for copy in from_core:
        copy.wait_recv()
    for copy in copies:
        copy.wait_send()


def kv_scatter(grads_ref, out_ref, got_core, sums, got_far, got_near, send_sem, recv_sem):
    coords, core = place_of_device()
    z, rows = coords[2], out_ref.shape[0]
    half = rows // 2
    up, down = device_at(moved(coords, 2, 1), core), device_at(moved(coords, 2, 3), core)
    up_z, down_z, far_z = (z + 1) % SIDE, (z + 3) % SIDE, (z + 2) % SIDE
    sibling = device_at(coords, 1 - core)
    greet([up, down, sibling])
    copies = []

    def send(src, dst, number, device):
        copy = remote(src, dst, send_sem.at[number], recv_sem.at[number], device)
        copy.start()
        copies.append(copy)
        return copy

    order = [far_z, up_z, down_z, z]
    cross = [send(grads_ref.at[at * 2 + 1 - core], got_core.at[n], n, sibling) for n, at in enumerate(order)]

    def total(n):
        cross[n].wait_recv()
        return grads_ref[order[n] * 2 + core].astype(F32) + got_core[n].astype(F32)

    sums[0] = total(0).astype(BF)
    far_up = send(sums.at[0, pl.ds(0, half)], got_far.at[0], 4, up)
    far_down = send(sums.at[0, pl.ds(half, half)], got_far.at[1], 5, down)
    up_sum, down_sum = total(1), total(2)
    sums[1, half:] = up_sum[half:].astype(BF)
    sums[2, :half] = down_sum[:half].astype(BF)
    far_up.wait_recv()
    sums[1, :half] = (up_sum[:half] + got_far[0].astype(F32)).astype(BF)
    near_up = send(sums.at[1], got_near.at[0], 6, up)
    far_down.wait_recv()
    sums[2, half:] = (down_sum[half:] + got_far[1].astype(F32)).astype(BF)
    near_down = send(sums.at[2], got_near.at[1], 7, down)
    own = total(3)
    near_up.wait_recv()
    near_down.wait_recv()
    out_ref[...] = (own + got_near[0].astype(F32) + got_near[1].astype(F32)).astype(BF)
    for copy in copies:
        copy.wait_send()

def gather_keys(own):
    return pl.pallas_call(
        kv_gather,
        out_shape=jax.ShapeDtypeStruct((2 * SIDE * own.shape[0], own.shape[1]), BF),
        in_specs=vmem_specs(1),
        out_specs=vmem_specs(1)[0],
        scratch_shapes=[pltpu.SemaphoreType.DMA((9,))] * 2,
        cost_estimate=LITTLE,
        compiler_params=pltpu.CompilerParams(
            collective_id=2, has_side_effects=True, vmem_limit_bytes=20 * 2**20
        ),
    )(own)


def scatter_key_grads(grads):
    block = grads.shape[1:]
    return pl.pallas_call(
        kv_scatter,
        out_shape=jax.ShapeDtypeStruct(block, BF),
        in_specs=vmem_specs(1),
        out_specs=vmem_specs(1)[0],
        scratch_shapes=[
            VMEM((SIDE,) + block, BF),
            VMEM((3,) + block, BF),
            VMEM((2, block[0] // 2, block[1]), BF),
            VMEM((2,) + block, BF),
            pltpu.SemaphoreType.DMA((8,)),
            pltpu.SemaphoreType.DMA((8,)),
        ],
        cost_estimate=LITTLE,
        compiler_params=pltpu.CompilerParams(
            collective_id=3, has_side_effects=True, vmem_limit_bytes=20 * 2**20
        ),
    )(grads)


def exchange_kernel(n, *refs):
    loads, outs = refs[: 5 * n], refs[5 * n : 6 * n]
    to_send, got, send_sem, recv_sem = refs[6 * n :]
    grp, seq = lax.axis_index("grp"), lax.axis_index("seq")
    peers, half = got.shape[1], got.shape[3]
    others = [(grp + d) % peers for d in range(1, peers)]
    greet([(other, seq) for other in others])
    for i in range(n):
        x_ref, put_left, put_right = loads[5 * i : 5 * i + 3]
        rows = dot(put_left[...], x_ref[:, :half]) + dot(put_right[...], x_ref[:, half:])
        to_send[i] = rows.astype(BF).reshape(to_send.shape[1:])
    copies = []
    for k, other in enumerate(others):
        copies.append(
            remote(to_send.at[:, other], got.at[:, grp], send_sem.at[k], recv_sem.at[k], (other, seq))
        )
        copies[-1].start()
    got[:, grp] = to_send[:, grp]
    for copy in copies:
        copy.wait()
    for i in range(n):
        take_left, take_right = loads[5 * i + 3 : 5 * i + 5]
        came = got[i].reshape(-1, half)
        outs[i][:, :half] = dot(take_left[...], came, ((0,), (0,))).astype(outs[i].dtype)
        outs[i][:, half:] = dot(take_right[...], came, ((0,), (0,))).astype(outs[i].dtype)


def exchange(number, *loads):
    peers, n = lax.axis_size("grp"), len(loads)
    x, put = loads[0][:2]
    slots = (n, peers, put[0].shape[0] // peers, x.shape[1] // 2)
    dma = pltpu.SemaphoreType.DMA
    return pl.pallas_call(
        functools.partial(exchange_kernel, n),
        out_shape=tuple(
            jax.ShapeDtypeStruct((take[0].shape[1], x.shape[1]), dtype) for x, _, take, dtype in loads
        ),
        in_specs=vmem_specs(5 * n),
        out_specs=tuple(vmem_specs(n)),
        scratch_shapes=[VMEM(slots, BF), VMEM(slots, BF), dma((peers - 1,)), dma((peers - 1,))],
        cost_estimate=LITTLE,
        compiler_params=pltpu.CompilerParams(
            collective_id=4 + number, has_side_effects=True, vmem_limit_bytes=24 * 2**20
        ),
    )(*[part for x, put, take, _ in loads for part in (x, *put, *take)])


FF_BLOCK = 1024
GELU_A, GELU_B = 0.7978845608028654, 0.044715


def expert_kernel(x_ref, in_ref, out_w_ref, out_ref, pre_ref, total):
    step = pl.program_id(0)

    @pl.when(step == 0)
    def _():
        total[...] = jnp.zeros_like(total)

    pre = dot(x_ref[...], in_ref[...])
    pre_ref[...] = pre
    act = 0.5 * pre * (1.0 + jnp.tanh(GELU_A * (pre + GELU_B * pre * pre * pre)))
    total[...] += dot(act.astype(BF), out_w_ref[...])

    @pl.when(step == pl.num_programs(0) - 1)
    def _():
        out_ref[...] = total[...].astype(BF)


def expert_forward(rows, first_mat, second_mat):
    width, hidden = first_mat.shape
    count = rows.shape[0]
    return pl.pallas_call(
        expert_kernel,
        grid=(hidden // FF_BLOCK,),
        out_shape=(jax.ShapeDtypeStruct(rows.shape, BF), jax.ShapeDtypeStruct((count, hidden), F32)),
        in_specs=[
            pl.BlockSpec((count, width), lambda j: (0, 0)),
            pl.BlockSpec((width, FF_BLOCK), lambda j: (0, j)),
            pl.BlockSpec((FF_BLOCK, width), lambda j: (j, 0)),
        ],
        out_specs=(
            pl.BlockSpec((count, width), lambda j: (0, 0)),
            pl.BlockSpec((count, FF_BLOCK), lambda j: (0, j)),
        ),
        scratch_shapes=[VMEM((count, width), F32)],
        cost_estimate=LITTLE,
        compiler_params=pltpu.CompilerParams(vmem_limit_bytes=50 * 2**20),
    )(rows, first_mat, second_mat)


def expert_back_kernel(again, x_ref, grad_ref, *refs):
    pre_ref, in_ref, out_w_ref, out_ref, gx_ref, gin_ref, gout_ref, total, out_total = (
        (None, *refs) if again else (*refs[:3], None, *refs[3:], None)
    )
    step = pl.program_id(0)

    @pl.when(step == 0)
    def _():
        total[...] = jnp.zeros_like(total)
        if again:
            out_total[...] = jnp.zeros_like(out_total)

    pre = dot(x_ref[...], in_ref[...]) if again else pre_ref[...]
    grad = grad_ref[...]
    square = pre * pre
    curve = jnp.tanh(GELU_A * (pre + GELU_B * pre * square))
    act = (0.5 * pre * (1.0 + curve)).astype(BF)
    slope = 0.5 * (1.0 + curve) + 0.5 * pre * (1.0 - curve * curve) * (GELU_A * (1.0 + 3.0 * GELU_B * square))
    grad_pre = (dot(grad, out_w_ref[...], ((1,), (1,))) * slope).astype(BF)
    total[...] += dot(grad_pre, in_ref[...], ((1,), (1,)))
    if again:
        out_total[...] += dot(act, out_w_ref[...])
    gin_ref[...] = dot(x_ref[...], grad_pre, ((0,), (0,))).astype(BF)
    gout_ref[...] = dot(act, grad, ((0,), (0,))).astype(BF)

    @pl.when(step == pl.num_programs(0) - 1)
    def _():
        gx_ref[...] = total[...].astype(BF)
        if again:
            out_ref[...] = out_total[...].astype(BF)


def expert_back(rows, grads, pre, first_mat, second_mat):
    width, hidden = first_mat.shape
    count, again = rows.shape[0], pre is None
    whole = pl.BlockSpec((count, width), lambda j: (0, 0))
    columns = pl.BlockSpec((width, FF_BLOCK), lambda j: (0, j))
    lines = pl.BlockSpec((FF_BLOCK, width), lambda j: (j, 0))
    row_like = jax.ShapeDtypeStruct(rows.shape, BF)
    return pl.pallas_call(
        functools.partial(expert_back_kernel, again),
        grid=(hidden // FF_BLOCK,),
        out_shape=(row_like,) * (1 + again)
        + (jax.ShapeDtypeStruct(first_mat.shape, BF), jax.ShapeDtypeStruct(second_mat.shape, BF)),
        in_specs=[whole, whole]
        + ([] if again else [pl.BlockSpec((count, FF_BLOCK), lambda j: (0, j))])
        + [columns, lines],
        out_specs=(whole,) * (1 + again) + (columns, lines),
        scratch_shapes=[VMEM((count, width), F32)] * (1 + again),
        cost_estimate=LITTLE,
        compiler_params=pltpu.CompilerParams(vmem_limit_bytes=50 * 2**20),
    )(rows, grads, *(() if again else (pre,)), first_mat, second_mat)


def gather_attn(wqkv, wout, segments, pick):
    layers, shard = wqkv.shape[0], wqkv.shape[1]
    own = jnp.concatenate([wqkv, wout], axis=2).reshape(layers, shard, 2 * SIDE, -1).transpose(2, 0, 1, 3)
    own = jnp.pad(own, ((0, 0), (0, 0), (0, 16 - shard), (0, 0)))
    seg = jnp.broadcast_to(segments.astype(F32), (8, segments.shape[1]))
    full, segs = attn_gather(own, seg, pick)
    return full.reshape(2 * SIDE, layers, D, -1), segs[:, :, 0].reshape(1, -1)


def gather_experts(w_in, w_out, layer_index):
    first = lax.all_gather(w_in[layer_index, 0], "seq", axis=0, tiled=True)
    second = lax.all_gather(w_out[layer_index, 0], "seq", axis=0, tiled=True)
    return first, second


def on_device(
    tokens,
    segments,
    rel_bucket,
    routes,
    gain_attn,
    wqkv,
    wout,
    bucket_bias_table,
    gain_ffn,
    router,
    w_in,
    w_out,
    cotangent,
):
    count_q = tokens.shape[0]
    experts = lax.axis_size("grp")
    blocks = lax.axis_size("seq")
    capacity = max(2, 3 * count_q * TOP // (2 * experts))
    window = (BACK + 1) * count_q
    span = window + count_q
    me = lax.axis_index("seq")
    start = first_key_block() * count_q
    off = (me * count_q - start).astype(jnp.int32)

    place = jnp.arange(span, dtype=jnp.int32)
    distance = off - jnp.where(place < window, place, place - span)
    pick = (distance[:, None] == jnp.arange(rel_bucket.shape[0], dtype=jnp.int32)[None, :]).astype(BF)
    bucket_at = dot(pick, rel_bucket.astype(BF)[:, None])[:, 0].astype(jnp.int32)
    in_range = (distance >= 0) & (distance < rel_bucket.shape[0])
    bucket_hot = (
        (bucket_at[None, :] == jnp.arange(BUCKETS, dtype=jnp.int32)[:, None]) & in_range[None, :]
    ).astype(BF)
    bias_rows = [dot(bucket_bias_table[l], bucket_hot, ((0,), (0,))) for l in range(LAYERS)]

    expert_ids = jnp.arange(experts, dtype=jnp.int32)
    flat_routes = jnp.concatenate([routes[:, 0], routes[:, 1]])
    hot = (flat_routes[:, None] == expert_ids[None, :]).astype(BF)
    number = jnp.arange(TOP * count_q, dtype=jnp.int32)
    ranks = dot((number[:, None] > number[None, :]).astype(BF), hot)
    rank = jnp.sum(ranks * hot.astype(F32), axis=1).astype(jnp.int32)
    target = flat_routes * capacity + rank
    slots = jnp.arange(experts * capacity, dtype=jnp.int32)
    halves = jnp.arange(2 * experts * capacity, dtype=jnp.int32)
    slot, right = halves // (2 * capacity) * capacity + halves % capacity, halves // capacity % 2
    pairs_at, tokens_at, rows_at = [], [], []
    for side in range(2):
        mine = jnp.where(right == side, slot, -1)[:, None]
        pairs_at.append((mine == target[None, :]).astype(BF))
        tokens_at.append(pairs_at[-1][:, :count_q] + pairs_at[-1][:, count_q:])
        rows_at.append((mine == slots[None, :]).astype(BF))
    route_hot = hot.astype(F32).reshape(TOP, count_q, experts)

    seg_own = segments[0].astype(F32)
    seg_col = seg_own[:, None]
    hidden_state = tokens.astype(F32)
    gains_a, gains_f = gain_attn.astype(F32), gain_ffn.astype(F32)
    stored = []
    shard = wqkv.shape[1]
    row = jnp.arange(blocks * shard, dtype=jnp.int32)[:, None]
    pick = (row // shard * 16 + row % shard == jnp.arange(blocks * 16, dtype=jnp.int32)[None, :]).astype(BF)
    attn_full, segs = gather_attn(wqkv, wout, segments, pick)
    seg_keys = lax.dynamic_slice_in_dim(segs, start, window, axis=1)
    expert_full = [gather_experts(w_in, w_out, l) for l in range(LAYERS)]
    for l in range(LAYERS):
        first_mat, second_mat = expert_full[l]
        scale_one = inv_root(hidden_state)
        normed = (hidden_state * scale_one * gains_a[l]).astype(BF)
        projected = project(normed, attn_full, l, 0, QKV_BLOCKS, BF)
        queries = projected[:, :D]
        kv_own = projected[:, D:]
        kv = gather_keys(kv_own)
        off_arr = off.reshape(1)
        attended, lse = attention(off_arr, queries, kv, seg_col, seg_keys, bias_rows[l])
        middle = hidden_state + project(attended, attn_full, l, QKV_BLOCKS, 2, F32)
        scale_two = inv_root(middle)
        mixed_in = (middle * scale_two * gains_f[l]).astype(BF)
        router_probs = jax.nn.softmax(dot(mixed_in, router[l]), axis=-1)
        gate_values = jnp.sum(router_probs[None] * route_hot, axis=2)
        if l < LAYERS - 1:
            (expert_rows,) = exchange(0, (mixed_in, tokens_at, rows_at, BF))
            expert_out, pre_act = expert_forward(expert_rows, first_mat, second_mat)
            (pair_out,) = exchange(1, (expert_out, rows_at, pairs_at, F32))
            last_grads = None
        else:
            grad_pairs = (gate_values[:, :, None] * cotangent[None]).astype(BF).reshape(-1, D)
            expert_rows, grad_rows = exchange(
                4, (mixed_in, tokens_at, rows_at, BF), (grad_pairs, pairs_at, rows_at, BF)
            )
            expert_out, grad_inputs, *last_grads = expert_back(expert_rows, grad_rows, None, first_mat, second_mat)
            pair_out, grad_mixed = exchange(
                5, (expert_out, rows_at, pairs_at, F32), (grad_inputs, rows_at, tokens_at, F32)
            )
            last_grads = (grad_mixed, *last_grads)
            pre_act = None
        pair_out = pair_out.reshape(TOP, count_q, D)
        new_state = middle + jnp.sum(gate_values[:, :, None] * pair_out, axis=0)
        stored.append(
            (hidden_state, scale_one, normed, queries, kv, lse, attended, middle, scale_two,
             mixed_in, router_probs, gate_values, pair_out, expert_rows, pre_act)
        )
        hidden_state = new_state
    out_tokens = hidden_state.astype(BF)

    grad_state = cotangent
    small = [None] * LAYERS
    attn_grads = [None] * LAYERS
    first_grads = [None] * LAYERS
    second_grads = [None] * LAYERS
    for l in reversed(range(LAYERS)):
        (state_in, scale_one, normed, queries, kv, lse, attended, middle, scale_two,
         mixed_in, router_probs, gate_values, pair_out, expert_rows, pre_act) = stored[l]
        first_mat, second_mat = expert_full[l]
        grad_gates = jnp.sum(grad_state[None] * pair_out, axis=2)
        if l == LAYERS - 1:
            grad_mixed, grad_first, grad_second = last_grads
        else:
            grad_pairs = (gate_values[:, :, None] * grad_state[None]).astype(BF).reshape(-1, D)
            (grad_rows,) = exchange(2, (grad_pairs, pairs_at, rows_at, BF))
            grad_inputs, grad_first, grad_second = expert_back(
                expert_rows, grad_rows, pre_act, first_mat, second_mat
            )
            (grad_mixed,) = exchange(3, (grad_inputs, rows_at, tokens_at, F32))
        first_grads[l] = lax.psum_scatter(grad_first, "seq", scatter_dimension=0, tiled=True)
        second_grads[l] = lax.psum_scatter(grad_second, "seq", scatter_dimension=0, tiled=True)
        grad_probs = jnp.sum(grad_gates[:, :, None] * route_hot, axis=0)
        grad_logits = router_probs * (
            grad_probs - jnp.sum(router_probs * grad_probs, axis=-1, keepdims=True)
        )
        router_grad = jnp.dot(mixed_in.astype(F32).T, grad_logits, precision=highest)
        grad_mixed = grad_mixed + jnp.dot(grad_logits, router[l].astype(F32).T, precision=highest)
        grad_mid, gain_f_grad = norm_backward(middle, scale_two, gains_f[l], grad_mixed)
        grad_mid = grad_mid + grad_state
        branch_grad = grad_mid.astype(BF)
        grad_attended = project_back(branch_grad, attn_full, l, QKV_BLOCKS, 2).astype(BF)
        if l < LAYERS - 1:
            grad_attended, first_grads[l + 1], second_grads[l + 1] = lax.optimization_barrier(
                (grad_attended, first_grads[l + 1], second_grads[l + 1])
            )
        dq, dkv, diag = attention_back(
            off_arr, queries, kv, seg_col, seg_keys, bias_rows[l], lse, grad_attended
        )
        table_grad = lax.dot_general(
            bucket_hot.astype(F32), diag, (((1,), (1,)), ((), ())), precision=highest
        )
        dkv_own = scatter_key_grads(dkv)
        grad_proj = jnp.concatenate([dq, dkv_own], axis=1)
        grad_normed = project_back(grad_proj, attn_full, l, 0, QKV_BLOCKS)
        grad_prev, gain_a_grad = norm_backward(state_in, scale_one, gains_a[l], grad_normed)
        grad_state = grad_mid + grad_prev
        attn_grads[l] = weight_grads(normed, attended, grad_proj, branch_grad)
        small[l] = (gain_a_grad, gain_f_grad, router_grad, table_grad)
    sizes = [D, D, D * experts, BUCKETS * HEADS]
    flat = jnp.concatenate([part.reshape(-1) for l in range(LAYERS) for part in small[l]])
    used = flat.size
    padded = -(-used // (3 * 8 * 128)) * 3 * 8 * 128
    whole = [g.reshape(SIDE, 2, SIDE, SIDE, 3, 16, -1) for g in attn_grads]
    attn, flat = reduce_all(*whole, jnp.pad(flat, (0, padded - used)).reshape(3, -1, 128), pick)
    attn = attn[:, :, :shard].astype(F32).transpose(1, 2, 0, 3).reshape(LAYERS, shard, -1)
    flat = flat.reshape(-1)[:used].reshape(LAYERS, -1)
    sums, at = [], 0
    for size in sizes:
        sums.append(flat[:, at : at + size])
        at += size
    return (
        out_tokens,
        grad_state,
        sums[0],
        attn[:, :, : 3 * D],
        attn[:, :, 3 * D :],
        sums[3].reshape(LAYERS, BUCKETS, HEADS),
        sums[1],
        sums[2].reshape(LAYERS, D, experts),
        jnp.stack(first_grads)[:, None].astype(F32),
        jnp.stack(second_grads)[:, None].astype(F32),
    )


def solution(mesh):
    rows = P(("grp", "seq"), None)
    slab = P(None, ("grp", "seq"), None)
    expert = P(None, "grp", "seq", None)
    return jax.shard_map(
        on_device,
        mesh=mesh,
        in_specs=(
            rows, P("grp", "seq"), P(), rows, P(), slab, slab, P(), P(), P(), expert, expert, rows,
        ),
        out_specs=(rows, rows, P(), slab, slab, P(), P(), P(), expert, expert),
        check_vma=False,
    )
```

```python
import functools

import jax
import jax.numpy as jnp
from jax import lax
from jax.experimental import pallas as pl
from jax.experimental.pallas import tpu as pltpu
from jax.sharding import PartitionSpec as P

D = 768
HEADS = 12
HEAD_DIM = 64
PAIRS = HEADS // 2
TOP = 2
BUCKETS = 32
LAYERS = 2
BACK = 4
EPS = 1e-06
MASKED = -1e30
SCALE = HEAD_DIM**-0.5
BF = jnp.bfloat16
F32 = jnp.float32
highest = lax.Precision.HIGHEST
VMEM = pltpu.VMEM
LITTLE = pl.CostEstimate(flops=1024, bytes_accessed=1024, transcendentals=0)


def dot(a, b, contract=((1,), (0,))):
    return lax.dot_general(a, b, (contract, ((), ())), preferred_element_type=F32)


def inv_root(values):
    return lax.rsqrt(jnp.mean(values * values, axis=-1, keepdims=True) + EPS)


def norm_backward(values, scale_rows, gain_row, grad_out):
    scaled = grad_out * gain_row
    grad_gain = jnp.sum(grad_out * values * scale_rows, axis=0)
    cubed = scale_rows * scale_rows * scale_rows
    input_gradient = scale_rows * scaled - values * cubed * jnp.mean(
        values * scaled, axis=-1, keepdims=True
    )
    return (input_gradient, grad_gain)


def head_scores(q2, k2, low_lanes, head, allowed, bias_ref, width, span):
    mine = low_lanes if head % 2 == 0 else jnp.logical_not(low_lanes)
    q_head = jnp.where(mine, q2, jnp.zeros_like(q2))
    scores = dot(q_head, k2, ((1,), (1,))) * SCALE
    row = jnp.broadcast_to(bias_ref[head : head + 1, :], (q2.shape[0], span))
    bias = pltpu.roll(row, 0, 1, stride=1, stride_axis=0)[:, :width]
    return q_head, mine, jnp.where(allowed, scores + bias, MASKED)


def first_key_block():
    me = lax.axis_index("seq")
    return me // BACK * (me % BACK)


def allowed_pairs(off_ref, segq_ref, segk_ref, rows, width):
    i = lax.broadcasted_iota(jnp.int32, (rows, width), 0)
    j = lax.broadcasted_iota(jnp.int32, (rows, width), 1)
    return (off_ref[0] + i - j >= 0) & (segq_ref[...] == segk_ref[...])


def attention_kernel(off_ref, q_ref, kv_ref, segq_ref, segk_ref, bias_ref, out_ref, lse_ref):
    rows, width, span = q_ref.shape[0], segk_ref.shape[1], bias_ref.shape[1]
    first = first_key_block()
    window = pl.ds(pl.multiple_of(first * rows, rows), width)
    allowed = allowed_pairs(off_ref, segq_ref, segk_ref, rows, width)
    low_lanes = lax.broadcasted_iota(jnp.int32, (rows, 128), 1) < HEAD_DIM
    lane = lax.broadcasted_iota(jnp.int32, (rows, 128), 1)
    totals = jnp.zeros((rows, 128), F32)
    for pair in range(PAIRS):
        at = slice(pair * 128, pair * 128 + 128)
        q2, k2 = q_ref[:, at], kv_ref[window, at]
        v2 = kv_ref[window, D + pair * 128 : D + pair * 128 + 128]
        both = []
        for head in (2 * pair, 2 * pair + 1):
            _, _, scores = head_scores(q2, k2, low_lanes, head, allowed, bias_ref, width, span)
            row_max = jnp.max(scores, axis=1, keepdims=True)
            exponent = jnp.exp(scores - row_max)
            row_total = jnp.sum(exponent, axis=1, keepdims=True)
            weights = (exponent / row_total).astype(BF)
            both.append(dot(weights, v2))
            totals = jnp.where(lane == head, row_max + jnp.log(row_total), totals)
        out_ref[:, at] = jnp.where(low_lanes, both[0], both[1]).astype(BF)
    lse_ref[...] = totals


def attention_back_kernel(
    off_ref, q_ref, kv_ref, segq_ref, segk_ref, bias_ref, lse_ref, grad_ref, dq_ref, dkv_ref, diag_ref
):
    rows, width, span = q_ref.shape[0], segk_ref.shape[1], bias_ref.shape[1]
    first = first_key_block()
    window = pl.ds(pl.multiple_of(first * rows, rows), width)
    allowed = allowed_pairs(off_ref, segq_ref, segk_ref, rows, width)
    low_lanes = lax.broadcasted_iota(jnp.int32, (rows, 128), 1) < HEAD_DIM
    lane = lax.broadcasted_iota(jnp.int32, (rows, 128), 1)
    i = lax.broadcasted_iota(jnp.int32, (rows, rows), 0)
    j = lax.broadcasted_iota(jnp.int32, (rows, rows), 1)
    flip = (i + j == rows - 1).astype(BF)
    dkv_ref[...] = jnp.zeros_like(dkv_ref)
    for pair in range(PAIRS):
        at = slice(pair * 128, pair * 128 + 128)
        at_v = slice(D + pair * 128, D + pair * 128 + 128)
        q2, k2, v2, g2 = q_ref[:, at], kv_ref[window, at], kv_ref[window, at_v], grad_ref[:, at]
        dq, dk, dv = [], None, None
        for head in (2 * pair, 2 * pair + 1):
            q_head, mine, scores = head_scores(q2, k2, low_lanes, head, allowed, bias_ref, width, span)
            log_total = jnp.sum(jnp.where(lane == head, lse_ref[...], 0.0), axis=1, keepdims=True)
            probs = jnp.exp(scores - log_total)
            g_head = jnp.where(mine, g2, jnp.zeros_like(g2))
            grad_probs = dot(g_head, v2, ((1,), (1,)))
            inner = jnp.sum(probs * grad_probs, axis=1, keepdims=True)
            grad_scores = (probs * (grad_probs - inner)).astype(BF)
            dq.append(dot(grad_scores, k2))
            dk_head = dot(grad_scores, q_head, ((0,), (0,)))
            dv_head = dot(probs.astype(BF), g_head, ((0,), (0,)))
            dk = dk_head if dk is None else dk + dk_head
            dv = dv_head if dv is None else dv + dv_head
            turned = jnp.concatenate(
                [dot(flip, grad_scores), jnp.zeros((rows, span - width), F32)], axis=1
            )
            turned = pltpu.roll(turned, span - (rows - 1), 1, stride=1, stride_axis=0)
            diag_ref[head : head + 1, :] = jnp.sum(turned, axis=0, keepdims=True)
        dq_ref[:, at] = (jnp.where(low_lanes, dq[0], dq[1]) * SCALE).astype(BF)
        blocks = pl.ds(first, width // rows)
        dkv_ref[blocks, :, at] = (dk * SCALE).astype(BF).reshape(-1, rows, 128)
        dkv_ref[blocks, :, at_v] = dv.astype(BF).reshape(-1, rows, 128)


def vmem_specs(n):
    return [pl.BlockSpec(memory_space=VMEM) for _ in range(n)]


def attention(off, queries, kv, segq, segk, bias):
    return pl.pallas_call(
        attention_kernel,
        out_shape=(
            jax.ShapeDtypeStruct(queries.shape, BF),
            jax.ShapeDtypeStruct((queries.shape[0], 128), F32),
        ),
        in_specs=[pl.BlockSpec(memory_space=pltpu.SMEM)] + vmem_specs(5),
        out_specs=tuple(vmem_specs(2)),
        cost_estimate=LITTLE,
        compiler_params=pltpu.CompilerParams(vmem_limit_bytes=32 * 2**20),
    )(off, queries, kv, segq, segk, bias)


def attention_back(off, queries, kv, segq, segk, bias, lse, grad):
    return pl.pallas_call(
        attention_back_kernel,
        out_shape=(
            jax.ShapeDtypeStruct(queries.shape, BF),
            jax.ShapeDtypeStruct((kv.shape[0] // queries.shape[0], queries.shape[0], kv.shape[1]), BF),
            jax.ShapeDtypeStruct(bias.shape, F32),
        ),
        in_specs=[pl.BlockSpec(memory_space=pltpu.SMEM)] + vmem_specs(7),
        out_specs=tuple(vmem_specs(3)),
        cost_estimate=LITTLE,
        compiler_params=pltpu.CompilerParams(vmem_limit_bytes=32 * 2**20),
    )(off, queries, kv, segq, segk, bias, lse, grad)


MESH_ID = pl.DeviceIdType.MESH
QKV_BLOCKS = 6
SIDE = 4


def place_of_device():
    grp, seq = lax.axis_index("grp"), lax.axis_index("seq")
    return [grp // SIDE, grp % SIDE, seq // 2], seq % 2


def device_at(coords, core):
    return (coords[0] * SIDE + coords[1], coords[2] * 2 + core)


def moved(coords, axis, delta):
    return [(c + delta) % SIDE if a == axis else c for a, c in enumerate(coords)]


def remote(src, dst, send_sem, recv_sem, device):
    return pltpu.make_async_remote_copy(
        src_ref=src, dst_ref=dst, send_sem=send_sem, recv_sem=recv_sem, device_id=device, device_id_type=MESH_ID
    )


def greet(devices):
    barrier = pltpu.get_barrier_semaphore()
    for device in devices:
        pl.semaphore_signal(barrier, inc=1, device_id=device, device_id_type=MESH_ID)
    pl.semaphore_wait(barrier, len(devices))


def sequence_partners(coords, core):
    seq = coords[2] * 2 + core
    others = [(seq + d) % (2 * SIDE) for d in range(1, 2 * SIDE)]
    return [(coords[0] * SIDE + coords[1], s) for s in others], others


def all_partners(coords, core):
    partners = [device_at(moved(coords, a, d), core) for a in range(2) for d in range(1, SIDE)]
    return partners + sequence_partners(coords, core)[0]


def attn_gather_kernel(
    own_ref, seg_ref, pick_ref, full_ref, segs_ref, rows_ref,
    row_send, row_recv, send_sem, recv_sem, core_send, core_recv, seg_send, seg_recv,
):
    coords, core = place_of_device()
    sibling = device_at(coords, 1 - core)
    y, x, z = coords
    seq = z * 2 + core
    greet(all_partners(coords, core))
    rows_ref[seq] = own_ref[seq]
    segs_ref[z, core] = seg_ref[...]
    devices, numbers = sequence_partners(coords, core)
    row_copies = []
    for n, (device, s) in enumerate(zip(devices, numbers)):
        row_copies.append(remote(own_ref.at[s], rows_ref.at[seq], row_send.at[n], row_recv.at[n], device))
        row_copies[-1].start()
    seg_copies = []
    for d in range(1, SIDE):
        one = segs_ref.at[z, core]
        seg_copies.append(remote(one, one, seg_send.at[d - 1], seg_recv.at[d - 1], device_at(moved(coords, 2, d), core)))
        seg_copies[-1].start()
    for copy in row_copies:
        copy.wait()
    for l in range(LAYERS):
        flat = rows_ref[:, l].reshape(-1, own_ref.shape[-1])
        block = dot(pick_ref[...], flat).astype(BF)
        for p in range(3):
            full_ref[z, core, l, y, x, p] = block[16 * p : 16 * p + 16]

    def region(p, free, fixed=None):
        at = [slice(None) if a in free else coords[a] for a in range(3)]
        if fixed is not None:
            at[fixed[0]] = fixed[1]
        return full_ref.at[at[2], core, :, at[0], at[1], p]

    copies = {}
    core_copies = []

    def to_sibling(part, number):
        core_copies.append(remote(part, part, core_send.at[number], core_recv.at[number], sibling))
        core_copies[-1].start()

    for k in range(3):
        for p in range(3):
            if k:
                for d in (1, 3, 2):
                    copies[k - 1, p, d].wait_recv()
            axis, free = (p + k) % 3, [(p + i) % 3 for i in range(k)]
            part = region(p, free)
            for d in (1, 3, 2):
                copies[k, p, d] = remote(
                    part, part, send_sem.at[k, p, d - 1], recv_sem.at[k, p, d - 1],
                    device_at(moved(coords, axis, d), core),
                )
                copies[k, p, d].start()
            if k == 2:
                to_sibling(part, 4 * p)
    for copy in seg_copies:
        copy.wait_recv()
    part = segs_ref.at[:, core]
    seg_last = remote(part, part, seg_send.at[3], seg_recv.at[3], sibling)
    seg_last.start()
    for d in (1, 3, 2):
        for p in range(3):
            axis = (p + 2) % 3
            copies[2, p, d].wait_recv()
            came = (coords[axis] + SIDE - d) % SIDE
            to_sibling(region(p, [a for a in range(3) if a != axis], (axis, came)), 4 * p + d)
    for copy in copies.values():
        copy.wait_send()
    for copy in seg_copies:
        copy.wait_send()
    seg_last.wait()
    for copy in core_copies:
        copy.wait()


def attn_gather(own, seg, pick):
    dma = pltpu.SemaphoreType.DMA
    width = own.shape[-1]
    return pl.pallas_call(
        attn_gather_kernel,
        out_shape=(
            jax.ShapeDtypeStruct((SIDE, 2, LAYERS, SIDE, SIDE, 3, 16, width), BF),
            jax.ShapeDtypeStruct((SIDE, 2) + seg.shape, F32),
        ),
        in_specs=vmem_specs(3),
        out_specs=tuple(vmem_specs(2)),
        scratch_shapes=[VMEM(own.shape, BF), dma((7,)), dma((7,)), dma((3, 3, 3)), dma((3, 3, 3)),
                        dma((12,)), dma((12,)), dma((4,)), dma((4,))],
        cost_estimate=LITTLE,
        compiler_params=pltpu.CompilerParams(
            collective_id=0, has_side_effects=True, vmem_limit_bytes=40 * 2**20
        ),
    )(own, seg, pick)


def reduce_kernel(
    x0_ref, x1_ref, small_ref, pick_ref, out_ref, small_out, got_core, y_ref, got_one, z_ref, got_two, w_ref, got_three,
    rows_ref, s_core, s_got, core_send, core_recv, send_sem, recv_sem, s_core_send, s_core_recv, s_send, s_recv,
    row_send, row_recv,
):
    coords, core = place_of_device()
    sibling = device_at(coords, 1 - core)
    greet(all_partners(coords, core))
    x_refs = (x0_ref, x1_ref)
    order = (2, 0, 1)
    first = {}
    for p in range(3):
        for l in range(LAYERS):
            first[p, l] = remote(
                x_refs[l].at[:, 1 - core, :, :, p], got_core.at[p, l], core_send.at[p, l], core_recv.at[p, l], sibling
            )
            first[p, l].start()
    s_first = remote(small_ref, s_core, s_core_send, s_core_recv, sibling)
    s_first.start()

    def axes_left(p, k):
        gone = [(p + i) % 3 for i in range(k)]
        return [a for a in order if a not in gone]

    def spread(p, k, source, target):
        axis, out = (p + k) % 3, []
        for d in (1, 3, 2):
            to = moved(coords, axis, d)
            index = tuple(to[axis] if a == axis else slice(None) for a in axes_left(p, k))
            copy = remote(
                source.at[(p, *index)], target.at[p, d - 1], send_sem.at[k, p, d - 1], recv_sem.at[k, p, d - 1],
                device_at(to, core),
            )
            copy.start()
            out.append(copy)
        return out

    def spread_small(p, k):
        axis, out = (p + k) % 3, []
        for d in (1, 3, 2):
            copy = remote(
                s_got.at[k, p, 0], s_got.at[k, p, d], s_send.at[k, p, d - 1], s_recv.at[k, p, d - 1],
                device_at(moved(coords, axis, d), core),
            )
            copy.start()
            out.append(copy)
        return out

    def small_sum(p, k):
        axis = (p + k) % 3
        total = s_got[k, p, coords[axis]]
        for v in range(1, SIDE):
            total = total + s_got[k, p, (coords[axis] + SIDE - v) % SIDE]
        return total

    sent, s_sent = {}, {}
    s_first.wait()
    for p in range(3):
        s_got[0, p, 0] = small_ref[p] + s_core[p]
        s_sent[0, p] = spread_small(p, 0)
    for p in range(3):
        for l in range(LAYERS):
            first[p, l].wait()

        def add_core(i, carry, p=p):
            a, b, c = i // (SIDE * SIDE), i // SIDE % SIDE, i % SIDE
            for l in range(LAYERS):
                total = x_refs[l][a, core, b, c, p].astype(F32) + got_core[p, l, a, b, c].astype(F32)
                y_ref[p, a, b, c, l] = total.astype(BF)
            return carry

        lax.fori_loop(0, SIDE**3, add_core, 0)
        sent[0, p] = spread(p, 0, y_ref, got_one)
    for p in range(3):
        for copy in s_sent[0, p]:
            copy.wait()
        s_got[1, p, 0] = small_sum(p, 0)
        s_sent[1, p] = spread_small(p, 1)
    for p in range(3):
        for copy in sent[0, p]:
            copy.wait()
        at = order.index(p)

        def add_one(i, carry, p=p, at=at):
            a, b = i // SIDE, i % SIDE
            index = [a, b]
            index.insert(at, coords[p])
            total = y_ref[(p, *index)].astype(F32)
            for d in range(3):
                total = total + got_one[p, d, a, b].astype(F32)
            z_ref[p, a, b] = total.astype(BF)
            return carry

        lax.fori_loop(0, SIDE**2, add_one, 0)
        sent[1, p] = spread(p, 1, z_ref, got_two)
    for p in range(3):
        for copy in s_sent[1, p]:
            copy.wait()
        s_got[2, p, 0] = small_sum(p, 1)
        s_sent[2, p] = spread_small(p, 2)
    for p in range(3):
        for copy in sent[1, p]:
            copy.wait()
        axis = (p + 1) % 3

        def add_two(i, carry, p=p, axis=axis):
            index = tuple(coords[axis] if a == axis else i for a in axes_left(p, 1))
            total = z_ref[(p, *index)].astype(F32)
            for d in range(3):
                total = total + got_two[p, d, i].astype(F32)
            w_ref[p, i] = total.astype(BF)
            return carry

        lax.fori_loop(0, SIDE, add_two, 0)
        sent[2, p] = spread(p, 2, w_ref, got_three)
    for p in range(3):
        for copy in s_sent[2, p]:
            copy.wait()
        small_out[p] = small_sum(p, 2)
    blocks = []
    for p in range(3):
        for copy in sent[2, p]:
            copy.wait()
        total = w_ref[p, coords[(p + 2) % 3]].astype(F32)
        for d in range(3):
            total = total + got_three[p, d].astype(F32)
        blocks.append(total.astype(BF))
    for l in range(LAYERS):
        block = jnp.concatenate([part[l] for part in blocks], axis=0)
        spread_rows = dot(pick_ref[...], block, ((0,), (0,))).astype(BF)
        rows_ref[:, l] = spread_rows.reshape(2 * SIDE, 16, -1)
    seq = coords[2] * 2 + core
    out_ref[seq] = rows_ref[seq]
    devices, numbers = sequence_partners(coords, core)
    last = []
    for n, (device, s) in enumerate(zip(devices, numbers)):
        last.append(remote(rows_ref.at[s], out_ref.at[seq], row_send.at[n], row_recv.at[n], device))
        last[-1].start()
    for copy in last:
        copy.wait()


def reduce_all(x0, x1, small, pick):
    width, part = x0.shape[-1], small.shape[1:]
    block = (LAYERS, 16, width)
    rows = (2 * SIDE, LAYERS, 16, width)
    dma = pltpu.SemaphoreType.DMA
    return pl.pallas_call(
        reduce_kernel,
        out_shape=(jax.ShapeDtypeStruct(rows, BF), jax.ShapeDtypeStruct(small.shape, F32)),
        in_specs=vmem_specs(4),
        out_specs=tuple(vmem_specs(2)),
        scratch_shapes=[
            VMEM((3, LAYERS, SIDE, SIDE, SIDE, 16, width), BF),
            VMEM((3, SIDE, SIDE, SIDE) + block, BF),
            VMEM((3, 3, SIDE, SIDE) + block, BF),
            VMEM((3, SIDE, SIDE) + block, BF),
            VMEM((3, 3, SIDE) + block, BF),
            VMEM((3, SIDE) + block, BF),
            VMEM((3, 3) + block, BF),
            VMEM(rows, BF),
            VMEM(small.shape, F32),
            VMEM((3, 3, SIDE) + part, F32),
            dma((3, LAYERS)), dma((3, LAYERS)), dma((3, 3, 3)), dma((3, 3, 3)), dma(()), dma(()),
            dma((3, 3, 3)), dma((3, 3, 3)), dma((7,)), dma((7,)),
        ],
        cost_estimate=LITTLE,
        compiler_params=pltpu.CompilerParams(
            collective_id=1, has_side_effects=True, vmem_limit_bytes=50 * 2**20
        ),
    )(x0, x1, small, pick)


def scaled_rows(values, gain_row):
    scale = inv_root(values)
    return scale, (values * scale * gain_row).astype(BF)


def queries_keys_kernel(x_ref, gain_ref, w_ref, q_ref, kv_ref, normed_ref, scale_ref):
    width, some = w_ref.shape[3], w_ref.shape[0]

    @pl.when(pl.program_id(0) == 0)
    def _():
        scale_ref[...], normed_ref[...] = scaled_rows(x_ref[...], gain_ref[...])
        for s in range(2):
            q_ref[:, s * width : (s + 1) * width] = dot(normed_ref[...], w_ref[s, 0]).astype(BF)
        kv_ref[:, :width] = dot(normed_ref[...], w_ref[2, 0]).astype(BF)

    @pl.when(pl.program_id(0) == 1)
    def _():
        for s in range(some):
            kv_ref[:, (s + 1) * width : (s + 2) * width] = dot(normed_ref[...], w_ref[s, 0]).astype(BF)


def queries_keys(x, gain, full, layer):
    depth, width = full.shape[2:]
    rows = x.shape[0]

    def whole(columns):
        return pl.BlockSpec((rows, columns), lambda s: (0, 0))

    return pl.pallas_call(
        queries_keys_kernel,
        grid=(2,),
        out_shape=(
            jax.ShapeDtypeStruct((rows, D), BF),
            jax.ShapeDtypeStruct((rows, 2 * D), BF),
            jax.ShapeDtypeStruct((rows, D), BF),
            jax.ShapeDtypeStruct((rows, 1), F32),
        ),
        in_specs=[
            whole(D),
            pl.BlockSpec((1, D), lambda s: (0, 0)),
            pl.BlockSpec((QKV_BLOCKS // 2, 1, depth, width), lambda s: (s, layer, 0, 0)),
        ],
        out_specs=(whole(D), whole(2 * D), whole(D), whole(1)),
        cost_estimate=LITTLE,
        compiler_params=pltpu.CompilerParams(vmem_limit_bytes=56 * 2**20),
    )(x, gain[None], full)


def after_attention_kernel(attended_ref, x_ref, gain_ref, w_ref, middle_ref, mixed_ref, scale_ref):
    width = w_ref.shape[3]
    for s in range(w_ref.shape[0]):
        at = slice(s * width, (s + 1) * width)
        middle_ref[:, at] = x_ref[:, at] + dot(attended_ref[...], w_ref[s, 0])
    scale_ref[...], mixed_ref[...] = scaled_rows(middle_ref[...], gain_ref[...])


def after_attention(attended, x, gain, full, layer):
    depth, width = full.shape[2:]
    rows = x.shape[0]
    whole = pl.BlockSpec((rows, D), lambda s: (0, 0))
    return pl.pallas_call(
        after_attention_kernel,
        grid=(1,),
        out_shape=(
            jax.ShapeDtypeStruct((rows, D), F32),
            jax.ShapeDtypeStruct((rows, D), BF),
            jax.ShapeDtypeStruct((rows, 1), F32),
        ),
        in_specs=[
            whole,
            whole,
            pl.BlockSpec((1, D), lambda s: (0, 0)),
            pl.BlockSpec((2, 1, depth, width), lambda s: (QKV_BLOCKS // 2, layer, 0, 0)),
        ],
        out_specs=(whole, whole, pl.BlockSpec((rows, 1), lambda s: (0, 0))),
        cost_estimate=LITTLE,
        compiler_params=pltpu.CompilerParams(vmem_limit_bytes=56 * 2**20),
    )(attended, x, gain[None], full)


def branch_back_kernel(x_ref, w_ref, out_ref):
    width = w_ref.shape[3]
    total = dot(x_ref[:, :width], w_ref[0, 0], ((1,), (1,)))
    out_ref[...] = (total + dot(x_ref[:, width:], w_ref[1, 0], ((1,), (1,)))).astype(BF)


def branch_back(x, full, layer):
    depth, width = full.shape[2:]
    whole = pl.BlockSpec(x.shape, lambda s: (0, 0))
    return pl.pallas_call(
        branch_back_kernel,
        grid=(1,),
        out_shape=jax.ShapeDtypeStruct(x.shape, BF),
        in_specs=[
            whole,
            pl.BlockSpec((2, 1, depth, width), lambda s: (QKV_BLOCKS // 2, layer, 0, 0)),
        ],
        out_specs=whole,
        cost_estimate=LITTLE,
        compiler_params=pltpu.CompilerParams(vmem_limit_bytes=56 * 2**20),
    )(x, full)


def input_grad_kernel(grad_ref, w_ref, x_ref, scale_ref, gain_ref, mid_ref, out_ref, gain_out, total):
    @pl.when(pl.program_id(0) == 0)
    def _():
        total[...] = jnp.zeros_like(total)

    width = w_ref.shape[3]
    for s in range(w_ref.shape[0]):
        total[...] += dot(grad_ref[:, s * width : (s + 1) * width], w_ref[s, 0], ((1,), (1,)))

    @pl.when(pl.program_id(0) == pl.num_programs(0) - 1)
    def _():
        grad, gain_grad = norm_backward(x_ref[...], scale_ref[...], gain_ref[...], total[...])
        out_ref[...] = mid_ref[...] + grad
        gain_out[...] = gain_grad[None]


def input_grad(grad_proj, full, layer, x, scale, gain, grad_mid):
    depth, width = full.shape[2:]
    rows = x.shape[0]
    some = QKV_BLOCKS // 2
    whole = pl.BlockSpec((rows, D), lambda s: (0, 0))
    line = pl.BlockSpec((1, D), lambda s: (0, 0))
    return pl.pallas_call(
        input_grad_kernel,
        grid=(2,),
        out_shape=(jax.ShapeDtypeStruct((rows, D), F32), jax.ShapeDtypeStruct((1, D), F32)),
        in_specs=[
            pl.BlockSpec((rows, some * width), lambda s: (0, s)),
            pl.BlockSpec((some, 1, depth, width), lambda s: (s, layer, 0, 0)),
            whole,
            pl.BlockSpec((rows, 1), lambda s: (0, 0)),
            line,
            whole,
        ],
        out_specs=(whole, line),
        scratch_shapes=[VMEM((rows, D), F32)],
        cost_estimate=LITTLE,
        compiler_params=pltpu.CompilerParams(vmem_limit_bytes=56 * 2**20),
    )(grad_proj, full, x, scale, gain[None], grad_mid)


def weight_grad_kernel(normed_ref, attended_ref, proj_ref, branch_ref, out_ref):
    step, width = pl.program_id(0), out_ref.shape[2]

    def fill(left, right):
        for s in range(out_ref.shape[0]):
            out_ref[s] = dot(left[...], right[:, s * width : (s + 1) * width], ((0,), (0,))).astype(BF)

    @pl.when(step < QKV_BLOCKS // 2)
    def _():
        fill(normed_ref, proj_ref)

    @pl.when(step >= QKV_BLOCKS // 2)
    def _():
        fill(attended_ref, branch_ref)


def weight_grads(normed, attended, grad_proj, branch_grad):
    rows, width = normed.shape[0], grad_proj.shape[1] // QKV_BLOCKS
    last = QKV_BLOCKS // 2 - 1
    return pl.pallas_call(
        weight_grad_kernel,
        grid=(SIDE,),
        out_shape=jax.ShapeDtypeStruct((2 * SIDE, D, width), BF),
        in_specs=[
            pl.BlockSpec((rows, D), lambda s: (0, 0)),
            pl.BlockSpec((rows, D), lambda s: (0, 0)),
            pl.BlockSpec((rows, 2 * width), lambda s: (0, jnp.minimum(s, last))),
            pl.BlockSpec((rows, 2 * width), lambda s: (0, 0)),
        ],
        out_specs=pl.BlockSpec((2, D, width), lambda s: (s, 0, 0)),
        cost_estimate=LITTLE,
        compiler_params=pltpu.CompilerParams(vmem_limit_bytes=56 * 2**20),
    )(normed, attended, grad_proj, branch_grad)


def kv_gather(own_ref, kv_ref, send_sem, recv_sem):
    coords, core = place_of_device()
    z, rows = coords[2], own_ref.shape[0]
    half = rows // 2
    up, down = moved(coords, 2, 1), moved(coords, 2, 3)
    up_z, down_z, far_z = (z + 1) % SIDE, (z + 3) % SIDE, (z + 2) % SIDE
    sibling = device_at(coords, 1 - core)

    def block(at, start=0, size=rows):
        return kv_ref.at[pl.ds(pl.multiple_of((at * 2 + core) * rows + start, half), size)]

    copies = []

    def send(part, number, device):
        copy = remote(part, part, send_sem.at[number], recv_sem.at[number], device)
        copy.start()
        copies.append(copy)
        return copy

    kv_ref[pl.ds(pl.multiple_of((z * 2 + core) * rows, rows), rows), :] = own_ref[...]
    greet([device_at(up, core), device_at(down, core), sibling])
    went_up = send(block(z), 0, device_at(up, core))
    went_down = send(block(z), 1, device_at(down, core))
    from_core = [send(block(z), 2, sibling)]
    went_up.wait_recv()
    far_up = send(block(down_z, 0, half), 3, device_at(up, core))
    from_core.append(send(block(down_z), 4, sibling))
    went_down.wait_recv()
    far_down = send(block(up_z, half, half), 5, device_at(down, core))
    from_core.append(send(block(up_z), 6, sibling))
    far_up.wait_recv()
    from_core.append(send(block(far_z, 0, half), 7, sibling))
    far_down.wait_recv()
    from_core.append(send(block(far_z, half, half), 8, sibling))
    for copy in from_core:
        copy.wait_recv()
    for copy in copies:
        copy.wait_send()


def kv_scatter(grads_ref, out_ref, got_core, sums, got_far, got_near, send_sem, recv_sem):
    coords, core = place_of_device()
    z, rows = coords[2], out_ref.shape[0]
    half = rows // 2
    up, down = device_at(moved(coords, 2, 1), core), device_at(moved(coords, 2, 3), core)
    up_z, down_z, far_z = (z + 1) % SIDE, (z + 3) % SIDE, (z + 2) % SIDE
    sibling = device_at(coords, 1 - core)
    greet([up, down, sibling])
    copies = []

    def send(src, dst, number, device):
        copy = remote(src, dst, send_sem.at[number], recv_sem.at[number], device)
        copy.start()
        copies.append(copy)
        return copy

    order = [far_z, up_z, down_z, z]
    cross = [send(grads_ref.at[at * 2 + 1 - core], got_core.at[n], n, sibling) for n, at in enumerate(order)]

    def total(n):
        cross[n].wait_recv()
        return grads_ref[order[n] * 2 + core].astype(F32) + got_core[n].astype(F32)

    sums[0] = total(0).astype(BF)
    far_up = send(sums.at[0, pl.ds(0, half)], got_far.at[0], 4, up)
    far_down = send(sums.at[0, pl.ds(half, half)], got_far.at[1], 5, down)
    up_sum, down_sum = total(1), total(2)
    sums[1, half:] = up_sum[half:].astype(BF)
    sums[2, :half] = down_sum[:half].astype(BF)
    far_up.wait_recv()
    sums[1, :half] = (up_sum[:half] + got_far[0].astype(F32)).astype(BF)
    near_up = send(sums.at[1], got_near.at[0], 6, up)
    far_down.wait_recv()
    sums[2, half:] = (down_sum[half:] + got_far[1].astype(F32)).astype(BF)
    near_down = send(sums.at[2], got_near.at[1], 7, down)
    own = total(3)
    near_up.wait_recv()
    near_down.wait_recv()
    out_ref[...] = (own + got_near[0].astype(F32) + got_near[1].astype(F32)).astype(BF)
    for copy in copies:
        copy.wait_send()

def gather_keys(own):
    return pl.pallas_call(
        kv_gather,
        out_shape=jax.ShapeDtypeStruct((2 * SIDE * own.shape[0], own.shape[1]), BF),
        in_specs=vmem_specs(1),
        out_specs=vmem_specs(1)[0],
        scratch_shapes=[pltpu.SemaphoreType.DMA((9,))] * 2,
        cost_estimate=LITTLE,
        compiler_params=pltpu.CompilerParams(
            collective_id=2, has_side_effects=True, vmem_limit_bytes=20 * 2**20
        ),
    )(own)


def scatter_key_grads(grads):
    block = grads.shape[1:]
    return pl.pallas_call(
        kv_scatter,
        out_shape=jax.ShapeDtypeStruct(block, BF),
        in_specs=vmem_specs(1),
        out_specs=vmem_specs(1)[0],
        scratch_shapes=[
            VMEM((SIDE,) + block, BF),
            VMEM((3,) + block, BF),
            VMEM((2, block[0] // 2, block[1]), BF),
            VMEM((2,) + block, BF),
            pltpu.SemaphoreType.DMA((8,)),
            pltpu.SemaphoreType.DMA((8,)),
        ],
        cost_estimate=LITTLE,
        compiler_params=pltpu.CompilerParams(
            collective_id=3, has_side_effects=True, vmem_limit_bytes=20 * 2**20
        ),
    )(grads)


def exchange_kernel(n, *refs):
    loads, outs = refs[: 5 * n], refs[5 * n : 6 * n]
    to_send, got, send_sem, recv_sem = refs[6 * n :]
    grp, seq = lax.axis_index("grp"), lax.axis_index("seq")
    peers, half = got.shape[1], got.shape[3]
    others = [(grp + d) % peers for d in range(1, peers)]
    greet([(other, seq) for other in others])
    for i in range(n):
        x_ref, put_left, put_right = loads[5 * i : 5 * i + 3]
        rows = dot(put_left[...], x_ref[:, :half]) + dot(put_right[...], x_ref[:, half:])
        to_send[i] = rows.astype(BF).reshape(to_send.shape[1:])
    copies = []
    for k, other in enumerate(others):
        copies.append(
            remote(to_send.at[:, other], got.at[:, grp], send_sem.at[k], recv_sem.at[k], (other, seq))
        )
        copies[-1].start()
    got[:, grp] = to_send[:, grp]
    for copy in copies:
        copy.wait()
    for i in range(n):
        take_left, take_right = loads[5 * i + 3 : 5 * i + 5]
        came = got[i].reshape(-1, half)
        outs[i][:, :half] = dot(take_left[...], came, ((0,), (0,))).astype(outs[i].dtype)
        outs[i][:, half:] = dot(take_right[...], came, ((0,), (0,))).astype(outs[i].dtype)


def exchange(number, *loads):
    peers, n = lax.axis_size("grp"), len(loads)
    x, put = loads[0][:2]
    slots = (n, peers, put[0].shape[0] // peers, x.shape[1] // 2)
    dma = pltpu.SemaphoreType.DMA
    return pl.pallas_call(
        functools.partial(exchange_kernel, n),
        out_shape=tuple(
            jax.ShapeDtypeStruct((take[0].shape[1], x.shape[1]), dtype) for x, _, take, dtype in loads
        ),
        in_specs=vmem_specs(5 * n),
        out_specs=tuple(vmem_specs(n)),
        scratch_shapes=[VMEM(slots, BF), VMEM(slots, BF), dma((peers - 1,)), dma((peers - 1,))],
        cost_estimate=LITTLE,
        compiler_params=pltpu.CompilerParams(
            collective_id=4 + number, has_side_effects=True, vmem_limit_bytes=24 * 2**20
        ),
    )(*[part for x, put, take, _ in loads for part in (x, *put, *take)])


FF_BLOCK = 1024
GELU_A, GELU_B = 0.7978845608028654, 0.044715


def expert_kernel(x_ref, in_ref, out_w_ref, out_ref, pre_ref, total):
    step = pl.program_id(0)

    @pl.when(step == 0)
    def _():
        total[...] = jnp.zeros_like(total)

    pre = dot(x_ref[...], in_ref[...])
    pre_ref[...] = pre
    act = 0.5 * pre * (1.0 + jnp.tanh(GELU_A * (pre + GELU_B * pre * pre * pre)))
    total[...] += dot(act.astype(BF), out_w_ref[...])

    @pl.when(step == pl.num_programs(0) - 1)
    def _():
        out_ref[...] = total[...].astype(BF)


def expert_forward(rows, first_mat, second_mat):
    width, hidden = first_mat.shape
    count = rows.shape[0]
    return pl.pallas_call(
        expert_kernel,
        grid=(hidden // FF_BLOCK,),
        out_shape=(jax.ShapeDtypeStruct(rows.shape, BF), jax.ShapeDtypeStruct((count, hidden), F32)),
        in_specs=[
            pl.BlockSpec((count, width), lambda j: (0, 0)),
            pl.BlockSpec((width, FF_BLOCK), lambda j: (0, j)),
            pl.BlockSpec((FF_BLOCK, width), lambda j: (j, 0)),
        ],
        out_specs=(
            pl.BlockSpec((count, width), lambda j: (0, 0)),
            pl.BlockSpec((count, FF_BLOCK), lambda j: (0, j)),
        ),
        scratch_shapes=[VMEM((count, width), F32)],
        cost_estimate=LITTLE,
        compiler_params=pltpu.CompilerParams(vmem_limit_bytes=50 * 2**20),
    )(rows, first_mat, second_mat)


def expert_back_kernel(again, x_ref, grad_ref, *refs):
    pre_ref, in_ref, out_w_ref, out_ref, gx_ref, gin_ref, gout_ref, total, out_total = (
        (None, *refs) if again else (*refs[:3], None, *refs[3:], None)
    )
    step = pl.program_id(0)

    @pl.when(step == 0)
    def _():
        total[...] = jnp.zeros_like(total)
        if again:
            out_total[...] = jnp.zeros_like(out_total)

    pre = dot(x_ref[...], in_ref[...]) if again else pre_ref[...]
    grad = grad_ref[...]
    square = pre * pre
    curve = jnp.tanh(GELU_A * (pre + GELU_B * pre * square))
    act = (0.5 * pre * (1.0 + curve)).astype(BF)
    slope = 0.5 * (1.0 + curve) + 0.5 * pre * (1.0 - curve * curve) * (GELU_A * (1.0 + 3.0 * GELU_B * square))
    grad_pre = (dot(grad, out_w_ref[...], ((1,), (1,))) * slope).astype(BF)
    total[...] += dot(grad_pre, in_ref[...], ((1,), (1,)))
    if again:
        out_total[...] += dot(act, out_w_ref[...])
    gin_ref[...] = dot(x_ref[...], grad_pre, ((0,), (0,))).astype(BF)
    gout_ref[...] = dot(act, grad, ((0,), (0,))).astype(BF)

    @pl.when(step == pl.num_programs(0) - 1)
    def _():
        gx_ref[...] = total[...].astype(BF)
        if again:
            out_ref[...] = out_total[...].astype(BF)


def expert_back(rows, grads, pre, first_mat, second_mat):
    width, hidden = first_mat.shape
    count, again = rows.shape[0], pre is None
    whole = pl.BlockSpec((count, width), lambda j: (0, 0))
    columns = pl.BlockSpec((width, FF_BLOCK), lambda j: (0, j))
    lines = pl.BlockSpec((FF_BLOCK, width), lambda j: (j, 0))
    row_like = jax.ShapeDtypeStruct(rows.shape, BF)
    return pl.pallas_call(
        functools.partial(expert_back_kernel, again),
        grid=(hidden // FF_BLOCK,),
        out_shape=(row_like,) * (1 + again)
        + (jax.ShapeDtypeStruct(first_mat.shape, BF), jax.ShapeDtypeStruct(second_mat.shape, BF)),
        in_specs=[whole, whole]
        + ([] if again else [pl.BlockSpec((count, FF_BLOCK), lambda j: (0, j))])
        + [columns, lines],
        out_specs=(whole,) * (1 + again) + (columns, lines),
        scratch_shapes=[VMEM((count, width), F32)] * (1 + again),
        cost_estimate=LITTLE,
        compiler_params=pltpu.CompilerParams(vmem_limit_bytes=50 * 2**20),
    )(rows, grads, *(() if again else (pre,)), first_mat, second_mat)


def gather_attn(wqkv, wout, segments, pick):
    layers, shard = wqkv.shape[0], wqkv.shape[1]
    own = jnp.concatenate([wqkv, wout], axis=2).reshape(layers, shard, 2 * SIDE, -1).transpose(2, 0, 1, 3)
    own = jnp.pad(own, ((0, 0), (0, 0), (0, 16 - shard), (0, 0)))
    seg = jnp.broadcast_to(segments.astype(F32), (8, segments.shape[1]))
    full, segs = attn_gather(own, seg, pick)
    return full.reshape(2 * SIDE, layers, D, -1), segs[:, :, 0].reshape(1, -1)


def gather_experts(w_in, w_out, layer_index):
    first = lax.all_gather(w_in[layer_index, 0], "seq", axis=0, tiled=True)
    second = lax.all_gather(w_out[layer_index, 0], "seq", axis=0, tiled=True)
    return first, second


def on_device(
    tokens,
    segments,
    rel_bucket,
    routes,
    gain_attn,
    wqkv,
    wout,
    bucket_bias_table,
    gain_ffn,
    router,
    w_in,
    w_out,
    cotangent,
):
    count_q = tokens.shape[0]
    experts = lax.axis_size("grp")
    blocks = lax.axis_size("seq")
    capacity = max(2, 3 * count_q * TOP // (2 * experts))
    window = (BACK + 1) * count_q
    span = window + count_q
    me = lax.axis_index("seq")
    start = first_key_block() * count_q
    off = (me * count_q - start).astype(jnp.int32)

    place = jnp.arange(span, dtype=jnp.int32)
    distance = off - jnp.where(place < window, place, place - span)
    pick = (distance[:, None] == jnp.arange(rel_bucket.shape[0], dtype=jnp.int32)[None, :]).astype(BF)
    bucket_at = dot(pick, rel_bucket.astype(BF)[:, None])[:, 0].astype(jnp.int32)
    in_range = (distance >= 0) & (distance < rel_bucket.shape[0])
    bucket_hot = (
        (bucket_at[None, :] == jnp.arange(BUCKETS, dtype=jnp.int32)[:, None]) & in_range[None, :]
    ).astype(BF)
    bias_rows = [dot(bucket_bias_table[l], bucket_hot, ((0,), (0,))) for l in range(LAYERS)]

    expert_ids = jnp.arange(experts, dtype=jnp.int32)
    flat_routes = jnp.concatenate([routes[:, 0], routes[:, 1]])
    hot = (flat_routes[:, None] == expert_ids[None, :]).astype(BF)
    number = jnp.arange(TOP * count_q, dtype=jnp.int32)
    ranks = dot((number[:, None] > number[None, :]).astype(BF), hot)
    rank = jnp.sum(ranks * hot.astype(F32), axis=1).astype(jnp.int32)
    target = flat_routes * capacity + rank
    slots = jnp.arange(experts * capacity, dtype=jnp.int32)
    halves = jnp.arange(2 * experts * capacity, dtype=jnp.int32)
    slot, right = halves // (2 * capacity) * capacity + halves % capacity, halves // capacity % 2
    pairs_at, tokens_at, rows_at = [], [], []
    for side in range(2):
        mine = jnp.where(right == side, slot, -1)[:, None]
        pairs_at.append((mine == target[None, :]).astype(BF))
        tokens_at.append(pairs_at[-1][:, :count_q] + pairs_at[-1][:, count_q:])
        rows_at.append((mine == slots[None, :]).astype(BF))
    route_hot = hot.astype(F32).reshape(TOP, count_q, experts)

    seg_own = segments[0].astype(F32)
    seg_col = seg_own[:, None]
    hidden_state = tokens.astype(F32)
    gains_a, gains_f = gain_attn.astype(F32), gain_ffn.astype(F32)
    stored = []
    shard = wqkv.shape[1]
    row = jnp.arange(blocks * shard, dtype=jnp.int32)[:, None]
    pick = (row // shard * 16 + row % shard == jnp.arange(blocks * 16, dtype=jnp.int32)[None, :]).astype(BF)
    attn_full, segs = gather_attn(wqkv, wout, segments, pick)
    seg_keys = lax.dynamic_slice_in_dim(segs, start, window, axis=1)
    w_in, w_out, seg_keys = lax.optimization_barrier((w_in, w_out, seg_keys))
    expert_full = [gather_experts(w_in, w_out, l) for l in range(LAYERS)]
    for l in range(LAYERS):
        first_mat, second_mat = expert_full[l]
        queries, kv_own, normed, scale_one = queries_keys(hidden_state, gains_a[l], attn_full, l)
        kv = gather_keys(kv_own)
        off_arr = off.reshape(1)
        attended, lse = attention(off_arr, queries, kv, seg_col, seg_keys, bias_rows[l])
        middle, mixed_in, scale_two = after_attention(attended, hidden_state, gains_f[l], attn_full, l)
        router_probs = jax.nn.softmax(dot(mixed_in, router[l]), axis=-1)
        gate_values = jnp.sum(router_probs[None] * route_hot, axis=2)
        if l < LAYERS - 1:
            (expert_rows,) = exchange(0, (mixed_in, tokens_at, rows_at, BF))
            expert_out, pre_act = expert_forward(expert_rows, first_mat, second_mat)
            (pair_out,) = exchange(1, (expert_out, rows_at, pairs_at, F32))
            last_grads = None
        else:
            grad_pairs = (gate_values[:, :, None] * cotangent[None]).astype(BF).reshape(-1, D)
            expert_rows, grad_rows = exchange(
                4, (mixed_in, tokens_at, rows_at, BF), (grad_pairs, pairs_at, rows_at, BF)
            )
            expert_out, grad_inputs, *last_grads = expert_back(expert_rows, grad_rows, None, first_mat, second_mat)
            pair_out, grad_mixed = exchange(
                5, (expert_out, rows_at, pairs_at, F32), (grad_inputs, rows_at, tokens_at, F32)
            )
            last_grads = (grad_mixed, *last_grads)
            pre_act = None
        pair_out = pair_out.reshape(TOP, count_q, D)
        new_state = middle + jnp.sum(gate_values[:, :, None] * pair_out, axis=0)
        stored.append(
            (hidden_state, scale_one, normed, queries, kv, lse, attended, middle, scale_two,
             mixed_in, router_probs, gate_values, pair_out, expert_rows, pre_act)
        )
        hidden_state = new_state
    out_tokens = hidden_state.astype(BF)

    grad_state = cotangent
    small = [None] * LAYERS
    attn_grads = [None] * LAYERS
    first_grads = [None] * LAYERS
    second_grads = [None] * LAYERS
    for l in reversed(range(LAYERS)):
        (state_in, scale_one, normed, queries, kv, lse, attended, middle, scale_two,
         mixed_in, router_probs, gate_values, pair_out, expert_rows, pre_act) = stored[l]
        first_mat, second_mat = expert_full[l]
        grad_gates = jnp.sum(grad_state[None] * pair_out, axis=2)
        if l == LAYERS - 1:
            grad_mixed, grad_first, grad_second = last_grads
        else:
            grad_pairs = (gate_values[:, :, None] * grad_state[None]).astype(BF).reshape(-1, D)
            (grad_rows,) = exchange(2, (grad_pairs, pairs_at, rows_at, BF))
            grad_inputs, grad_first, grad_second = expert_back(
                expert_rows, grad_rows, pre_act, first_mat, second_mat
            )
            (grad_mixed,) = exchange(3, (grad_inputs, rows_at, tokens_at, F32))
        first_grads[l] = lax.psum_scatter(grad_first, "seq", scatter_dimension=0, tiled=True)
        second_grads[l] = lax.psum_scatter(grad_second, "seq", scatter_dimension=0, tiled=True)
        grad_probs = jnp.sum(grad_gates[:, :, None] * route_hot, axis=0)
        grad_logits = router_probs * (
            grad_probs - jnp.sum(router_probs * grad_probs, axis=-1, keepdims=True)
        )
        router_grad = jnp.dot(mixed_in.astype(F32).T, grad_logits, precision=highest)
        grad_mixed = grad_mixed + jnp.dot(grad_logits, router[l].astype(F32).T, precision=highest)
        grad_mid, gain_f_grad = norm_backward(middle, scale_two, gains_f[l], grad_mixed)
        grad_mid = grad_mid + grad_state
        branch_grad = grad_mid.astype(BF)
        grad_attended = branch_back(branch_grad, attn_full, l)
        if l < LAYERS - 1:
            grad_attended, first_grads[l + 1], second_grads[l + 1] = lax.optimization_barrier(
                (grad_attended, first_grads[l + 1], second_grads[l + 1])
            )
        dq, dkv, diag = attention_back(
            off_arr, queries, kv, seg_col, seg_keys, bias_rows[l], lse, grad_attended
        )
        table_grad = lax.dot_general(
            bucket_hot.astype(F32), diag, (((1,), (1,)), ((), ())), precision=highest
        )
        dkv_own = scatter_key_grads(dkv)
        grad_proj = jnp.concatenate([dq, dkv_own], axis=1)
        grad_state, gain_a_grad = input_grad(
            grad_proj, attn_full, l, state_in, scale_one, gains_a[l], grad_mid
        )
        attn_grads[l] = weight_grads(normed, attended, grad_proj, branch_grad)
        small[l] = (gain_a_grad, gain_f_grad, router_grad, table_grad)
    sizes = [D, D, D * experts, BUCKETS * HEADS]
    flat = jnp.concatenate([part.reshape(-1) for l in range(LAYERS) for part in small[l]])
    used = flat.size
    padded = -(-used // (3 * 8 * 128)) * 3 * 8 * 128
    whole = [g.reshape(SIDE, 2, SIDE, SIDE, 3, 16, -1) for g in attn_grads]
    attn, flat = reduce_all(*whole, jnp.pad(flat, (0, padded - used)).reshape(3, -1, 128), pick)
    attn = attn[:, :, :shard].astype(F32).transpose(1, 2, 0, 3).reshape(LAYERS, shard, -1)
    flat = flat.reshape(-1)[:used].reshape(LAYERS, -1)
    sums, at = [], 0
    for size in sizes:
        sums.append(flat[:, at : at + size])
        at += size
    return (
        out_tokens,
        grad_state,
        sums[0],
        attn[:, :, : 3 * D],
        attn[:, :, 3 * D :],
        sums[3].reshape(LAYERS, BUCKETS, HEADS),
        sums[1],
        sums[2].reshape(LAYERS, D, experts),
        jnp.stack(first_grads)[:, None].astype(F32),
        jnp.stack(second_grads)[:, None].astype(F32),
    )


def solution(mesh):
    rows = P(("grp", "seq"), None)
    slab = P(None, ("grp", "seq"), None)
    expert = P(None, "grp", "seq", None)
    return jax.shard_map(
        on_device,
        mesh=mesh,
        in_specs=(
            rows, P("grp", "seq"), P(), rows, P(), slab, slab, P(), P(), P(), expert, expert, rows,
        ),
        out_specs=(rows, rows, P(), slab, slab, P(), P(), P(), expert, expert),
        check_vma=False,
    )
```

```python
import functools

import jax
import jax.numpy as jnp
from jax import lax
from jax.experimental import pallas as pl
from jax.experimental.pallas import tpu as pltpu
from jax.sharding import PartitionSpec as P

D = 768
HEADS = 12
HEAD_DIM = 64
PAIRS = HEADS // 2
TOP = 2
BUCKETS = 32
LAYERS = 2
BACK = 4
EPS = 1e-06
MASKED = -1e30
SCALE = HEAD_DIM**-0.5
BF = jnp.bfloat16
F32 = jnp.float32
highest = lax.Precision.HIGHEST
VMEM = pltpu.VMEM
LITTLE = pl.CostEstimate(flops=1024, bytes_accessed=1024, transcendentals=0)


def dot(a, b, contract=((1,), (0,))):
    return lax.dot_general(a, b, (contract, ((), ())), preferred_element_type=F32)


def inv_root(values):
    return lax.rsqrt(jnp.mean(values * values, axis=-1, keepdims=True) + EPS)


def norm_backward(values, scale_rows, gain_row, grad_out):
    scaled = grad_out * gain_row
    grad_gain = jnp.sum(grad_out * values * scale_rows, axis=0)
    cubed = scale_rows * scale_rows * scale_rows
    input_gradient = scale_rows * scaled - values * cubed * jnp.mean(
        values * scaled, axis=-1, keepdims=True
    )
    return (input_gradient, grad_gain)


def head_scores(q2, k2, low_lanes, head, allowed, bias_ref, width, span):
    mine = low_lanes if head % 2 == 0 else jnp.logical_not(low_lanes)
    q_head = jnp.where(mine, q2, jnp.zeros_like(q2))
    scores = dot(q_head, k2, ((1,), (1,))) * SCALE
    row = jnp.broadcast_to(bias_ref[head : head + 1, :], (q2.shape[0], span))
    bias = pltpu.roll(row, 0, 1, stride=1, stride_axis=0)[:, :width]
    return q_head, mine, jnp.where(allowed, scores + bias, MASKED)


def first_key_block():
    me = lax.axis_index("seq")
    return me // BACK * (me % BACK)


def allowed_pairs(off_ref, segq_ref, segk_ref, rows, width):
    i = lax.broadcasted_iota(jnp.int32, (rows, width), 0)
    j = lax.broadcasted_iota(jnp.int32, (rows, width), 1)
    return (off_ref[0] + i - j >= 0) & (segq_ref[...] == segk_ref[...])


def attention_kernel(off_ref, q_ref, kv_ref, segq_ref, segk_ref, bias_ref, out_ref, lse_ref):
    rows, width, span = q_ref.shape[0], segk_ref.shape[1], bias_ref.shape[1]
    first = first_key_block()
    window = pl.ds(pl.multiple_of(first * rows, rows), width)
    allowed = allowed_pairs(off_ref, segq_ref, segk_ref, rows, width)
    low_lanes = lax.broadcasted_iota(jnp.int32, (rows, 128), 1) < HEAD_DIM
    lane = lax.broadcasted_iota(jnp.int32, (rows, 128), 1)
    totals = jnp.zeros((rows, 128), F32)
    for pair in range(PAIRS):
        at = slice(pair * 128, pair * 128 + 128)
        q2, k2 = q_ref[:, at], kv_ref[window, at]
        v2 = kv_ref[window, D + pair * 128 : D + pair * 128 + 128]
        both = []
        for head in (2 * pair, 2 * pair + 1):
            _, _, scores = head_scores(q2, k2, low_lanes, head, allowed, bias_ref, width, span)
            row_max = jnp.max(scores, axis=1, keepdims=True)
            exponent = jnp.exp(scores - row_max)
            row_total = jnp.sum(exponent, axis=1, keepdims=True)
            weights = (exponent / row_total).astype(BF)
            both.append(dot(weights, v2))
            totals = jnp.where(lane == head, row_max + jnp.log(row_total), totals)
        out_ref[:, at] = jnp.where(low_lanes, both[0], both[1]).astype(BF)
    lse_ref[...] = totals


def attention_back_kernel(
    off_ref, q_ref, kv_ref, segq_ref, segk_ref, bias_ref, lse_ref, grad_ref, dq_ref, dkv_ref, diag_ref
):
    rows, width, span = q_ref.shape[0], segk_ref.shape[1], bias_ref.shape[1]
    first = first_key_block()
    window = pl.ds(pl.multiple_of(first * rows, rows), width)
    allowed = allowed_pairs(off_ref, segq_ref, segk_ref, rows, width)
    low_lanes = lax.broadcasted_iota(jnp.int32, (rows, 128), 1) < HEAD_DIM
    lane = lax.broadcasted_iota(jnp.int32, (rows, 128), 1)
    i = lax.broadcasted_iota(jnp.int32, (rows, rows), 0)
    j = lax.broadcasted_iota(jnp.int32, (rows, rows), 1)
    flip = (i + j == rows - 1).astype(BF)
    dkv_ref[...] = jnp.zeros_like(dkv_ref)
    for pair in range(PAIRS):
        at = slice(pair * 128, pair * 128 + 128)
        at_v = slice(D + pair * 128, D + pair * 128 + 128)
        q2, k2, v2, g2 = q_ref[:, at], kv_ref[window, at], kv_ref[window, at_v], grad_ref[:, at]
        dq, dk, dv = [], None, None
        for head in (2 * pair, 2 * pair + 1):
            q_head, mine, scores = head_scores(q2, k2, low_lanes, head, allowed, bias_ref, width, span)
            log_total = jnp.sum(jnp.where(lane == head, lse_ref[...], 0.0), axis=1, keepdims=True)
            probs = jnp.exp(scores - log_total)
            g_head = jnp.where(mine, g2, jnp.zeros_like(g2))
            grad_probs = dot(g_head, v2, ((1,), (1,)))
            inner = jnp.sum(probs * grad_probs, axis=1, keepdims=True)
            grad_scores = (probs * (grad_probs - inner)).astype(BF)
            dq.append(dot(grad_scores, k2))
            dk_head = dot(grad_scores, q_head, ((0,), (0,)))
            dv_head = dot(probs.astype(BF), g_head, ((0,), (0,)))
            dk = dk_head if dk is None else dk + dk_head
            dv = dv_head if dv is None else dv + dv_head
            turned = jnp.concatenate(
                [dot(flip, grad_scores), jnp.zeros((rows, span - width), F32)], axis=1
            )
            turned = pltpu.roll(turned, span - (rows - 1), 1, stride=1, stride_axis=0)
            diag_ref[head : head + 1, :] = jnp.sum(turned, axis=0, keepdims=True)
        dq_ref[:, at] = (jnp.where(low_lanes, dq[0], dq[1]) * SCALE).astype(BF)
        blocks = pl.ds(first, width // rows)
        dkv_ref[blocks, :, at] = (dk * SCALE).astype(BF).reshape(-1, rows, 128)
        dkv_ref[blocks, :, at_v] = dv.astype(BF).reshape(-1, rows, 128)


def vmem_specs(n):
    return [pl.BlockSpec(memory_space=VMEM) for _ in range(n)]


def attention(off, queries, kv, segq, segk, bias):
    return pl.pallas_call(
        attention_kernel,
        out_shape=(
            jax.ShapeDtypeStruct(queries.shape, BF),
            jax.ShapeDtypeStruct((queries.shape[0], 128), F32),
        ),
        in_specs=[pl.BlockSpec(memory_space=pltpu.SMEM)] + vmem_specs(5),
        out_specs=tuple(vmem_specs(2)),
        cost_estimate=LITTLE,
        compiler_params=pltpu.CompilerParams(vmem_limit_bytes=32 * 2**20),
    )(off, queries, kv, segq, segk, bias)


def attention_back(off, queries, kv, segq, segk, bias, lse, grad):
    return pl.pallas_call(
        attention_back_kernel,
        out_shape=(
            jax.ShapeDtypeStruct(queries.shape, BF),
            jax.ShapeDtypeStruct((kv.shape[0] // queries.shape[0], queries.shape[0], kv.shape[1]), BF),
            jax.ShapeDtypeStruct(bias.shape, F32),
        ),
        in_specs=[pl.BlockSpec(memory_space=pltpu.SMEM)] + vmem_specs(7),
        out_specs=tuple(vmem_specs(3)),
        cost_estimate=LITTLE,
        compiler_params=pltpu.CompilerParams(vmem_limit_bytes=32 * 2**20),
    )(off, queries, kv, segq, segk, bias, lse, grad)


MESH_ID = pl.DeviceIdType.MESH
QKV_BLOCKS = 6
SIDE = 4


def place_of_device():
    grp, seq = lax.axis_index("grp"), lax.axis_index("seq")
    return [grp // SIDE, grp % SIDE, seq // 2], seq % 2


def device_at(coords, core):
    return (coords[0] * SIDE + coords[1], coords[2] * 2 + core)


def moved(coords, axis, delta):
    return [(c + delta) % SIDE if a == axis else c for a, c in enumerate(coords)]


def remote(src, dst, send_sem, recv_sem, device):
    return pltpu.make_async_remote_copy(
        src_ref=src, dst_ref=dst, send_sem=send_sem, recv_sem=recv_sem, device_id=device, device_id_type=MESH_ID
    )


def greet(devices):
    barrier = pltpu.get_barrier_semaphore()
    for device in devices:
        pl.semaphore_signal(barrier, inc=1, device_id=device, device_id_type=MESH_ID)
    pl.semaphore_wait(barrier, len(devices))


def sequence_partners(coords, core):
    seq = coords[2] * 2 + core
    others = [(seq + d) % (2 * SIDE) for d in range(1, 2 * SIDE)]
    return [(coords[0] * SIDE + coords[1], s) for s in others], others


def all_partners(coords, core):
    partners = [device_at(moved(coords, a, d), core) for a in range(2) for d in range(1, SIDE)]
    return partners + sequence_partners(coords, core)[0]


def attn_gather_kernel(
    own_ref, seg_ref, pick_ref, full_ref, segs_ref, rows_ref,
    row_send, row_recv, send_sem, recv_sem, core_send, core_recv, seg_send, seg_recv,
):
    coords, core = place_of_device()
    sibling = device_at(coords, 1 - core)
    y, x, z = coords
    seq = z * 2 + core
    greet(all_partners(coords, core))
    rows_ref[seq] = own_ref[seq]
    segs_ref[z, core] = seg_ref[...]
    devices, numbers = sequence_partners(coords, core)
    row_copies = []
    for n, (device, s) in enumerate(zip(devices, numbers)):
        row_copies.append(remote(own_ref.at[s], rows_ref.at[seq], row_send.at[n], row_recv.at[n], device))
        row_copies[-1].start()
    seg_copies = []
    for d in range(1, SIDE):
        one = segs_ref.at[z, core]
        seg_copies.append(remote(one, one, seg_send.at[d - 1], seg_recv.at[d - 1], device_at(moved(coords, 2, d), core)))
        seg_copies[-1].start()
    for copy in row_copies:
        copy.wait()
    for l in range(LAYERS):
        flat = rows_ref[:, l].reshape(-1, own_ref.shape[-1])
        block = dot(pick_ref[...], flat).astype(BF)
        for p in range(3):
            full_ref[z, core, l, y, x, p] = block[16 * p : 16 * p + 16]

    def region(p, free, fixed=None):
        at = [slice(None) if a in free else coords[a] for a in range(3)]
        if fixed is not None:
            at[fixed[0]] = fixed[1]
        return full_ref.at[at[2], core, :, at[0], at[1], p]

    copies = {}
    core_copies = []

    def to_sibling(part, number):
        core_copies.append(remote(part, part, core_send.at[number], core_recv.at[number], sibling))
        core_copies[-1].start()

    for k in range(3):
        for p in range(3):
            if k:
                for d in (1, 3, 2):
                    copies[k - 1, p, d].wait_recv()
            axis, free = (p + k) % 3, [(p + i) % 3 for i in range(k)]
            part = region(p, free)
            for d in (1, 3, 2):
                copies[k, p, d] = remote(
                    part, part, send_sem.at[k, p, d - 1], recv_sem.at[k, p, d - 1],
                    device_at(moved(coords, axis, d), core),
                )
                copies[k, p, d].start()
            if k == 2:
                to_sibling(part, 4 * p)
    for copy in seg_copies:
        copy.wait_recv()
    part = segs_ref.at[:, core]
    seg_last = remote(part, part, seg_send.at[3], seg_recv.at[3], sibling)
    seg_last.start()
    for d in (1, 3, 2):
        for p in range(3):
            axis = (p + 2) % 3
            copies[2, p, d].wait_recv()
            came = (coords[axis] + SIDE - d) % SIDE
            to_sibling(region(p, [a for a in range(3) if a != axis], (axis, came)), 4 * p + d)
    for copy in copies.values():
        copy.wait_send()
    for copy in seg_copies:
        copy.wait_send()
    seg_last.wait()
    for copy in core_copies:
        copy.wait()


def attn_gather(own, seg, pick):
    dma = pltpu.SemaphoreType.DMA
    width = own.shape[-1]
    return pl.pallas_call(
        attn_gather_kernel,
        out_shape=(
            jax.ShapeDtypeStruct((SIDE, 2, LAYERS, SIDE, SIDE, 3, 16, width), BF),
            jax.ShapeDtypeStruct((SIDE, 2) + seg.shape, F32),
        ),
        in_specs=vmem_specs(3),
        out_specs=tuple(vmem_specs(2)),
        scratch_shapes=[VMEM(own.shape, BF), dma((7,)), dma((7,)), dma((3, 3, 3)), dma((3, 3, 3)),
                        dma((12,)), dma((12,)), dma((4,)), dma((4,))],
        cost_estimate=LITTLE,
        compiler_params=pltpu.CompilerParams(
            collective_id=0, has_side_effects=True, vmem_limit_bytes=40 * 2**20
        ),
    )(own, seg, pick)


def reduce_kernel(
    x0_ref, x1_ref, small_ref, pick_ref, out_ref, small_out, got_core, y_ref, got_one, z_ref, got_two, w_ref, got_three,
    rows_ref, s_core, s_got, core_send, core_recv, send_sem, recv_sem, s_core_send, s_core_recv, s_send, s_recv,
    row_send, row_recv,
):
    coords, core = place_of_device()
    sibling = device_at(coords, 1 - core)
    greet(all_partners(coords, core))
    x_refs = (x0_ref, x1_ref)
    order = (2, 0, 1)
    first = {}
    for p in range(3):
        for l in range(LAYERS):
            first[p, l] = remote(
                x_refs[l].at[:, 1 - core, :, :, p], got_core.at[p, l], core_send.at[p, l], core_recv.at[p, l], sibling
            )
            first[p, l].start()
    s_first = remote(small_ref, s_core, s_core_send, s_core_recv, sibling)
    s_first.start()

    def axes_left(p, k):
        gone = [(p + i) % 3 for i in range(k)]
        return [a for a in order if a not in gone]

    def spread(p, k, source, target):
        axis, out = (p + k) % 3, []
        for d in (1, 3, 2):
            to = moved(coords, axis, d)
            index = tuple(to[axis] if a == axis else slice(None) for a in axes_left(p, k))
            copy = remote(
                source.at[(p, *index)], target.at[p, d - 1], send_sem.at[k, p, d - 1], recv_sem.at[k, p, d - 1],
                device_at(to, core),
            )
            copy.start()
            out.append(copy)
        return out

    def spread_small(p, k):
        axis, out = (p + k) % 3, []
        for d in (1, 3, 2):
            copy = remote(
                s_got.at[k, p, 0], s_got.at[k, p, d], s_send.at[k, p, d - 1], s_recv.at[k, p, d - 1],
                device_at(moved(coords, axis, d), core),
            )
            copy.start()
            out.append(copy)
        return out

    def small_sum(p, k):
        axis = (p + k) % 3
        total = s_got[k, p, coords[axis]]
        for v in range(1, SIDE):
            total = total + s_got[k, p, (coords[axis] + SIDE - v) % SIDE]
        return total

    sent, s_sent = {}, {}
    s_first.wait()
    for p in range(3):
        s_got[0, p, 0] = small_ref[p] + s_core[p]
        s_sent[0, p] = spread_small(p, 0)
    for p in range(3):
        for l in range(LAYERS):
            first[p, l].wait()

        def add_core(i, carry, p=p):
            a, b, c = i // (SIDE * SIDE), i // SIDE % SIDE, i % SIDE
            for l in range(LAYERS):
                total = x_refs[l][a, core, b, c, p].astype(F32) + got_core[p, l, a, b, c].astype(F32)
                y_ref[p, a, b, c, l] = total.astype(BF)
            return carry

        lax.fori_loop(0, SIDE**3, add_core, 0)
        sent[0, p] = spread(p, 0, y_ref, got_one)
    for p in range(3):
        for copy in s_sent[0, p]:
            copy.wait()
        s_got[1, p, 0] = small_sum(p, 0)
        s_sent[1, p] = spread_small(p, 1)
    for p in range(3):
        for copy in sent[0, p]:
            copy.wait()
        at = order.index(p)

        def add_one(i, carry, p=p, at=at):
            a, b = i // SIDE, i % SIDE
            index = [a, b]
            index.insert(at, coords[p])
            total = y_ref[(p, *index)].astype(F32)
            for d in range(3):
                total = total + got_one[p, d, a, b].astype(F32)
            z_ref[p, a, b] = total.astype(BF)
            return carry

        lax.fori_loop(0, SIDE**2, add_one, 0)
        sent[1, p] = spread(p, 1, z_ref, got_two)
    for p in range(3):
        for copy in s_sent[1, p]:
            copy.wait()
        s_got[2, p, 0] = small_sum(p, 1)
        s_sent[2, p] = spread_small(p, 2)
    for p in range(3):
        for copy in sent[1, p]:
            copy.wait()
        axis = (p + 1) % 3

        def add_two(i, carry, p=p, axis=axis):
            index = tuple(coords[axis] if a == axis else i for a in axes_left(p, 1))
            total = z_ref[(p, *index)].astype(F32)
            for d in range(3):
                total = total + got_two[p, d, i].astype(F32)
            w_ref[p, i] = total.astype(BF)
            return carry

        lax.fori_loop(0, SIDE, add_two, 0)
        sent[2, p] = spread(p, 2, w_ref, got_three)
    for p in range(3):
        for copy in s_sent[2, p]:
            copy.wait()
        small_out[p] = small_sum(p, 2)
    blocks = []
    for p in range(3):
        for copy in sent[2, p]:
            copy.wait()
        total = w_ref[p, coords[(p + 2) % 3]].astype(F32)
        for d in range(3):
            total = total + got_three[p, d].astype(F32)
        blocks.append(total.astype(BF))
    for l in range(LAYERS):
        block = jnp.concatenate([part[l] for part in blocks], axis=0)
        spread_rows = dot(pick_ref[...], block, ((0,), (0,))).astype(BF)
        rows_ref[:, l] = spread_rows.reshape(2 * SIDE, 16, -1)
    seq = coords[2] * 2 + core
    out_ref[seq] = rows_ref[seq]
    devices, numbers = sequence_partners(coords, core)
    last = []
    for n, (device, s) in enumerate(zip(devices, numbers)):
        last.append(remote(rows_ref.at[s], out_ref.at[seq], row_send.at[n], row_recv.at[n], device))
        last[-1].start()
    for copy in last:
        copy.wait()


def reduce_all(x0, x1, small, pick):
    width, part = x0.shape[-1], small.shape[1:]
    block = (LAYERS, 16, width)
    rows = (2 * SIDE, LAYERS, 16, width)
    dma = pltpu.SemaphoreType.DMA
    return pl.pallas_call(
        reduce_kernel,
        out_shape=(jax.ShapeDtypeStruct(rows, BF), jax.ShapeDtypeStruct(small.shape, F32)),
        in_specs=vmem_specs(4),
        out_specs=tuple(vmem_specs(2)),
        scratch_shapes=[
            VMEM((3, LAYERS, SIDE, SIDE, SIDE, 16, width), BF),
            VMEM((3, SIDE, SIDE, SIDE) + block, BF),
            VMEM((3, 3, SIDE, SIDE) + block, BF),
            VMEM((3, SIDE, SIDE) + block, BF),
            VMEM((3, 3, SIDE) + block, BF),
            VMEM((3, SIDE) + block, BF),
            VMEM((3, 3) + block, BF),
            VMEM(rows, BF),
            VMEM(small.shape, F32),
            VMEM((3, 3, SIDE) + part, F32),
            dma((3, LAYERS)), dma((3, LAYERS)), dma((3, 3, 3)), dma((3, 3, 3)), dma(()), dma(()),
            dma((3, 3, 3)), dma((3, 3, 3)), dma((7,)), dma((7,)),
        ],
        cost_estimate=LITTLE,
        compiler_params=pltpu.CompilerParams(
            collective_id=1, has_side_effects=True, vmem_limit_bytes=50 * 2**20
        ),
    )(x0, x1, small, pick)


def scaled_rows(values, gain_row):
    scale = inv_root(values)
    return scale, (values * scale * gain_row).astype(BF)


def queries_keys_kernel(x_ref, gain_ref, w_ref, q_ref, kv_ref, normed_ref, scale_ref):
    width, some = w_ref.shape[3], w_ref.shape[0]

    @pl.when(pl.program_id(0) == 0)
    def _():
        scale_ref[...], normed_ref[...] = scaled_rows(x_ref[...], gain_ref[...])
        for s in range(2):
            q_ref[:, s * width : (s + 1) * width] = dot(normed_ref[...], w_ref[s, 0]).astype(BF)
        kv_ref[:, :width] = dot(normed_ref[...], w_ref[2, 0]).astype(BF)

    @pl.when(pl.program_id(0) == 1)
    def _():
        for s in range(some):
            kv_ref[:, (s + 1) * width : (s + 2) * width] = dot(normed_ref[...], w_ref[s, 0]).astype(BF)


def queries_keys(x, gain, full, layer):
    depth, width = full.shape[2:]
    rows = x.shape[0]

    def whole(columns):
        return pl.BlockSpec((rows, columns), lambda s: (0, 0))

    return pl.pallas_call(
        queries_keys_kernel,
        grid=(2,),
        out_shape=(
            jax.ShapeDtypeStruct((rows, D), BF),
            jax.ShapeDtypeStruct((rows, 2 * D), BF),
            jax.ShapeDtypeStruct((rows, D), BF),
            jax.ShapeDtypeStruct((rows, 1), F32),
        ),
        in_specs=[
            whole(D),
            pl.BlockSpec((1, D), lambda s: (0, 0)),
            pl.BlockSpec((QKV_BLOCKS // 2, 1, depth, width), lambda s: (s, layer, 0, 0)),
        ],
        out_specs=(whole(D), whole(2 * D), whole(D), whole(1)),
        cost_estimate=LITTLE,
        compiler_params=pltpu.CompilerParams(vmem_limit_bytes=56 * 2**20),
    )(x, gain[None], full)


def after_attention_kernel(attended_ref, x_ref, gain_ref, w_ref, middle_ref, mixed_ref, scale_ref):
    width = w_ref.shape[3]
    for s in range(w_ref.shape[0]):
        at = slice(s * width, (s + 1) * width)
        middle_ref[:, at] = x_ref[:, at] + dot(attended_ref[...], w_ref[s, 0])
    scale_ref[...], mixed_ref[...] = scaled_rows(middle_ref[...], gain_ref[...])


def after_attention(attended, x, gain, full, layer):
    depth, width = full.shape[2:]
    rows = x.shape[0]
    whole = pl.BlockSpec((rows, D), lambda s: (0, 0))
    return pl.pallas_call(
        after_attention_kernel,
        grid=(1,),
        out_shape=(
            jax.ShapeDtypeStruct((rows, D), F32),
            jax.ShapeDtypeStruct((rows, D), BF),
            jax.ShapeDtypeStruct((rows, 1), F32),
        ),
        in_specs=[
            whole,
            whole,
            pl.BlockSpec((1, D), lambda s: (0, 0)),
            pl.BlockSpec((2, 1, depth, width), lambda s: (QKV_BLOCKS // 2, layer, 0, 0)),
        ],
        out_specs=(whole, whole, pl.BlockSpec((rows, 1), lambda s: (0, 0))),
        cost_estimate=LITTLE,
        compiler_params=pltpu.CompilerParams(vmem_limit_bytes=56 * 2**20),
    )(attended, x, gain[None], full)


def branch_back_kernel(x_ref, w_ref, out_ref):
    width = w_ref.shape[3]
    total = dot(x_ref[:, :width], w_ref[0, 0], ((1,), (1,)))
    out_ref[...] = (total + dot(x_ref[:, width:], w_ref[1, 0], ((1,), (1,)))).astype(BF)


def branch_back(x, full, layer):
    depth, width = full.shape[2:]
    whole = pl.BlockSpec(x.shape, lambda s: (0, 0))
    return pl.pallas_call(
        branch_back_kernel,
        grid=(1,),
        out_shape=jax.ShapeDtypeStruct(x.shape, BF),
        in_specs=[
            whole,
            pl.BlockSpec((2, 1, depth, width), lambda s: (QKV_BLOCKS // 2, layer, 0, 0)),
        ],
        out_specs=whole,
        cost_estimate=LITTLE,
        compiler_params=pltpu.CompilerParams(vmem_limit_bytes=56 * 2**20),
    )(x, full)


def input_grad_kernel(grad_ref, w_ref, x_ref, scale_ref, gain_ref, mid_ref, out_ref, gain_out, total):
    @pl.when(pl.program_id(0) == 0)
    def _():
        total[...] = jnp.zeros_like(total)

    width = w_ref.shape[3]
    for s in range(w_ref.shape[0]):
        total[...] += dot(grad_ref[:, s * width : (s + 1) * width], w_ref[s, 0], ((1,), (1,)))

    @pl.when(pl.program_id(0) == pl.num_programs(0) - 1)
    def _():
        grad, gain_grad = norm_backward(x_ref[...], scale_ref[...], gain_ref[...], total[...])
        out_ref[...] = mid_ref[...] + grad
        gain_out[...] = gain_grad[None]


def input_grad(grad_proj, full, layer, x, scale, gain, grad_mid):
    depth, width = full.shape[2:]
    rows = x.shape[0]
    some = QKV_BLOCKS // 2
    whole = pl.BlockSpec((rows, D), lambda s: (0, 0))
    line = pl.BlockSpec((1, D), lambda s: (0, 0))
    return pl.pallas_call(
        input_grad_kernel,
        grid=(2,),
        out_shape=(jax.ShapeDtypeStruct((rows, D), F32), jax.ShapeDtypeStruct((1, D), F32)),
        in_specs=[
            pl.BlockSpec((rows, some * width), lambda s: (0, s)),
            pl.BlockSpec((some, 1, depth, width), lambda s: (s, layer, 0, 0)),
            whole,
            pl.BlockSpec((rows, 1), lambda s: (0, 0)),
            line,
            whole,
        ],
        out_specs=(whole, line),
        scratch_shapes=[VMEM((rows, D), F32)],
        cost_estimate=LITTLE,
        compiler_params=pltpu.CompilerParams(vmem_limit_bytes=56 * 2**20),
    )(grad_proj, full, x, scale, gain[None], grad_mid)


def weight_grad_kernel(normed_ref, attended_ref, proj_ref, branch_ref, out_ref):
    step, width = pl.program_id(0), out_ref.shape[2]

    def fill(left, right):
        for s in range(out_ref.shape[0]):
            out_ref[s] = dot(left[...], right[:, s * width : (s + 1) * width], ((0,), (0,))).astype(BF)

    @pl.when(step < QKV_BLOCKS // 2)
    def _():
        fill(normed_ref, proj_ref)

    @pl.when(step >= QKV_BLOCKS // 2)
    def _():
        fill(attended_ref, branch_ref)


def weight_grads(normed, attended, grad_proj, branch_grad):
    rows, width = normed.shape[0], grad_proj.shape[1] // QKV_BLOCKS
    last = QKV_BLOCKS // 2 - 1
    return pl.pallas_call(
        weight_grad_kernel,
        grid=(SIDE,),
        out_shape=jax.ShapeDtypeStruct((2 * SIDE, D, width), BF),
        in_specs=[
            pl.BlockSpec((rows, D), lambda s: (0, 0)),
            pl.BlockSpec((rows, D), lambda s: (0, 0)),
            pl.BlockSpec((rows, 2 * width), lambda s: (0, jnp.minimum(s, last))),
            pl.BlockSpec((rows, 2 * width), lambda s: (0, 0)),
        ],
        out_specs=pl.BlockSpec((2, D, width), lambda s: (s, 0, 0)),
        cost_estimate=LITTLE,
        compiler_params=pltpu.CompilerParams(vmem_limit_bytes=56 * 2**20),
    )(normed, attended, grad_proj, branch_grad)


def kv_gather(own_ref, kv_ref, send_sem, recv_sem):
    coords, core = place_of_device()
    z, rows = coords[2], own_ref.shape[0]
    half = rows // 2
    up, down = moved(coords, 2, 1), moved(coords, 2, 3)
    up_z, down_z, far_z = (z + 1) % SIDE, (z + 3) % SIDE, (z + 2) % SIDE
    sibling = device_at(coords, 1 - core)

    def block(at, start=0, size=rows):
        return kv_ref.at[pl.ds(pl.multiple_of((at * 2 + core) * rows + start, half), size)]

    copies = []

    def send(part, number, device):
        copy = remote(part, part, send_sem.at[number], recv_sem.at[number], device)
        copy.start()
        copies.append(copy)
        return copy

    kv_ref[pl.ds(pl.multiple_of((z * 2 + core) * rows, rows), rows), :] = own_ref[...]
    greet([device_at(up, core), device_at(down, core), sibling])
    went_up = send(block(z), 0, device_at(up, core))
    went_down = send(block(z), 1, device_at(down, core))
    from_core = [send(block(z), 2, sibling)]
    went_up.wait_recv()
    far_up = send(block(down_z, 0, half), 3, device_at(up, core))
    from_core.append(send(block(down_z), 4, sibling))
    went_down.wait_recv()
    far_down = send(block(up_z, half, half), 5, device_at(down, core))
    from_core.append(send(block(up_z), 6, sibling))
    far_up.wait_recv()
    from_core.append(send(block(far_z, 0, half), 7, sibling))
    far_down.wait_recv()
    from_core.append(send(block(far_z, half, half), 8, sibling))
    for copy in from_core:
        copy.wait_recv()
    for copy in copies:
        copy.wait_send()


def kv_scatter(grads_ref, out_ref, got_core, sums, got_far, got_up, got_near, send_sem, recv_sem):
    coords, core = place_of_device()
    z, rows = coords[2], out_ref.shape[0]
    half = rows // 2
    up, down = device_at(moved(coords, 2, 1), core), device_at(moved(coords, 2, 3), core)
    down_z, far_z = (z + 3) % SIDE, (z + 2) % SIDE
    sibling = device_at(coords, 1 - core)
    greet([up, down, sibling])
    copies = []

    def send(src, dst, number, device):
        copy = remote(src, dst, send_sem.at[number], recv_sem.at[number], device)
        copy.start()
        copies.append(copy)
        return copy

    order = [far_z, down_z, z]
    cross = [send(grads_ref.at[at * 2 + 1 - core], got_core.at[n], n, sibling) for n, at in enumerate(order)]

    def total(n):
        cross[n].wait_recv()
        return grads_ref[order[n] * 2 + core].astype(F32) + got_core[n].astype(F32)

    sums[0] = total(0).astype(BF)
    far_up = send(sums.at[0, pl.ds(0, half)], got_far.at[0], 4, up)
    far_down = send(sums.at[0, pl.ds(half, half)], got_far.at[1], 5, down)
    down_sum = total(1)
    sums[1, :half] = down_sum[:half].astype(BF)
    far_up.wait_recv()
    near_up = send(got_far.at[0], got_up, 6, up)
    far_down.wait_recv()
    sums[1, half:] = (down_sum[half:] + got_far[1].astype(F32)).astype(BF)
    near_down = send(sums.at[1], got_near, 7, down)
    own = total(2)
    near_up.wait_recv()
    near_down.wait_recv()
    near = got_near[...].astype(F32)
    out_ref[:half] = (own[:half] + got_up[...].astype(F32) + near[:half]).astype(BF)
    out_ref[half:] = (own[half:] + near[half:]).astype(BF)
    for copy in copies:
        copy.wait_send()

def gather_keys(own):
    return pl.pallas_call(
        kv_gather,
        out_shape=jax.ShapeDtypeStruct((2 * SIDE * own.shape[0], own.shape[1]), BF),
        in_specs=vmem_specs(1),
        out_specs=vmem_specs(1)[0],
        scratch_shapes=[pltpu.SemaphoreType.DMA((9,))] * 2,
        cost_estimate=LITTLE,
        compiler_params=pltpu.CompilerParams(
            collective_id=2, has_side_effects=True, vmem_limit_bytes=20 * 2**20
        ),
    )(own)


def scatter_key_grads(grads):
    block = grads.shape[1:]
    return pl.pallas_call(
        kv_scatter,
        out_shape=jax.ShapeDtypeStruct(block, BF),
        in_specs=vmem_specs(1),
        out_specs=vmem_specs(1)[0],
        scratch_shapes=[
            VMEM((3,) + block, BF),
            VMEM((2,) + block, BF),
            VMEM((2, block[0] // 2, block[1]), BF),
            VMEM((block[0] // 2, block[1]), BF),
            VMEM(block, BF),
            pltpu.SemaphoreType.DMA((8,)),
            pltpu.SemaphoreType.DMA((8,)),
        ],
        cost_estimate=LITTLE,
        compiler_params=pltpu.CompilerParams(
            collective_id=3, has_side_effects=True, vmem_limit_bytes=20 * 2**20
        ),
    )(grads)


def exchange_kernel(n, *refs):
    loads, outs = refs[: 5 * n], refs[5 * n : 6 * n]
    to_send, got, send_sem, recv_sem = refs[6 * n :]
    grp, seq = lax.axis_index("grp"), lax.axis_index("seq")
    peers, half = got.shape[1], got.shape[3]
    others = [(grp + d) % peers for d in range(1, peers)]
    greet([(other, seq) for other in others])
    for i in range(n):
        x_ref, put_left, put_right = loads[5 * i : 5 * i + 3]
        rows = dot(put_left[...], x_ref[:, :half]) + dot(put_right[...], x_ref[:, half:])
        to_send[i] = rows.astype(BF).reshape(to_send.shape[1:])
    copies = []
    for k, other in enumerate(others):
        copies.append(
            remote(to_send.at[:, other], got.at[:, grp], send_sem.at[k], recv_sem.at[k], (other, seq))
        )
        copies[-1].start()
    got[:, grp] = to_send[:, grp]
    for copy in copies:
        copy.wait()
    for i in range(n):
        take_left, take_right = loads[5 * i + 3 : 5 * i + 5]
        came = got[i].reshape(-1, half)
        outs[i][:, :half] = dot(take_left[...], came, ((0,), (0,))).astype(outs[i].dtype)
        outs[i][:, half:] = dot(take_right[...], came, ((0,), (0,))).astype(outs[i].dtype)


def exchange(number, *loads):
    peers, n = lax.axis_size("grp"), len(loads)
    x, put = loads[0][:2]
    slots = (n, peers, put[0].shape[0] // peers, x.shape[1] // 2)
    dma = pltpu.SemaphoreType.DMA
    return pl.pallas_call(
        functools.partial(exchange_kernel, n),
        out_shape=tuple(
            jax.ShapeDtypeStruct((take[0].shape[1], x.shape[1]), dtype) for x, _, take, dtype in loads
        ),
        in_specs=vmem_specs(5 * n),
        out_specs=tuple(vmem_specs(n)),
        scratch_shapes=[VMEM(slots, BF), VMEM(slots, BF), dma((peers - 1,)), dma((peers - 1,))],
        cost_estimate=LITTLE,
        compiler_params=pltpu.CompilerParams(
            collective_id=4 + number, has_side_effects=True, vmem_limit_bytes=24 * 2**20
        ),
    )(*[part for x, put, take, _ in loads for part in (x, *put, *take)])


FF_BLOCK = 1024
GELU_A, GELU_B = 0.7978845608028654, 0.044715


def expert_kernel(x_ref, in_ref, out_w_ref, out_ref, pre_ref, total):
    step = pl.program_id(0)

    @pl.when(step == 0)
    def _():
        total[...] = jnp.zeros_like(total)

    pre = dot(x_ref[...], in_ref[...])
    pre_ref[...] = pre
    act = 0.5 * pre * (1.0 + jnp.tanh(GELU_A * (pre + GELU_B * pre * pre * pre)))
    total[...] += dot(act.astype(BF), out_w_ref[...])

    @pl.when(step == pl.num_programs(0) - 1)
    def _():
        out_ref[...] = total[...].astype(BF)


def expert_forward(rows, first_mat, second_mat):
    width, hidden = first_mat.shape
    count = rows.shape[0]
    return pl.pallas_call(
        expert_kernel,
        grid=(hidden // FF_BLOCK,),
        out_shape=(jax.ShapeDtypeStruct(rows.shape, BF), jax.ShapeDtypeStruct((count, hidden), F32)),
        in_specs=[
            pl.BlockSpec((count, width), lambda j: (0, 0)),
            pl.BlockSpec((width, FF_BLOCK), lambda j: (0, j)),
            pl.BlockSpec((FF_BLOCK, width), lambda j: (j, 0)),
        ],
        out_specs=(
            pl.BlockSpec((count, width), lambda j: (0, 0)),
            pl.BlockSpec((count, FF_BLOCK), lambda j: (0, j)),
        ),
        scratch_shapes=[VMEM((count, width), F32)],
        cost_estimate=LITTLE,
        compiler_params=pltpu.CompilerParams(vmem_limit_bytes=50 * 2**20),
    )(rows, first_mat, second_mat)


def expert_back_kernel(again, x_ref, grad_ref, *refs):
    pre_ref, in_ref, out_w_ref, out_ref, gx_ref, gin_ref, gout_ref, total, out_total = (
        (None, *refs) if again else (*refs[:3], None, *refs[3:], None)
    )
    step = pl.program_id(0)

    @pl.when(step == 0)
    def _():
        total[...] = jnp.zeros_like(total)
        if again:
            out_total[...] = jnp.zeros_like(out_total)

    pre = dot(x_ref[...], in_ref[...]) if again else pre_ref[...]
    grad = grad_ref[...]
    square = pre * pre
    curve = jnp.tanh(GELU_A * (pre + GELU_B * pre * square))
    act = (0.5 * pre * (1.0 + curve)).astype(BF)
    slope = 0.5 * (1.0 + curve) + 0.5 * pre * (1.0 - curve * curve) * (GELU_A * (1.0 + 3.0 * GELU_B * square))
    grad_pre = (dot(grad, out_w_ref[...], ((1,), (1,))) * slope).astype(BF)
    total[...] += dot(grad_pre, in_ref[...], ((1,), (1,)))
    if again:
        out_total[...] += dot(act, out_w_ref[...])
    gin_ref[...] = dot(x_ref[...], grad_pre, ((0,), (0,))).astype(BF)
    gout_ref[...] = dot(act, grad, ((0,), (0,))).astype(BF)

    @pl.when(step == pl.num_programs(0) - 1)
    def _():
        gx_ref[...] = total[...].astype(BF)
        if again:
            out_ref[...] = out_total[...].astype(BF)


def expert_back(rows, grads, pre, first_mat, second_mat):
    width, hidden = first_mat.shape
    count, again = rows.shape[0], pre is None
    whole = pl.BlockSpec((count, width), lambda j: (0, 0))
    columns = pl.BlockSpec((width, FF_BLOCK), lambda j: (0, j))
    lines = pl.BlockSpec((FF_BLOCK, width), lambda j: (j, 0))
    row_like = jax.ShapeDtypeStruct(rows.shape, BF)
    return pl.pallas_call(
        functools.partial(expert_back_kernel, again),
        grid=(hidden // FF_BLOCK,),
        out_shape=(row_like,) * (1 + again)
        + (jax.ShapeDtypeStruct(first_mat.shape, BF), jax.ShapeDtypeStruct(second_mat.shape, BF)),
        in_specs=[whole, whole]
        + ([] if again else [pl.BlockSpec((count, FF_BLOCK), lambda j: (0, j))])
        + [columns, lines],
        out_specs=(whole,) * (1 + again) + (columns, lines),
        scratch_shapes=[VMEM((count, width), F32)] * (1 + again),
        cost_estimate=LITTLE,
        compiler_params=pltpu.CompilerParams(vmem_limit_bytes=50 * 2**20),
    )(rows, grads, *(() if again else (pre,)), first_mat, second_mat)


def gather_attn(wqkv, wout, segments, pick):
    layers, shard = wqkv.shape[0], wqkv.shape[1]
    own = jnp.concatenate([wqkv, wout], axis=2).reshape(layers, shard, 2 * SIDE, -1).transpose(2, 0, 1, 3)
    own = jnp.pad(own, ((0, 0), (0, 0), (0, 16 - shard), (0, 0)))
    seg = jnp.broadcast_to(segments.astype(F32), (8, segments.shape[1]))
    full, segs = attn_gather(own, seg, pick)
    return full.reshape(2 * SIDE, layers, D, -1), segs[:, :, 0].reshape(1, -1)


def gather_experts(w_in, w_out, layer_index):
    first = lax.all_gather(w_in[layer_index, 0], "seq", axis=0, tiled=True)
    second = lax.all_gather(w_out[layer_index, 0], "seq", axis=0, tiled=True)
    return first, second


def on_device(
    tokens,
    segments,
    rel_bucket,
    routes,
    gain_attn,
    wqkv,
    wout,
    bucket_bias_table,
    gain_ffn,
    router,
    w_in,
    w_out,
    cotangent,
):
    count_q = tokens.shape[0]
    experts = lax.axis_size("grp")
    blocks = lax.axis_size("seq")
    capacity = max(2, 3 * count_q * TOP // (2 * experts))
    window = (BACK + 1) * count_q
    span = window + count_q
    me = lax.axis_index("seq")
    start = first_key_block() * count_q
    off = (me * count_q - start).astype(jnp.int32)

    place = jnp.arange(span, dtype=jnp.int32)
    distance = off - jnp.where(place < window, place, place - span)
    pick = (distance[:, None] == jnp.arange(rel_bucket.shape[0], dtype=jnp.int32)[None, :]).astype(BF)
    bucket_at = dot(pick, rel_bucket.astype(BF)[:, None])[:, 0].astype(jnp.int32)
    in_range = (distance >= 0) & (distance < rel_bucket.shape[0])
    bucket_hot = (
        (bucket_at[None, :] == jnp.arange(BUCKETS, dtype=jnp.int32)[:, None]) & in_range[None, :]
    ).astype(BF)
    bias_rows = [dot(bucket_bias_table[l], bucket_hot, ((0,), (0,))) for l in range(LAYERS)]

    expert_ids = jnp.arange(experts, dtype=jnp.int32)
    flat_routes = jnp.concatenate([routes[:, 0], routes[:, 1]])
    hot = (flat_routes[:, None] == expert_ids[None, :]).astype(BF)
    number = jnp.arange(TOP * count_q, dtype=jnp.int32)
    ranks = dot((number[:, None] > number[None, :]).astype(BF), hot)
    rank = jnp.sum(ranks * hot.astype(F32), axis=1).astype(jnp.int32)
    target = flat_routes * capacity + rank
    slots = jnp.arange(experts * capacity, dtype=jnp.int32)
    halves = jnp.arange(2 * experts * capacity, dtype=jnp.int32)
    slot, right = halves // (2 * capacity) * capacity + halves % capacity, halves // capacity % 2
    pairs_at, tokens_at, rows_at = [], [], []
    for side in range(2):
        mine = jnp.where(right == side, slot, -1)[:, None]
        pairs_at.append((mine == target[None, :]).astype(BF))
        tokens_at.append(pairs_at[-1][:, :count_q] + pairs_at[-1][:, count_q:])
        rows_at.append((mine == slots[None, :]).astype(BF))
    route_hot = hot.astype(F32).reshape(TOP, count_q, experts)

    seg_own = segments[0].astype(F32)
    seg_col = seg_own[:, None]
    hidden_state = tokens.astype(F32)
    gains_a, gains_f = gain_attn.astype(F32), gain_ffn.astype(F32)
    stored = []
    shard = wqkv.shape[1]
    row = jnp.arange(blocks * shard, dtype=jnp.int32)[:, None]
    pick = (row // shard * 16 + row % shard == jnp.arange(blocks * 16, dtype=jnp.int32)[None, :]).astype(BF)
    attn_full, segs = gather_attn(wqkv, wout, segments, pick)
    seg_keys = lax.dynamic_slice_in_dim(segs, start, window, axis=1)
    w_in, w_out, seg_keys = lax.optimization_barrier((w_in, w_out, seg_keys))
    expert_full = [gather_experts(w_in, w_out, l) for l in range(LAYERS)]
    for l in range(LAYERS):
        first_mat, second_mat = expert_full[l]
        queries, kv_own, normed, scale_one = queries_keys(hidden_state, gains_a[l], attn_full, l)
        kv = gather_keys(kv_own)
        off_arr = off.reshape(1)
        attended, lse = attention(off_arr, queries, kv, seg_col, seg_keys, bias_rows[l])
        middle, mixed_in, scale_two = after_attention(attended, hidden_state, gains_f[l], attn_full, l)
        router_probs = jax.nn.softmax(dot(mixed_in, router[l]), axis=-1)
        gate_values = jnp.sum(router_probs[None] * route_hot, axis=2)
        if l < LAYERS - 1:
            (expert_rows,) = exchange(0, (mixed_in, tokens_at, rows_at, BF))
            expert_out, pre_act = expert_forward(expert_rows, first_mat, second_mat)
            (pair_out,) = exchange(1, (expert_out, rows_at, pairs_at, F32))
            last_grads = None
        else:
            grad_pairs = (gate_values[:, :, None] * cotangent[None]).astype(BF).reshape(-1, D)
            expert_rows, grad_rows = exchange(
                4, (mixed_in, tokens_at, rows_at, BF), (grad_pairs, pairs_at, rows_at, BF)
            )
            expert_out, grad_inputs, *last_grads = expert_back(expert_rows, grad_rows, None, first_mat, second_mat)
            pair_out, grad_mixed = exchange(
                5, (expert_out, rows_at, pairs_at, F32), (grad_inputs, rows_at, tokens_at, F32)
            )
            last_grads = (grad_mixed, *last_grads)
            pre_act = None
        pair_out = pair_out.reshape(TOP, count_q, D)
        new_state = middle + jnp.sum(gate_values[:, :, None] * pair_out, axis=0)
        stored.append(
            (hidden_state, scale_one, normed, queries, kv, lse, attended, middle, scale_two,
             mixed_in, router_probs, gate_values, pair_out, expert_rows, pre_act)
        )
        hidden_state = new_state
    out_tokens = hidden_state.astype(BF)

    grad_state = cotangent
    small = [None] * LAYERS
    attn_grads = [None] * LAYERS
    first_grads = [None] * LAYERS
    second_grads = [None] * LAYERS
    for l in reversed(range(LAYERS)):
        (state_in, scale_one, normed, queries, kv, lse, attended, middle, scale_two,
         mixed_in, router_probs, gate_values, pair_out, expert_rows, pre_act) = stored[l]
        first_mat, second_mat = expert_full[l]
        grad_gates = jnp.sum(grad_state[None] * pair_out, axis=2)
        if l == LAYERS - 1:
            grad_mixed, grad_first, grad_second = last_grads
        else:
            grad_pairs = (gate_values[:, :, None] * grad_state[None]).astype(BF).reshape(-1, D)
            (grad_rows,) = exchange(2, (grad_pairs, pairs_at, rows_at, BF))
            grad_inputs, grad_first, grad_second = expert_back(
                expert_rows, grad_rows, pre_act, first_mat, second_mat
            )
            (grad_mixed,) = exchange(3, (grad_inputs, rows_at, tokens_at, F32))
        first_grads[l] = lax.psum_scatter(grad_first, "seq", scatter_dimension=0, tiled=True)
        second_grads[l] = lax.psum_scatter(grad_second, "seq", scatter_dimension=0, tiled=True)
        grad_probs = jnp.sum(grad_gates[:, :, None] * route_hot, axis=0)
        grad_logits = router_probs * (
            grad_probs - jnp.sum(router_probs * grad_probs, axis=-1, keepdims=True)
        )
        router_grad = jnp.dot(mixed_in.astype(F32).T, grad_logits, precision=highest)
        grad_mixed = grad_mixed + jnp.dot(grad_logits, router[l].astype(F32).T, precision=highest)
        grad_mid, gain_f_grad = norm_backward(middle, scale_two, gains_f[l], grad_mixed)
        grad_mid = grad_mid + grad_state
        branch_grad = grad_mid.astype(BF)
        grad_attended = branch_back(branch_grad, attn_full, l)
        if l < LAYERS - 1:
            grad_attended, first_grads[l + 1], second_grads[l + 1] = lax.optimization_barrier(
                (grad_attended, first_grads[l + 1], second_grads[l + 1])
            )
        dq, dkv, diag = attention_back(
            off_arr, queries, kv, seg_col, seg_keys, bias_rows[l], lse, grad_attended
        )
        table_grad = lax.dot_general(
            bucket_hot.astype(F32), diag, (((1,), (1,)), ((), ())), precision=highest
        )
        dkv_own = scatter_key_grads(dkv)
        grad_proj = jnp.concatenate([dq, dkv_own], axis=1)
        grad_state, gain_a_grad = input_grad(
            grad_proj, attn_full, l, state_in, scale_one, gains_a[l], grad_mid
        )
        attn_grads[l] = weight_grads(normed, attended, grad_proj, branch_grad)
        small[l] = (gain_a_grad, gain_f_grad, router_grad, table_grad)
    sizes = [D, D, D * experts, BUCKETS * HEADS]
    flat = jnp.concatenate([part.reshape(-1) for l in range(LAYERS) for part in small[l]])
    used = flat.size
    padded = -(-used // (3 * 8 * 128)) * 3 * 8 * 128
    whole = [g.reshape(SIDE, 2, SIDE, SIDE, 3, 16, -1) for g in attn_grads]
    attn, flat = reduce_all(*whole, jnp.pad(flat, (0, padded - used)).reshape(3, -1, 128), pick)
    attn = attn[:, :, :shard].astype(F32).transpose(1, 2, 0, 3).reshape(LAYERS, shard, -1)
    flat = flat.reshape(-1)[:used].reshape(LAYERS, -1)
    sums, at = [], 0
    for size in sizes:
        sums.append(flat[:, at : at + size])
        at += size
    return (
        out_tokens,
        grad_state,
        sums[0],
        attn[:, :, : 3 * D],
        attn[:, :, 3 * D :],
        sums[3].reshape(LAYERS, BUCKETS, HEADS),
        sums[1],
        sums[2].reshape(LAYERS, D, experts),
        jnp.stack(first_grads)[:, None].astype(F32),
        jnp.stack(second_grads)[:, None].astype(F32),
    )


def solution(mesh):
    rows = P(("grp", "seq"), None)
    slab = P(None, ("grp", "seq"), None)
    expert = P(None, "grp", "seq", None)
    return jax.shard_map(
        on_device,
        mesh=mesh,
        in_specs=(
            rows, P("grp", "seq"), P(), rows, P(), slab, slab, P(), P(), P(), expert, expert, rows,
        ),
        out_specs=(rows, rows, P(), slab, slab, P(), P(), P(), expert, expert),
        check_vma=False,
    )
```
